256 devices in a mesh: dp: 32 (over y, x, core), rep: 8 (over z).
Axes of the slice: x: 4, y: 4, z: 8, core: 2. Of those that a mesh axis runs over, the one named last changes fastest.
Arguments:
- queries: bfloat16 [4096, 6144], P(('rep', 'dp')), parts along dimension 0, may hold values from -240 to 240
- cache_keys: bfloat16 [262144, 512], P(('rep', 'dp')), parts along dimension 0, may hold values from -6 to 6
- cache_values: bfloat16 [262144, 512], P(('rep', 'dp')), parts along dimension 0, may hold values from -6 to 6
- lengths: int32 [4096], P(('rep', 'dp')), parts along dimension 0, may hold values from 1 to 512, as said below
- counts: int32 [256], P(('rep', 'dp')), parts along dimension 0, may hold values from 1 to 16, 320 in all
- norm_gain: float32 [6144], replicated, may hold values from 0.1 to 1.9
- up_weight: bfloat16 [6144, 14336], P(None, 'dp'), may hold values from -0.078125 to 0.078125
- down_weight: bfloat16 [14336, 6144], P('dp'), may hold values from -0.046875 to 0.046875
Outputs:
- mixed: bfloat16 [4096, 6144], P(('rep', 'dp')), parts along dimension 0
The draws below stay inside these ranges and needn't reach their ends.
There are 8 independent parts, one for each index of `rep`. The reference program is written for one: setup_inputs(seed, part) draws one part's arguments, and reference() takes and returns one part's arrays. A program takes and returns all parts, laid end to end along the dimension named above; an argument that names none is the same for every part. Nothing has to cross between parts.
Inputs may be any that keep to these rules, and one draw needn't show every extreme that they name: The 16 slots of one device have lengths summing to at most 1024; on every device one slot holds exactly half of 1024 positions. Over the devices of one replica the counts sum to exactly 320.
All inputs are finite; a program needn't handle non-finite values.
Results may differ from the reference program's by a relative error of at most 0.02.
Values may be sent and summed in bfloat16 or wider, within the bound.
No kernel may reach another device: no remote copies, remote signals or barrier semaphores. Data moves between devices by JAX's collectives and lax.ppermute only.
A program may use at most 128 MiB of HBM per device.

```python
import math
import jax
import jax.numpy as jnp
import numpy as np
from jax import lax

HQ = 48
KVH = 4
HD = 128
D = 6144
FF = 14336
CAP = 16
POOL = 1024
LIVE = 320
N_DP = 32


def draw_queries(key, part):
    key = jax.random.fold_in(key, 5)
    first_key = jax.random.fold_in(key, 0)
    values = jax.random.normal(first_key, (N_DP * CAP, HQ * HD), jnp.float32)
    return jnp.clip(values, -240.0, 240.0).astype(jnp.bfloat16)


def draw_lengths(key, part):
    key = jax.random.fold_in(key, 11)
    first_key, second_key = jax.random.split(key)
    longest = POOL // 2
    spare = POOL // 2 - (CAP - 1)
    shares = jax.random.randint(first_key, (N_DP, CAP), 1, 101)
    longest_slot = jax.random.randint(second_key, (N_DP, 1), 0, CAP)
    slot_ids = jnp.arange(CAP, dtype=jnp.int32)[None, :]
    is_long = slot_ids == longest_slot
    share_sum = jnp.sum(jnp.where(is_long, 0, shares), axis=1, keepdims=True)
    small = 1 + shares * spare // share_sum
    lengths_all = jnp.where(is_long, longest, small)
    return lengths_all.reshape(N_DP * CAP).astype(jnp.int32)


def block_levels(own_key, shape, pieces, low, largest):
    factor_of, own = 1.0, jax.random.fold_in(own_key, 6)
    for position, parts in pieces:
        heights = jnp.exp(jax.random.uniform(jax.random.fold_in(own, position), (parts,), jnp.float32, low / len(pieces), largest / len(pieces)))
        factor_of = factor_of * jnp.repeat(heights, shape[position] // parts).reshape([-1 if axis == position else 1 for axis in range(len(shape))])
    return factor_of


def profile(number_of, total, reach, slope):
    weights = [(1 << 20) // math.isqrt(rank ** slope) + 1 for rank in range(2, number_of + 1)]
    surplus, given = total - reach - (number_of - 1), [1] * (number_of - 1)
    while surplus > 0:
        movable = [i for i in range(number_of - 1) if given[i] < reach]
        whole, budget = sum([weights[i] for i in movable]), surplus
        for i in movable:
            more = min(reach - given[i], max(1, budget * weights[i] // whole), surplus)
            given[i] = given[i] + more
            surplus = surplus - more
    return np.array([reach] + given)


def ragged_sizes(rng, amount, total, bound, lean):
    if amount == 2:
        one = jax.random.randint(rng, (), max(1, total - bound), min(bound, total - 1) + 1)
        return jnp.stack([one, total - one])
    sizes = jnp.asarray(profile(amount, total, bound, lean), jnp.int32)
    twos = (amount - 1) // 2
    donor, receiver = sizes[1:1 + 2 * twos:2], sizes[2:2 + 2 * twos:2]
    room = jnp.minimum(donor - 1, bound - receiver)
    passed = jax.random.randint(jax.random.fold_in(rng, 1), (twos,), 0, 1 << 20) % (room + 1)
    sizes = sizes.at[1:1 + 2 * twos:2].set(donor - passed).at[2:2 + 2 * twos:2].set(receiver + passed)
    return sizes[jax.random.permutation(jax.random.fold_in(rng, 2), amount)]


def scatter_about(rng, shape, deviation, bound, cuts=(), kind=jnp.bfloat16):
    entries = deviation * jax.random.normal(rng, shape, jnp.float32)
    if cuts:
        entries = entries * block_levels(rng, shape, cuts, -0.22, 0.18)
    return jnp.clip(entries, -bound, bound).astype(kind)


def setup_inputs(seed: int = 0, part: int = 0) -> dict:
    keys = jax.random.split(jax.random.key(seed), 9)
    own_keys = jax.random.split(jax.random.fold_in(keys[8], part), 9)
    return {
        "queries": draw_queries(jax.random.fold_in(jax.random.fold_in(keys[8], part), 71), part),
        "cache_keys": scatter_about(own_keys[1], (N_DP * POOL, KVH * HD), 1.0, 6.0, ((0, 32),)),
        "cache_values": scatter_about(own_keys[2], (N_DP * POOL, KVH * HD), 1.0, 6.0, ((0, 32),)),
        "lengths": draw_lengths(jax.random.fold_in(jax.random.fold_in(keys[8], part), 71), part),
        "counts": ragged_sizes(own_keys[4], N_DP, LIVE, CAP, 2).astype(jnp.int32),
        "norm_gain": jnp.clip(1.0 + 0.18 * jax.random.normal(keys[5], (D,), jnp.float32), 0.1, 1.9),
        "up_weight": scatter_about(keys[6], (D, FF), D ** -0.5, 0.078125, ((1, 32),)),
        "down_weight": scatter_about(keys[7], (FF, D), FF ** -0.5, 0.046875, ((0, 32),)),
    }


def attend(query_rows, key_rows, value_rows, cache_lengths, live_count):
    group = HQ // KVH
    query_heads = query_rows.reshape(CAP, KVH, group, HD).astype(jnp.float32)
    key_heads = key_rows.reshape(POOL, KVH, HD).astype(jnp.float32)
    value_heads = value_rows.reshape(POOL, KVH, HD).astype(jnp.float32)
    scores = jnp.einsum('ckgd,pkd->ckgp', query_heads, key_heads) * HD ** (-0.5)
    ends = jnp.cumsum(cache_lengths)
    starts = ends - cache_lengths
    positions = jnp.arange(POOL, dtype=jnp.int32)
    inside = (positions[None, :] >= starts[:, None]) & (positions[None, :] < ends[:, None])
    inside = inside[:, None, None, :]
    masked = jnp.where(inside, scores, jnp.float32(-1e+30))
    row_max = lax.optimization_barrier(jnp.max(masked, axis=-1, keepdims=True))
    raised = jnp.where(inside, jnp.exp(masked - row_max), jnp.float32(0.0))
    row_total = lax.optimization_barrier(jnp.sum(raised, axis=-1, keepdims=True))
    weights = (raised / row_total).astype(jnp.bfloat16)
    mixed_heads = jnp.einsum('ckgp,pkd->ckgd', weights.astype(jnp.float32), value_heads)
    live_mask = jnp.arange(CAP, dtype=jnp.int32) < live_count
    flat_rows = mixed_heads.reshape(CAP, HQ * HD)
    return jnp.where(live_mask[:, None], flat_rows, jnp.float32(0.0)).astype(jnp.bfloat16)

def reference(queries, cache_keys, cache_values, lengths, counts, norm_gain, up_weight, down_weight):
    width = HQ * HD

    def one_rank(items):
        return attend(items[0], items[1], items[2], items[3], items[4])
    attended = lax.map(one_rank, (queries.reshape(N_DP, CAP, width), cache_keys.reshape(N_DP, POOL, KVH * HD), cache_values.reshape(N_DP, POOL, KVH * HD), lengths.reshape(N_DP, CAP), counts))
    attended_wide = attended.reshape(N_DP * CAP, width).astype(jnp.float32)
    mean_square = lax.optimization_barrier(jnp.mean(attended_wide * attended_wide, axis=-1, keepdims=True))
    normed = (attended_wide * lax.rsqrt(mean_square + 1e-05) * norm_gain).astype(jnp.bfloat16)
    up_proj = jnp.dot(normed, up_weight, preferred_element_type=jnp.float32)
    activated = jax.nn.silu(up_proj).astype(jnp.bfloat16)
    projected = jnp.dot(activated, down_weight, preferred_element_type=jnp.float32)
    return (attended_wide + projected).astype(jnp.bfloat16)
```

```python
import functools

import jax
import jax.numpy as jnp
from jax import lax
from jax.experimental import pallas as pl
from jax.experimental.pallas import tpu as pltpu
from jax.sharding import PartitionSpec as P

HQ = 48
KVH = 4
HD = 128
GROUP = HQ // KVH
D = HQ * HD
HALF = D // 2
SLOTS = 16
POOL = 1024
HIDDEN = 448
SIDE = 4
N_DP = 32
WIDE = SIDE * SLOTS
CHUNK = 512


def device(y, x, c):
    return ((y % SIDE) * SIDE + x % SIDE) * 2 + c


def routes():
    out = {name: [] for name in ("xa", "xb", "x2", "ya", "yb", "y2", "core")}
    for y in range(SIDE):
        for x in range(SIDE):
            for c in range(2):
                way = 1 if c == 0 else -1
                me = device(y, x, c)
                out["xa"].append((me, device(y, x + way, c)))
                out["xb"].append((me, device(y, x - way, c)))
                out["x2"].append((me, device(y, x + 2, c)))
                out["ya"].append((me, device(y + way, x, c)))
                out["yb"].append((me, device(y - way, x, c)))
                out["y2"].append((me, device(y + 2, x, c)))
                out["core"].append((me, device(y, x, 1 - c)))
    return out


ROUTES = routes()


def send(value, route):
    return lax.ppermute(value, "dp", ROUTES[route])


def attend_kernel(lengths, counts, q, k, v, gain, attended, first, second):
    row = lax.broadcasted_iota(jnp.int32, (SLOTS, 1), 0)
    starts = jnp.zeros((SLOTS, 1), jnp.int32)
    ends = jnp.zeros((SLOTS, 1), jnp.int32)
    at = jnp.int32(0)
    for i in range(SLOTS):
        after = at + lengths[i]
        starts = jnp.where(row == i, at, starts)
        ends = jnp.where(row == i, after, ends)
        at = after
    position = lax.broadcasted_iota(jnp.int32, (SLOTS, POOL), 1)
    inside = (position >= starts) & (position < ends)
    offset = jnp.where(inside, jnp.float32(0.0), jnp.float32(-1e30))
    live = row < counts[0]
    squares = jnp.zeros((SLOTS, HD), jnp.float32)
    for kv in range(KVH):
        heads = range(kv * GROUP, (kv + 1) * GROUP)
        rows = jnp.concatenate([q[:, h * HD : (h + 1) * HD] for h in heads], axis=0)
        scores = lax.dot_general(
            rows,
            k[:, kv * HD : (kv + 1) * HD],
            (((1,), (1,)), ((), ())),
            preferred_element_type=jnp.float32,
        )
        masked = scores.reshape(GROUP, SLOTS, POOL) + offset[None]
        top = jnp.max(masked, axis=-1, keepdims=True)
        raised = jnp.exp((masked - top) * jnp.float32(HD ** (-0.5)))
        total = jnp.sum(raised, axis=-1, keepdims=True)
        mixed = lax.dot_general(
            raised.astype(jnp.bfloat16).reshape(GROUP * SLOTS, POOL),
            v[:, kv * HD : (kv + 1) * HD],
            (((1,), (0,)), ((), ())),
            preferred_element_type=jnp.float32,
        )
        mixed = mixed.reshape(GROUP, SLOTS, HD) / total
        for g, h in enumerate(heads):
            part = jnp.where(live, mixed[g], jnp.float32(0.0)).astype(jnp.bfloat16)
            attended[:, h * HD : (h + 1) * HD] = part
            wide = part.astype(jnp.float32)
            squares = squares + wide * wide
    mean_square = jnp.sum(squares, axis=-1, keepdims=True) / D
    factor = lax.rsqrt(mean_square + 1e-05)
    for out, base in ((first, 0), (second, HALF)):
        wide = attended[:, base : base + HALF].astype(jnp.float32)
        out[...] = (wide * factor * gain[:, base : base + HALF]).astype(jnp.bfloat16)


def attend(queries, cache_keys, cache_values, lengths, counts, norm_gain):
    vmem = pl.BlockSpec(memory_space=pltpu.VMEM)
    smem = pl.BlockSpec(memory_space=pltpu.SMEM)
    return pl.pallas_call(
        attend_kernel,
        out_shape=(
            jax.ShapeDtypeStruct((SLOTS, D), jnp.bfloat16),
            jax.ShapeDtypeStruct((SLOTS, HALF), jnp.bfloat16),
            jax.ShapeDtypeStruct((SLOTS, HALF), jnp.bfloat16),
        ),
        in_specs=[smem, smem, vmem, vmem, vmem, vmem],
        out_specs=(vmem, vmem, vmem),
        compiler_params=pltpu.CompilerParams(vmem_limit_bytes=24 * 2**20),
        name="attend",
    )(lengths, counts, queries, cache_keys, cache_values, norm_gain.reshape(1, D))


def block_copies(refs, rows, sems):
    pairs = []
    for core in range(2):
        for i in range(SIDE):
            pairs.append((refs[core * 8 + i], rows.at[core, i, :, :, pl.ds(0, HALF)]))
            pairs.append((refs[core * 8 + 4 + i], rows.at[core, :, i, :, pl.ds(HALF, HALF)]))
    return pairs


def ffn_kernel(*args):
    ins, up, down, outs = args[:16], args[16], args[17], args[18:34]
    rows, up_held, down_held, total, hidden, sem_in, sem_w, sem_out = args[34:]
    copies = [
        pltpu.make_async_copy(a, b, sem_in.at[i])
        for i, (a, b) in enumerate(block_copies(ins, rows, None))
    ]
    for copy in copies:
        copy.start()
    up_copy = pltpu.make_async_copy(up, up_held, sem_w.at[0])
    up_copy.start()
    down_copy = pltpu.make_async_copy(down, down_held, sem_w.at[1])
    down_copy.start()
    up_copy.wait()
    for copy in copies:
        copy.wait()
    m = 2 * SIDE * SIDE * SLOTS
    total[...] = jnp.zeros_like(total)

    @pl.loop(0, D // CHUNK)
    def _(step):
        cols = pl.ds(pl.multiple_of(step * CHUNK, CHUNK), CHUNK)
        total[...] += lax.dot_general(
            rows[:, :, :, :, cols].reshape(m, CHUNK),
            up_held[:, cols],
            (((1,), (1,)), ((), ())),
            preferred_element_type=jnp.float32,
        )

    value = total[...]
    hidden[...] = (value / (1.0 + jnp.exp(-value))).astype(jnp.bfloat16)
    down_copy.wait()

    @pl.loop(0, D // CHUNK)
    def _(step):
        cols = pl.ds(pl.multiple_of(step * CHUNK, CHUNK), CHUNK)
        product = jnp.dot(hidden[...], down_held[:, cols], preferred_element_type=jnp.float32)
        rows[:, :, :, :, cols] = product.astype(jnp.bfloat16).reshape(
            2, SIDE, SIDE, SLOTS, CHUNK
        )

    back = [
        pltpu.make_async_copy(b, a, sem_out.at[i])
        for i, (a, b) in enumerate(block_copies(outs, rows, None))
    ]
    for copy in back:
        copy.start()
    for copy in back:
        copy.wait()


def feed_forward(blocks, up_rows, down_rows):
    any_space = pl.BlockSpec(memory_space=pl.ANY)
    m = 2 * SIDE * SIDE * SLOTS
    return pl.pallas_call(
        ffn_kernel,
        out_shape=[jax.ShapeDtypeStruct((SIDE, SLOTS, HALF), jnp.bfloat16)] * 16,
        in_specs=[any_space] * 18,
        out_specs=[any_space] * 16,
        scratch_shapes=[
            pltpu.VMEM((2, SIDE, SIDE, SLOTS, D), jnp.bfloat16),
            pltpu.VMEM((HIDDEN, D), jnp.bfloat16),
            pltpu.VMEM((HIDDEN, D), jnp.bfloat16),
            pltpu.VMEM((m, HIDDEN), jnp.float32),
            pltpu.VMEM((m, HIDDEN), jnp.bfloat16),
            pltpu.SemaphoreType.DMA((16,)),
            pltpu.SemaphoreType.DMA((2,)),
            pltpu.SemaphoreType.DMA((16,)),
        ],
        compiler_params=pltpu.CompilerParams(vmem_limit_bytes=48 * 2**20),
        name="feed_forward",
    )(*blocks, up_rows, down_rows)


def ring_gather(own, axis):
    from_a = send(own, axis + "a")
    from_b = send(own, axis + "b")
    return own, from_a, from_b, send(from_a, axis + "a")


def ring_reduce(blocks, axis):
    own, of_a, of_b, of_2 = blocks
    far = send(of_2, axis + "b")
    near = send(of_b, axis + "a")
    back = send((of_a.astype(jnp.float32) + far.astype(jnp.float32)).astype(jnp.bfloat16), axis + "b")
    return own.astype(jnp.float32) + near.astype(jnp.float32) + back.astype(jnp.float32)


def on_device(
    queries, cache_keys, cache_values, lengths, counts, norm_gain, up_weight, down_weight
):
    attended, first, second = attend(
        queries, cache_keys, cache_values, lengths, counts, norm_gain
    )
    row = jnp.stack(ring_gather(first, "x"))
    column = jnp.stack(ring_gather(second, "y"))
    own = [*ring_gather(row, "y"), *ring_gather(column, "x")]
    blocks = own + [send(b, "core") for b in own]
    parts = feed_forward(blocks, up_weight.T, down_weight)
    summed = [
        (a.astype(jnp.float32) + send(b, "core").astype(jnp.float32)).astype(jnp.bfloat16)
        for a, b in zip(parts[:8], parts[8:])
    ]
    row = ring_reduce(summed[:4], "y").astype(jnp.bfloat16)
    column = ring_reduce(summed[4:], "x").astype(jnp.bfloat16)
    first = ring_reduce([row[i] for i in range(SIDE)], "x")
    second = ring_reduce([column[i] for i in range(SIDE)], "y")
    projected = jnp.concatenate([first, second], axis=1)
    return (attended.astype(jnp.float32) + projected).astype(jnp.bfloat16)


def solution(mesh):
    in_specs = (
        P(("rep", "dp"), None),
        P(("rep", "dp"), None),
        P(("rep", "dp"), None),
        P(("rep", "dp")),
        P(("rep", "dp")),
        P(),
        P(None, "dp"),
        P("dp", None),
    )
    out_specs = P(("rep", "dp"), None)
    return jax.shard_map(
        on_device, mesh=mesh, in_specs=in_specs, out_specs=out_specs, check_vma=False
    )
```

```python
import jax
import jax.numpy as jnp
from jax import lax
from jax.experimental import pallas as pl
from jax.experimental.pallas import tpu as pltpu
from jax.sharding import PartitionSpec as P

HQ = 48
KVH = 4
HD = 128
GROUP = HQ // KVH
D = HQ * HD
SLOTS = 16
POOL = 1024
HIDDEN = 448
SIDE = 4
PAIR = 2 * SLOTS
CHUNK = 3072


def device(y, x, c):
    return ((y % SIDE) * SIDE + x % SIDE) * 2 + c


def routes():
    out = {name: [] for name in ("sa", "sb", "s2", "ta", "tb", "core")}
    for y in range(SIDE):
        for x in range(SIDE):
            for c in range(2):
                me = device(y, x, c)
                for name, by in (("a", 1), ("b", -1), ("2", 2)):
                    along_x, along_y = device(y, x + by, c), device(y + by, x, c)
                    out["s" + name].append((me, along_x if c == 0 else along_y))
                    if name != "2":
                        out["t" + name].append((me, along_y if c == 0 else along_x))
                out["core"].append((me, device(y, x, 1 - c)))
    return out


ROUTES = routes()


def send(value, route, what):
    with jax.named_scope(what + "_" + route):
        return lax.ppermute(value, "dp", ROUTES[route])


def in_hbm(x):
    return pltpu.with_memory_space_constraint(x, pltpu.HBM)


def attend_kernel(
    counts, lengths_in, q_in, k_in, v_in, gain_in, attended, normed, lengths, q, k, v, gain, sems
):
    copies = [
        pltpu.make_async_copy(a, b, sems.at[i])
        for i, (a, b) in enumerate(
            (
                (lengths_in, lengths),
                (k_in, k),
                (q_in, q),
                (v_in, v),
                (gain_in, gain),
            )
        )
    ]
    for copy in copies:
        copy.start()
    copies[0].wait()
    row = lax.broadcasted_iota(jnp.int32, (SLOTS, 1), 0)
    starts = jnp.zeros((SLOTS, 1), jnp.int32)
    ends = jnp.zeros((SLOTS, 1), jnp.int32)
    at = jnp.int32(0)
    for i in range(SLOTS):
        after = at + lengths[i]
        starts = jnp.where(row == i, at, starts)
        ends = jnp.where(row == i, after, ends)
        at = after
    position = lax.broadcasted_iota(jnp.int32, (SLOTS, POOL), 1)
    inside = (position >= starts) & (position < ends)
    offset = jnp.where(inside, jnp.float32(0.0), jnp.float32(-1e30))
    live = row < counts[0]
    squares = jnp.zeros((SLOTS, HD), jnp.float32)
    copies[1].wait()
    copies[2].wait()
    for kv in range(KVH):
        heads = range(kv * GROUP, (kv + 1) * GROUP)
        rows = jnp.concatenate([q[:, h * HD : (h + 1) * HD] for h in heads], axis=0)
        scores = lax.dot_general(
            rows,
            k[:, kv * HD : (kv + 1) * HD],
            (((1,), (1,)), ((), ())),
            preferred_element_type=jnp.float32,
        )
        masked = scores.reshape(GROUP, SLOTS, POOL) + offset[None]
        top = jnp.max(masked, axis=-1, keepdims=True)
        raised = jnp.exp((masked - top) * jnp.float32(HD ** (-0.5)))
        total = jnp.sum(raised, axis=-1, keepdims=True)
        if kv == 0:
            copies[3].wait()
        mixed = lax.dot_general(
            raised.astype(jnp.bfloat16).reshape(GROUP * SLOTS, POOL),
            v[:, kv * HD : (kv + 1) * HD],
            (((1,), (0,)), ((), ())),
            preferred_element_type=jnp.float32,
        )
        mixed = mixed.reshape(GROUP, SLOTS, HD) / total
        for g, h in enumerate(heads):
            part = jnp.where(live, mixed[g], jnp.float32(0.0)).astype(jnp.bfloat16)
            attended[:, h * HD : (h + 1) * HD] = part
            wide = part.astype(jnp.float32)
            squares = squares + wide * wide
    mean_square = jnp.sum(squares, axis=-1, keepdims=True) / D
    factor = lax.rsqrt(mean_square + 1e-05)
    copies[4].wait()
    normed[...] = (attended[...].astype(jnp.float32) * factor * gain[...]).astype(jnp.bfloat16)


def attend(queries, cache_keys, cache_values, lengths, counts, norm_gain):
    vmem = pl.BlockSpec(memory_space=pltpu.VMEM)
    any_space = pl.BlockSpec(memory_space=pl.ANY)
    return pl.pallas_call(
        attend_kernel,
        out_shape=(jax.ShapeDtypeStruct((SLOTS, D), jnp.bfloat16),) * 2,
        in_specs=[pl.BlockSpec(memory_space=pltpu.SMEM)] + [any_space] * 5,
        out_specs=(vmem, vmem),
        scratch_shapes=[
            pltpu.SMEM((SLOTS,), jnp.int32),
            pltpu.VMEM((SLOTS, D), jnp.bfloat16),
            pltpu.VMEM((POOL, KVH * HD), jnp.bfloat16),
            pltpu.VMEM((POOL, KVH * HD), jnp.bfloat16),
            pltpu.VMEM((1, D), jnp.float32),
            pltpu.SemaphoreType.DMA((5,)),
        ],
        compiler_params=pltpu.CompilerParams(vmem_limit_bytes=16 * 2**20),
        name="attend",
    )(counts, *map(in_hbm, (lengths, queries, cache_keys, cache_values, norm_gain.reshape(1, D))))


def fetch_kernel(up, down, after, up_held, down_held, sems):
    copies = [
        pltpu.make_async_copy(up, up_held, sems.at[0]),
        pltpu.make_async_copy(down, down_held, sems.at[1]),
    ]
    for copy in copies:
        copy.start()
    for copy in copies:
        copy.wait()


def fetch(up_rows, down_rows, after):
    any_space = pl.BlockSpec(memory_space=pl.ANY)
    vmem = pl.BlockSpec(memory_space=pltpu.VMEM)
    return pl.pallas_call(
        fetch_kernel,
        out_shape=[jax.ShapeDtypeStruct((HIDDEN, D), jnp.bfloat16)] * 2,
        in_specs=[any_space] * 3,
        out_specs=[vmem] * 2,
        scratch_shapes=[pltpu.SemaphoreType.DMA((2,))],
        compiler_params=pltpu.CompilerParams(vmem_limit_bytes=16 * 2**20),
        cost_estimate=pl.CostEstimate(flops=0, bytes_accessed=4 * HIDDEN * D, transcendentals=0),
        name="fetch",
    )(in_hbm(up_rows), in_hbm(down_rows), after)


def ffn_kernel(*args):
    blocks, up, down, outs, (total, hidden) = args[:8], args[8:10], args[10:12], args[12:20], args[20:]
    total[...] = jnp.zeros_like(total)

    @pl.loop(0, D // CHUNK)
    def _(step):
        cols = pl.ds(pl.multiple_of(step * CHUNK, CHUNK), CHUNK)
        total[...] += lax.dot_general(
            jnp.concatenate([w[:, cols] for w in up], axis=0),
            jnp.concatenate([b[:, cols] for b in blocks], axis=0),
            (((1,), (1,)), ((), ())),
            preferred_element_type=jnp.float32,
        )

    value = total[...]
    hidden[...] = (value / (1.0 + jnp.exp(-value))).astype(jnp.bfloat16).T

    @pl.loop(0, D // CHUNK)
    def _(step):
        cols = pl.ds(pl.multiple_of(step * CHUNK, CHUNK), CHUNK)
        product = jnp.dot(
            hidden[...],
            jnp.concatenate([w[:, cols] for w in down], axis=0),
            preferred_element_type=jnp.float32,
        ).astype(jnp.bfloat16)
        for i, out in enumerate(outs):
            out[:, cols] = product[i * PAIR : (i + 1) * PAIR]


def feed_forward(blocks, up, down):
    vmem = pl.BlockSpec(memory_space=pltpu.VMEM)
    return pl.pallas_call(
        ffn_kernel,
        out_shape=[jax.ShapeDtypeStruct((PAIR, D), jnp.bfloat16)] * 8,
        in_specs=[vmem] * 12,
        out_specs=[vmem] * 8,
        scratch_shapes=[
            pltpu.VMEM((2 * HIDDEN, 8 * PAIR), jnp.float32),
            pltpu.VMEM((8 * PAIR, 2 * HIDDEN), jnp.bfloat16),
        ],
        compiler_params=pltpu.CompilerParams(vmem_limit_bytes=16 * 2**20),
        name="feed_forward",
    )(*blocks, *up, *down)


def f32(x):
    return x.astype(jnp.float32)


def add(*terms):
    return sum(map(f32, terms)).astype(jnp.bfloat16)


def on_device(
    queries, cache_keys, cache_values, lengths, counts, norm_gain, up_weight, down_weight
):
    up_own, down_own = up_weight.T, down_weight
    up_other = send(up_own, "core", "up")
    down_other = send(down_own, "core", "down")
    attended, normed = attend(queries, cache_keys, cache_values, lengths, counts, norm_gain)
    by_a, by_b, by_2 = [send(normed, r, "gather") for r in ("sa", "sb", "s2")]
    first = jnp.concatenate([normed, by_a], axis=0)
    second = jnp.concatenate([by_b, by_2], axis=0)
    first_a, second_b = send(first, "ta", "gather"), send(second, "tb", "gather")
    first_b, second_a = send(first, "tb", "gather"), send(second, "ta", "gather")
    first_2, second_2 = send(first_a, "ta", "gather2"), send(second_b, "tb", "gather2")
    up_held, down_held = fetch(up_own, down_own, second)
    blocks = [first, second, first_a, second_b, first_b, second_a, first_2, second_2]
    first, second, first_a, second_b, first_b, second_a, first_2, second_2 = feed_forward(
        blocks, (up_held, up_other), (down_held, down_other)
    )
    far_first = send(first_2, "tb", "reduce2")
    far_second = send(second_2, "ta", "reduce2")
    near_first = send(first_b, "ta", "reduce")
    near_second = send(second_a, "tb", "reduce")
    back_first = send(add(first_a, far_first), "tb", "reduce")
    back_second = send(add(second_b, far_second), "ta", "reduce")
    first = f32(first) + f32(near_first) + f32(back_first)
    second = f32(second) + f32(near_second) + f32(back_second)
    home_a = send(first[SLOTS:].astype(jnp.bfloat16), "sb", "home")
    home_b = send(second[:SLOTS].astype(jnp.bfloat16), "sa", "home")
    home_2 = send(second[SLOTS:].astype(jnp.bfloat16), "s2", "home")
    projected = first[:SLOTS] + f32(home_a) + f32(home_b) + f32(home_2)
    return (f32(attended) + projected).astype(jnp.bfloat16)


def solution(mesh):
    in_specs = (
        P(("rep", "dp"), None),
        P(("rep", "dp"), None),
        P(("rep", "dp"), None),
        P(("rep", "dp")),
        P(("rep", "dp")),
        P(),
        P(None, "dp"),
        P("dp", None),
    )
    out_specs = P(("rep", "dp"), None)
    return jax.shard_map(
        on_device, mesh=mesh, in_specs=in_specs, out_specs=out_specs, check_vma=False
    )
```

```python
import jax
import jax.numpy as jnp
from jax import lax
from jax.experimental import pallas as pl
from jax.experimental.pallas import tpu as pltpu
from jax.sharding import PartitionSpec as P

HQ = 48
KVH = 4
HD = 128
GROUP = HQ // KVH
D = HQ * HD
SLOTS = 16
POOL = 1024
HIDDEN = 448
SIDE = 4
PAIR = 2 * SLOTS
CHUNK = 3072


def device(y, x, c):
    return (y * SIDE + x) * 2 + c


def routes():
    other = {"near": (1, 0, 3, 2), "wrap": (3, 2, 1, 0), "far": (2, 3, 0, 1)}
    out = {"core": [], **{axis + name: [] for axis in "st" for name in other}}
    for y in range(SIDE):
        for x in range(SIDE):
            for c in range(2):
                me = device(y, x, c)
                for name, to in other.items():
                    along_x, along_y = device(y, to[x], c), device(to[y], x, c)
                    out["s" + name].append((me, along_x if c == 0 else along_y))
                    out["t" + name].append((me, along_y if c == 0 else along_x))
                out["core"].append((me, device(y, x, 1 - c)))
    return out


ROUTES = routes()


def send(value, route, what):
    with jax.named_scope(what + "_" + route):
        return lax.ppermute(value, "dp", ROUTES[route])


def in_hbm(x):
    return pltpu.with_memory_space_constraint(x, pltpu.HBM)


def attend_kernel(
    counts, lengths_in, q_in, k_in, v_in, gain_in, attended, normed, lengths, q, k, v, gain, sems
):
    copies = [
        pltpu.make_async_copy(a, b, sems.at[i])
        for i, (a, b) in enumerate(
            (
                (lengths_in, lengths),
                (k_in, k),
                (q_in, q),
                (v_in, v),
                (gain_in, gain),
            )
        )
    ]
    for copy in copies:
        copy.start()
    copies[0].wait()
    row = lax.broadcasted_iota(jnp.int32, (SLOTS, 1), 0)
    starts = jnp.zeros((SLOTS, 1), jnp.int32)
    ends = jnp.zeros((SLOTS, 1), jnp.int32)
    at = jnp.int32(0)
    for i in range(SLOTS):
        after = at + lengths[i]
        starts = jnp.where(row == i, at, starts)
        ends = jnp.where(row == i, after, ends)
        at = after
    position = lax.broadcasted_iota(jnp.int32, (SLOTS, POOL), 1)
    inside = (position >= starts) & (position < ends)
    offset = jnp.where(inside, jnp.float32(0.0), jnp.float32(-1e30))
    live = row < counts[0]
    squares = jnp.zeros((SLOTS, HD), jnp.float32)
    copies[1].wait()
    copies[2].wait()
    for kv in range(KVH):
        heads = range(kv * GROUP, (kv + 1) * GROUP)
        rows = jnp.concatenate([q[:, h * HD : (h + 1) * HD] for h in heads], axis=0)
        scores = lax.dot_general(
            rows,
            k[:, kv * HD : (kv + 1) * HD],
            (((1,), (1,)), ((), ())),
            preferred_element_type=jnp.float32,
        )
        masked = scores.reshape(GROUP, SLOTS, POOL) + offset[None]
        top = jnp.max(masked, axis=-1, keepdims=True)
        raised = jnp.exp((masked - top) * jnp.float32(HD ** (-0.5)))
        total = jnp.sum(raised, axis=-1, keepdims=True)
        if kv == 0:
            copies[3].wait()
        mixed = lax.dot_general(
            raised.astype(jnp.bfloat16).reshape(GROUP * SLOTS, POOL),
            v[:, kv * HD : (kv + 1) * HD],
            (((1,), (0,)), ((), ())),
            preferred_element_type=jnp.float32,
        )
        mixed = mixed.reshape(GROUP, SLOTS, HD) / total
        for g, h in enumerate(heads):
            part = jnp.where(live, mixed[g], jnp.float32(0.0)).astype(jnp.bfloat16)
            attended[:, h * HD : (h + 1) * HD] = part
            wide = part.astype(jnp.float32)
            squares = squares + wide * wide
    mean_square = jnp.sum(squares, axis=-1, keepdims=True) / D
    factor = lax.rsqrt(mean_square + 1e-05)
    copies[4].wait()
    normed[...] = (attended[...].astype(jnp.float32) * factor * gain[...]).astype(jnp.bfloat16)


def attend(queries, cache_keys, cache_values, lengths, counts, norm_gain):
    vmem = pl.BlockSpec(memory_space=pltpu.VMEM)
    any_space = pl.BlockSpec(memory_space=pl.ANY)
    return pl.pallas_call(
        attend_kernel,
        out_shape=(jax.ShapeDtypeStruct((SLOTS, D), jnp.bfloat16),) * 2,
        in_specs=[pl.BlockSpec(memory_space=pltpu.SMEM)] + [any_space] * 5,
        out_specs=(vmem, vmem),
        scratch_shapes=[
            pltpu.SMEM((SLOTS,), jnp.int32),
            pltpu.VMEM((SLOTS, D), jnp.bfloat16),
            pltpu.VMEM((POOL, KVH * HD), jnp.bfloat16),
            pltpu.VMEM((POOL, KVH * HD), jnp.bfloat16),
            pltpu.VMEM((1, D), jnp.float32),
            pltpu.SemaphoreType.DMA((5,)),
        ],
        compiler_params=pltpu.CompilerParams(vmem_limit_bytes=16 * 2**20),
        name="attend",
    )(counts, *map(in_hbm, (lengths, queries, cache_keys, cache_values, norm_gain.reshape(1, D))))


def fetch_kernel(up, down, after, up_held, down_held, sems):
    copies = [
        pltpu.make_async_copy(up, up_held, sems.at[0]),
        pltpu.make_async_copy(down, down_held, sems.at[1]),
    ]
    for copy in copies:
        copy.start()
    for copy in copies:
        copy.wait()


def fetch(up_rows, down_rows, after):
    any_space = pl.BlockSpec(memory_space=pl.ANY)
    vmem = pl.BlockSpec(memory_space=pltpu.VMEM)
    return pl.pallas_call(
        fetch_kernel,
        out_shape=[jax.ShapeDtypeStruct((HIDDEN, D), jnp.bfloat16)] * 2,
        in_specs=[any_space] * 3,
        out_specs=[vmem] * 2,
        scratch_shapes=[pltpu.SemaphoreType.DMA((2,))],
        compiler_params=pltpu.CompilerParams(vmem_limit_bytes=16 * 2**20),
        cost_estimate=pl.CostEstimate(flops=0, bytes_accessed=4 * HIDDEN * D, transcendentals=0),
        name="fetch",
    )(in_hbm(up_rows), in_hbm(down_rows), after)


def ffn_kernel(*args):
    blocks, up, down, outs, (total, hidden) = args[:8], args[8:10], args[10:12], args[12:20], args[20:]
    total[...] = jnp.zeros_like(total)

    @pl.loop(0, D // CHUNK)
    def _(step):
        cols = pl.ds(pl.multiple_of(step * CHUNK, CHUNK), CHUNK)
        total[...] += lax.dot_general(
            jnp.concatenate([w[:, cols] for w in up], axis=0),
            jnp.concatenate([b[:, cols] for b in blocks], axis=0),
            (((1,), (1,)), ((), ())),
            preferred_element_type=jnp.float32,
        )

    value = total[...]
    hidden[...] = (value / (1.0 + jnp.exp(-value))).astype(jnp.bfloat16).T

    @pl.loop(0, D // CHUNK)
    def _(step):
        cols = pl.ds(pl.multiple_of(step * CHUNK, CHUNK), CHUNK)
        product = jnp.dot(
            hidden[...],
            jnp.concatenate([w[:, cols] for w in down], axis=0),
            preferred_element_type=jnp.float32,
        ).astype(jnp.bfloat16)
        for i, out in enumerate(outs):
            out[:, cols] = product[i * PAIR : (i + 1) * PAIR]


def feed_forward(blocks, up, down):
    vmem = pl.BlockSpec(memory_space=pltpu.VMEM)
    return pl.pallas_call(
        ffn_kernel,
        out_shape=[jax.ShapeDtypeStruct((PAIR, D), jnp.bfloat16)] * 8,
        in_specs=[vmem] * 12,
        out_specs=[vmem] * 8,
        scratch_shapes=[
            pltpu.VMEM((2 * HIDDEN, 8 * PAIR), jnp.float32),
            pltpu.VMEM((8 * PAIR, 2 * HIDDEN), jnp.bfloat16),
        ],
        compiler_params=pltpu.CompilerParams(vmem_limit_bytes=16 * 2**20),
        name="feed_forward",
    )(*blocks, *up, *down)


def f32(x):
    return x.astype(jnp.float32)


def add(*terms):
    return sum(map(f32, terms)).astype(jnp.bfloat16)


def on_device(
    queries, cache_keys, cache_values, lengths, counts, norm_gain, up_weight, down_weight
):
    up_own, down_own = up_weight.T, down_weight
    up_other = send(up_own, "core", "up")
    down_other = send(down_own, "core", "down")
    attended, normed = attend(queries, cache_keys, cache_values, lengths, counts, norm_gain)
    by_wrap, by_far, by_near = [send(normed, r, "gather") for r in ("swrap", "sfar", "snear")]
    first = jnp.concatenate([normed, by_near], axis=0)
    second = jnp.concatenate([by_wrap, by_far], axis=0)
    first_w, second_n = send(first, "twrap", "gather"), send(second, "tnear", "gather")
    second_w, first_n = send(second, "twrap", "gather"), send(first, "tnear", "gather")
    first_f, second_f = send(first_w, "tnear", "gather2"), send(second_n, "twrap", "gather2")
    up_held, down_held = fetch(up_own, down_own, second)
    blocks = [first, second, first_w, second_n, first_n, second_w, first_f, second_f]
    first, second, first_w, second_n, first_n, second_w, first_f, second_f = feed_forward(
        blocks, (up_held, up_other), (down_held, down_other)
    )
    far_first = send(first_f, "tnear", "reduce2")
    far_second = send(second_f, "twrap", "reduce2")
    near_first = send(first_n, "tnear", "reduce")
    near_second = send(second_w, "twrap", "reduce")
    back_first = send(add(first_w, far_first), "twrap", "reduce")
    back_second = send(add(second_n, far_second), "tnear", "reduce")
    first = f32(first) + f32(near_first) + f32(back_first)
    second = f32(second) + f32(near_second) + f32(back_second)
    home_near = send(first[SLOTS:].astype(jnp.bfloat16), "snear", "home")
    home_wrap = send(second[:SLOTS].astype(jnp.bfloat16), "swrap", "home")
    home_far = send(second[SLOTS:].astype(jnp.bfloat16), "sfar", "home")
    projected = first[:SLOTS] + f32(home_near) + f32(home_wrap) + f32(home_far)
    return (f32(attended) + projected).astype(jnp.bfloat16)


def solution(mesh):
    in_specs = (
        P(("rep", "dp"), None),
        P(("rep", "dp"), None),
        P(("rep", "dp"), None),
        P(("rep", "dp")),
        P(("rep", "dp")),
        P(),
        P(None, "dp"),
        P("dp", None),
    )
    out_specs = P(("rep", "dp"), None)
    return jax.shard_map(
        on_device, mesh=mesh, in_specs=in_specs, out_specs=out_specs, check_vma=False
    )
```

```python
import jax
import jax.numpy as jnp
from jax import lax
from jax.experimental import pallas as pl
from jax.experimental.pallas import tpu as pltpu
from jax.sharding import PartitionSpec as P

HQ = 48
KVH = 4
HD = 128
GROUP = HQ // KVH
D = HQ * HD
SLOTS = 16
POOL = 1024
HIDDEN = 448
SIDE = 4
PAIR = 2 * SLOTS
CHUNK = 3072


def device(y, x, c):
    return (y * SIDE + x) * 2 + c


def routes():
    other = {"near": (1, 0, 3, 2), "wrap": (3, 2, 1, 0), "far": (2, 3, 0, 1)}
    out = {"core": [], **{axis + name: [] for axis in "st" for name in other}}
    for y in range(SIDE):
        for x in range(SIDE):
            for c in range(2):
                me = device(y, x, c)
                for name, to in other.items():
                    along_x, along_y = device(y, to[x], c), device(to[y], x, c)
                    out["s" + name].append((me, along_x if c == 0 else along_y))
                    out["t" + name].append((me, along_y if c == 0 else along_x))
                out["core"].append((me, device(y, x, 1 - c)))
    return out


ROUTES = routes()


def send(value, route, what):
    with jax.named_scope(what + "_" + route):
        return lax.ppermute(value, "dp", ROUTES[route])


def in_hbm(x):
    return pltpu.with_memory_space_constraint(x, pltpu.HBM)


def attend_kernel(
    counts, lengths_in, q_in, k_in, v_in, gain_in, down, attended, normed, down_held, lengths, q, k, v, gain, sems
):
    copies = [
        pltpu.make_async_copy(a, b, sems.at[i])
        for i, (a, b) in enumerate(
            (
                (lengths_in, lengths),
                (k_in, k),
                (q_in, q),
                (v_in, v),
                (gain_in, gain),
                (down, down_held),
            )
        )
    ]
    for copy in copies:
        copy.start()
    copies[0].wait()
    row = lax.broadcasted_iota(jnp.int32, (SLOTS, 1), 0)
    starts = jnp.zeros((SLOTS, 1), jnp.int32)
    ends = jnp.zeros((SLOTS, 1), jnp.int32)
    at = jnp.int32(0)
    for i in range(SLOTS):
        after = at + lengths[i]
        starts = jnp.where(row == i, at, starts)
        ends = jnp.where(row == i, after, ends)
        at = after
    position = lax.broadcasted_iota(jnp.int32, (SLOTS, POOL), 1)
    inside = (position >= starts) & (position < ends)
    offset = jnp.where(inside, jnp.float32(0.0), jnp.float32(-1e30))
    live = row < counts[0]
    squares = jnp.zeros((SLOTS, HD), jnp.float32)
    copies[1].wait()
    copies[2].wait()
    for kv in range(KVH):
        heads = range(kv * GROUP, (kv + 1) * GROUP)
        rows = jnp.concatenate([q[:, h * HD : (h + 1) * HD] for h in heads], axis=0)
        scores = lax.dot_general(
            rows,
            k[:, kv * HD : (kv + 1) * HD],
            (((1,), (1,)), ((), ())),
            preferred_element_type=jnp.float32,
        )
        masked = scores.reshape(GROUP, SLOTS, POOL) + offset[None]
        top = jnp.max(masked, axis=-1, keepdims=True)
        raised = jnp.exp((masked - top) * jnp.float32(HD ** (-0.5)))
        total = jnp.sum(raised, axis=-1, keepdims=True)
        if kv == 0:
            copies[3].wait()
        mixed = lax.dot_general(
            raised.astype(jnp.bfloat16).reshape(GROUP * SLOTS, POOL),
            v[:, kv * HD : (kv + 1) * HD],
            (((1,), (0,)), ((), ())),
            preferred_element_type=jnp.float32,
        )
        mixed = mixed.reshape(GROUP, SLOTS, HD) / total
        for g, h in enumerate(heads):
            part = jnp.where(live, mixed[g], jnp.float32(0.0)).astype(jnp.bfloat16)
            attended[:, h * HD : (h + 1) * HD] = part
            wide = part.astype(jnp.float32)
            squares = squares + wide * wide
    mean_square = jnp.sum(squares, axis=-1, keepdims=True) / D
    factor = lax.rsqrt(mean_square + 1e-05)
    copies[4].wait()
    normed[...] = (attended[...].astype(jnp.float32) * factor * gain[...]).astype(jnp.bfloat16)
    copies[5].wait()


def attend(queries, cache_keys, cache_values, lengths, counts, norm_gain, down_rows):
    vmem = pl.BlockSpec(memory_space=pltpu.VMEM)
    any_space = pl.BlockSpec(memory_space=pl.ANY)
    return pl.pallas_call(
        attend_kernel,
        out_shape=(
            jax.ShapeDtypeStruct((SLOTS, D), jnp.bfloat16),
            jax.ShapeDtypeStruct((SLOTS, D), jnp.bfloat16),
            jax.ShapeDtypeStruct((HIDDEN, D), jnp.bfloat16),
        ),
        in_specs=[pl.BlockSpec(memory_space=pltpu.SMEM)] + [any_space] * 6,
        out_specs=(vmem, vmem, vmem),
        scratch_shapes=[
            pltpu.SMEM((SLOTS,), jnp.int32),
            pltpu.VMEM((SLOTS, D), jnp.bfloat16),
            pltpu.VMEM((POOL, KVH * HD), jnp.bfloat16),
            pltpu.VMEM((POOL, KVH * HD), jnp.bfloat16),
            pltpu.VMEM((1, D), jnp.float32),
            pltpu.SemaphoreType.DMA((6,)),
        ],
        compiler_params=pltpu.CompilerParams(vmem_limit_bytes=16 * 2**20),
        name="attend",
    )(counts, *map(in_hbm, (lengths, queries, cache_keys, cache_values, norm_gain.reshape(1, D), down_rows)))


def fetch_kernel(weights, after, held, sem):
    copy = pltpu.make_async_copy(weights, held, sem)
    copy.start()
    copy.wait()


def fetch(weights, after):
    any_space = pl.BlockSpec(memory_space=pl.ANY)
    return pl.pallas_call(
        fetch_kernel,
        out_shape=jax.ShapeDtypeStruct((HIDDEN, D), jnp.bfloat16),
        in_specs=[any_space] * 2,
        out_specs=pl.BlockSpec(memory_space=pltpu.VMEM),
        scratch_shapes=[pltpu.SemaphoreType.DMA],
        compiler_params=pltpu.CompilerParams(vmem_limit_bytes=16 * 2**20),
        cost_estimate=pl.CostEstimate(flops=0, bytes_accessed=4 * HIDDEN * D, transcendentals=0),
        name="fetch",
    )(in_hbm(weights), after)


def ffn_kernel(*args):
    blocks, up, down, outs, (total, hidden) = args[:8], args[8:10], args[10:12], args[12:20], args[20:]
    total[...] = jnp.zeros_like(total)

    @pl.loop(0, D // CHUNK)
    def _(step):
        cols = pl.ds(pl.multiple_of(step * CHUNK, CHUNK), CHUNK)
        total[...] += lax.dot_general(
            jnp.concatenate([w[:, cols] for w in up], axis=0),
            jnp.concatenate([b[:, cols] for b in blocks], axis=0),
            (((1,), (1,)), ((), ())),
            preferred_element_type=jnp.float32,
        )

    value = total[...]
    hidden[...] = (value / (1.0 + jnp.exp(-value))).astype(jnp.bfloat16).T

    @pl.loop(0, D // CHUNK)
    def _(step):
        cols = pl.ds(pl.multiple_of(step * CHUNK, CHUNK), CHUNK)
        product = jnp.dot(
            hidden[...],
            jnp.concatenate([w[:, cols] for w in down], axis=0),
            preferred_element_type=jnp.float32,
        ).astype(jnp.bfloat16)
        for i, out in enumerate(outs):
            out[:, cols] = product[i * PAIR : (i + 1) * PAIR]


def feed_forward(blocks, up, down):
    vmem = pl.BlockSpec(memory_space=pltpu.VMEM)
    return pl.pallas_call(
        ffn_kernel,
        out_shape=[jax.ShapeDtypeStruct((PAIR, D), jnp.bfloat16)] * 8,
        in_specs=[vmem] * 12,
        out_specs=[vmem] * 8,
        scratch_shapes=[
            pltpu.VMEM((2 * HIDDEN, 8 * PAIR), jnp.float32),
            pltpu.VMEM((8 * PAIR, 2 * HIDDEN), jnp.bfloat16),
        ],
        compiler_params=pltpu.CompilerParams(vmem_limit_bytes=16 * 2**20),
        name="feed_forward",
    )(*blocks, *up, *down)


def f32(x):
    return x.astype(jnp.float32)


def pack_kernel(own, near, wrap, far, held, after, first, second, handed):
    first[:SLOTS] = own[...]
    first[SLOTS:] = near[...]
    second[:SLOTS] = wrap[...]
    second[SLOTS:] = far[...]


def pack(own, near, wrap, far, held, after):
    vmem = pl.BlockSpec(memory_space=pltpu.VMEM)
    block = jax.ShapeDtypeStruct((PAIR, D), jnp.bfloat16)
    return pl.pallas_call(
        pack_kernel,
        out_shape=[block, block, jax.ShapeDtypeStruct(held.shape, held.dtype)],
        in_specs=[vmem] * 5 + [pl.BlockSpec(memory_space=pl.ANY)],
        out_specs=[vmem] * 3,
        input_output_aliases={4: 2},
        compiler_params=pltpu.CompilerParams(vmem_limit_bytes=16 * 2**20),
        name="pack",
    )(own, near, wrap, far, held, after)


def merge_kernel(mine, arrived, *refs):
    waiting, (total, *later) = refs[: len(refs) // 2], refs[len(refs) // 2 :]
    total[...] = (mine[...].astype(jnp.float32) + arrived[...].astype(jnp.float32)).astype(jnp.bfloat16)
    for source, target in zip(waiting, later):
        target[...] = source[...]


def merge(mine, arrived, *waiting):
    vmem = pl.BlockSpec(memory_space=pltpu.VMEM)
    n = 1 + len(waiting)
    return pl.pallas_call(
        merge_kernel,
        out_shape=[jax.ShapeDtypeStruct((PAIR, D), jnp.bfloat16)] * n,
        in_specs=[vmem] * (n + 1),
        out_specs=[vmem] * n,
        compiler_params=pltpu.CompilerParams(vmem_limit_bytes=16 * 2**20),
        name="merge",
    )(mine, arrived, *waiting)


def on_device(
    queries, cache_keys, cache_values, lengths, counts, norm_gain, up_weight, down_weight
):
    up_own = up_weight.T
    up_other = send(up_own, "core", "up")
    attended, normed, down_held = attend(
        queries, cache_keys, cache_values, lengths, counts, norm_gain, down_weight
    )
    by_wrap, by_far, by_near = [send(normed, r, "gather") for r in ("swrap", "sfar", "snear")]
    first, second, down_held = pack(normed, by_near, by_wrap, by_far, down_held, up_other)
    down_other = send(down_held, "core", "down")
    up_held = fetch(up_own, second)
    first_w, second_n = send(first, "twrap", "gather"), send(second, "tnear", "gather")
    second_w, first_n = send(second, "twrap", "gather"), send(first, "tnear", "gather")
    first_f, second_f = send(first_w, "tnear", "gather2"), send(second_n, "twrap", "gather2")
    blocks = [first, second, first_w, second_n, first_n, second_w, first_f, second_f]
    first, second, first_w, second_n, first_n, second_w, first_f, second_f = feed_forward(
        blocks, (up_held, up_other), (down_held, down_other)
    )
    far_first = send(first_f, "tnear", "reduce2")
    far_second = send(second_f, "twrap", "reduce2")
    first_w, first_n, second_w = merge(first_w, far_first, first_n, second_w)
    back_first = send(first_w, "twrap", "reduce")
    near_first = send(first_n, "tnear", "reduce")
    near_second = send(second_w, "twrap", "reduce")
    (second_n,) = merge(second_n, far_second)
    back_second = send(second_n, "tnear", "reduce")
    first = f32(first) + f32(near_first) + f32(back_first)
    second = f32(second) + f32(near_second) + f32(back_second)
    home_near = send(first[SLOTS:].astype(jnp.bfloat16), "snear", "home")
    home_wrap = send(second[:SLOTS].astype(jnp.bfloat16), "swrap", "home")
    home_far = send(second[SLOTS:].astype(jnp.bfloat16), "sfar", "home")
    projected = first[:SLOTS] + f32(home_near) + f32(home_wrap) + f32(home_far)
    return (f32(attended) + projected).astype(jnp.bfloat16)


def solution(mesh):
    in_specs = (
        P(("rep", "dp"), None),
        P(("rep", "dp"), None),
        P(("rep", "dp"), None),
        P(("rep", "dp")),
        P(("rep", "dp")),
        P(),
        P(None, "dp"),
        P("dp", None),
    )
    out_specs = P(("rep", "dp"), None)
    return jax.shard_map(
        on_device, mesh=mesh, in_specs=in_specs, out_specs=out_specs, check_vma=False
    )
```

```python
import functools

import jax
import jax.numpy as jnp
from jax import lax
from jax.experimental import pallas as pl
from jax.experimental.pallas import tpu as pltpu
from jax.sharding import PartitionSpec as P

HQ = 48
KVH = 4
HD = 128
GROUP = HQ // KVH
D = HQ * HD
SLOTS = 16
POOL = 1024
HIDDEN = 448
SIDE = 4
PAIR = 2 * SLOTS
CHUNK = 3072


def device(y, x, c):
    return (y * SIDE + x) * 2 + c


def routes():
    other = {"near": (1, 0, 3, 2), "wrap": (3, 2, 1, 0), "far": (2, 3, 0, 1)}
    out = {"core": [], **{axis + name: [] for axis in "st" for name in other}}
    for y in range(SIDE):
        for x in range(SIDE):
            for c in range(2):
                me = device(y, x, c)
                for name, to in other.items():
                    along_x, along_y = device(y, to[x], c), device(to[y], x, c)
                    out["s" + name].append((me, along_x if c == 0 else along_y))
                    out["t" + name].append((me, along_y if c == 0 else along_x))
                out["core"].append((me, device(y, x, 1 - c)))
    return out


ROUTES = routes()


def send(value, route, what):
    with jax.named_scope(what + "_" + route):
        return lax.ppermute(value, "dp", ROUTES[route])


def in_hbm(x):
    return pltpu.with_memory_space_constraint(x, pltpu.HBM)


def attend_kernel(
    counts, lengths_in, q_in, k_in, v_in, gain_in, up, down, attended, normed, weights, lengths, q, k, v, gain, sems
):
    copies = [
        pltpu.make_async_copy(a, b, sems.at[i])
        for i, (a, b) in enumerate(
            (
                (lengths_in, lengths),
                (k_in, k),
                (q_in, q),
                (v_in, v),
                (gain_in, gain),
                (up, weights.at[:HIDDEN]),
                (down, weights.at[HIDDEN:]),
            )
        )
    ]
    for copy in copies:
        copy.start()
    copies[0].wait()
    row = lax.broadcasted_iota(jnp.int32, (SLOTS, 1), 0)
    starts = jnp.zeros((SLOTS, 1), jnp.int32)
    ends = jnp.zeros((SLOTS, 1), jnp.int32)
    at = jnp.int32(0)
    for i in range(SLOTS):
        after = at + lengths[i]
        starts = jnp.where(row == i, at, starts)
        ends = jnp.where(row == i, after, ends)
        at = after
    position = lax.broadcasted_iota(jnp.int32, (SLOTS, POOL), 1)
    inside = (position >= starts) & (position < ends)
    offset = jnp.where(inside, jnp.float32(0.0), jnp.float32(-1e30))
    live = row < counts[0]
    squares = jnp.zeros((SLOTS, HD), jnp.float32)
    copies[1].wait()
    copies[2].wait()
    for kv in range(KVH):
        heads = range(kv * GROUP, (kv + 1) * GROUP)
        rows = jnp.concatenate([q[:, h * HD : (h + 1) * HD] for h in heads], axis=0)
        scores = lax.dot_general(
            rows,
            k[:, kv * HD : (kv + 1) * HD],
            (((1,), (1,)), ((), ())),
            preferred_element_type=jnp.float32,
        )
        masked = scores.reshape(GROUP, SLOTS, POOL) + offset[None]
        top = jnp.max(masked, axis=-1, keepdims=True)
        raised = jnp.exp((masked - top) * jnp.float32(HD ** (-0.5)))
        total = jnp.sum(raised, axis=-1, keepdims=True)
        if kv == 0:
            copies[3].wait()
        mixed = lax.dot_general(
            raised.astype(jnp.bfloat16).reshape(GROUP * SLOTS, POOL),
            v[:, kv * HD : (kv + 1) * HD],
            (((1,), (0,)), ((), ())),
            preferred_element_type=jnp.float32,
        )
        mixed = mixed.reshape(GROUP, SLOTS, HD) / total
        for g, h in enumerate(heads):
            part = jnp.where(live, mixed[g], jnp.float32(0.0)).astype(jnp.bfloat16)
            attended[:, h * HD : (h + 1) * HD] = part
            wide = part.astype(jnp.float32)
            squares = squares + wide * wide
    mean_square = jnp.sum(squares, axis=-1, keepdims=True) / D
    factor = lax.rsqrt(mean_square + 1e-05)
    copies[4].wait()
    normed[...] = (attended[...].astype(jnp.float32) * factor * gain[...]).astype(jnp.bfloat16)
    copies[5].wait()
    copies[6].wait()


def attend(queries, cache_keys, cache_values, lengths, counts, norm_gain, up_rows, down_rows):
    vmem = pl.BlockSpec(memory_space=pltpu.VMEM)
    any_space = pl.BlockSpec(memory_space=pl.ANY)
    return pl.pallas_call(
        attend_kernel,
        out_shape=(
            jax.ShapeDtypeStruct((SLOTS, D), jnp.bfloat16),
            jax.ShapeDtypeStruct((SLOTS, D), jnp.bfloat16),
            jax.ShapeDtypeStruct((2 * HIDDEN, D), jnp.bfloat16),
        ),
        in_specs=[pl.BlockSpec(memory_space=pltpu.SMEM)] + [any_space] * 7,
        out_specs=(vmem, vmem, vmem),
        scratch_shapes=[
            pltpu.SMEM((SLOTS,), jnp.int32),
            pltpu.VMEM((SLOTS, D), jnp.bfloat16),
            pltpu.VMEM((POOL, KVH * HD), jnp.bfloat16),
            pltpu.VMEM((POOL, KVH * HD), jnp.bfloat16),
            pltpu.VMEM((1, D), jnp.float32),
            pltpu.SemaphoreType.DMA((7,)),
        ],
        compiler_params=pltpu.CompilerParams(vmem_limit_bytes=16 * 2**20),
        name="attend",
    )(counts, *map(in_hbm, (lengths, queries, cache_keys, cache_values, norm_gain.reshape(1, D), up_rows, down_rows)))


def up_kernel(*args):
    blocks, weights, (hidden, total) = args[:8], args[8:10], args[10:]
    total[...] = jnp.zeros_like(total)

    @pl.loop(0, D // CHUNK)
    def _(step):
        cols = pl.ds(pl.multiple_of(step * CHUNK, CHUNK), CHUNK)
        total[...] += lax.dot_general(
            jnp.concatenate([w[:HIDDEN, cols] for w in weights], axis=0),
            jnp.concatenate([b[:, cols] for b in blocks], axis=0),
            (((1,), (1,)), ((), ())),
            preferred_element_type=jnp.float32,
        )

    value = total[...]
    hidden[...] = (value / (1.0 + jnp.exp(-value))).astype(jnp.bfloat16).T


def project_up(blocks, weights):
    vmem = pl.BlockSpec(memory_space=pltpu.VMEM)
    rows = len(blocks) * PAIR
    return pl.pallas_call(
        up_kernel,
        out_shape=jax.ShapeDtypeStruct((rows, 2 * HIDDEN), jnp.bfloat16),
        in_specs=[vmem] * 10,
        out_specs=vmem,
        scratch_shapes=[pltpu.VMEM((2 * HIDDEN, rows), jnp.float32)],
        compiler_params=pltpu.CompilerParams(vmem_limit_bytes=16 * 2**20),
        cost_estimate=pl.CostEstimate(flops=4 * rows * HIDDEN * D, bytes_accessed=2 * rows * D, transcendentals=0),
        name="up",
    )(*blocks, *weights)


def down_kernel(begin, hidden, one, two, *outs):
    rows = pl.ds(begin * PAIR, len(outs) * PAIR)

    @pl.loop(0, D // CHUNK)
    def _(step):
        cols = pl.ds(pl.multiple_of(step * CHUNK, CHUNK), CHUNK)
        product = jnp.dot(
            hidden[rows, :],
            jnp.concatenate([one[HIDDEN:, cols], two[HIDDEN:, cols]], axis=0),
            preferred_element_type=jnp.float32,
        ).astype(jnp.bfloat16)
        for i, out in enumerate(outs):
            out[:, cols] = product[i * PAIR : (i + 1) * PAIR]


def project_down(hidden, weights, begin, end):
    vmem = pl.BlockSpec(memory_space=pltpu.VMEM)
    n = end - begin
    return pl.pallas_call(
        functools.partial(down_kernel, begin),
        out_shape=[jax.ShapeDtypeStruct((PAIR, D), jnp.bfloat16)] * n,
        in_specs=[vmem] * 3,
        out_specs=[vmem] * n,
        compiler_params=pltpu.CompilerParams(vmem_limit_bytes=16 * 2**20),
        cost_estimate=pl.CostEstimate(
            flops=4 * n * PAIR * HIDDEN * D, bytes_accessed=2 * n * PAIR * D, transcendentals=0
        ),
        name="down",
    )(hidden, *weights)


def f32(x):
    return x.astype(jnp.float32)


def pack_kernel(one, two, block):
    block[:SLOTS] = one[...]
    block[SLOTS:] = two[...]


def pack(one, two):
    vmem = pl.BlockSpec(memory_space=pltpu.VMEM)
    return pl.pallas_call(
        pack_kernel,
        out_shape=jax.ShapeDtypeStruct((PAIR, D), jnp.bfloat16),
        in_specs=[vmem] * 2,
        out_specs=vmem,
        compiler_params=pltpu.CompilerParams(vmem_limit_bytes=16 * 2**20),
        name="pack",
    )(one, two)


def merge_kernel(mine, arrived, *refs):
    waiting, (total, *later) = refs[: len(refs) // 2], refs[len(refs) // 2 :]
    total[...] = (mine[...].astype(jnp.float32) + arrived[...].astype(jnp.float32)).astype(jnp.bfloat16)
    for source, target in zip(waiting, later):
        target[...] = source[...]


def merge(mine, arrived, *waiting):
    vmem = pl.BlockSpec(memory_space=pltpu.VMEM)
    n = 1 + len(waiting)
    return pl.pallas_call(
        merge_kernel,
        out_shape=[jax.ShapeDtypeStruct((PAIR, D), jnp.bfloat16)] * n,
        in_specs=[vmem] * (n + 1),
        out_specs=[vmem] * n,
        compiler_params=pltpu.CompilerParams(vmem_limit_bytes=16 * 2**20),
        name="merge",
    )(mine, arrived, *waiting)


def on_device(
    queries, cache_keys, cache_values, lengths, counts, norm_gain, up_weight, down_weight
):
    attended, normed, weights = attend(
        queries, cache_keys, cache_values, lengths, counts, norm_gain, up_weight.T, down_weight
    )
    weights = weights, send(weights, "core", "weights")
    by_wrap, by_far, by_near = [send(normed, r, "gather") for r in ("swrap", "sfar", "snear")]
    first = pack(normed, by_near)
    second = pack(by_wrap, by_far)
    first_w, second_n = send(first, "twrap", "gather"), send(second, "tnear", "gather")
    second_w, first_n = send(second, "twrap", "gather"), send(first, "tnear", "gather")
    first_f, second_f = send(first_w, "tnear", "gather2"), send(second_n, "twrap", "gather2")
    hidden = project_up(
        [first, second, first_w, second_n, first_n, second_w, first_f, second_f], weights
    )
    first_f, second_f = project_down(hidden, weights, 6, 8)
    first, second, first_w, second_n, first_n, second_w = project_down(hidden, weights, 0, 6)
    far_first = send(first_f, "tnear", "reduce2")
    far_second = send(second_f, "twrap", "reduce2")
    first_w, first_n, second_w = merge(first_w, far_first, first_n, second_w)
    back_first = send(first_w, "twrap", "reduce")
    near_first = send(first_n, "tnear", "reduce")
    near_second = send(second_w, "twrap", "reduce")
    (second_n,) = merge(second_n, far_second)
    back_second = send(second_n, "tnear", "reduce")
    first = f32(first) + f32(near_first) + f32(back_first)
    second = f32(second) + f32(near_second) + f32(back_second)
    home_near = send(first[SLOTS:].astype(jnp.bfloat16), "snear", "home")
    home_wrap = send(second[:SLOTS].astype(jnp.bfloat16), "swrap", "home")
    home_far = send(second[SLOTS:].astype(jnp.bfloat16), "sfar", "home")
    projected = first[:SLOTS] + f32(home_near) + f32(home_wrap) + f32(home_far)
    return (f32(attended) + projected).astype(jnp.bfloat16)


def solution(mesh):
    in_specs = (
        P(("rep", "dp"), None),
        P(("rep", "dp"), None),
        P(("rep", "dp"), None),
        P(("rep", "dp")),
        P(("rep", "dp")),
        P(),
        P(None, "dp"),
        P("dp", None),
    )
    out_specs = P(("rep", "dp"), None)
    return jax.shard_map(
        on_device, mesh=mesh, in_specs=in_specs, out_specs=out_specs, check_vma=False
    )
```

```python
import functools

import jax
import jax.numpy as jnp
from jax import lax
from jax.experimental import pallas as pl
from jax.experimental.pallas import tpu as pltpu
from jax.sharding import PartitionSpec as P

HQ = 48
KVH = 4
HD = 128
GROUP = HQ // KVH
D = HQ * HD
SLOTS = 16
POOL = 1024
HIDDEN = 448
SIDE = 4
PAIR = 2 * SLOTS
CHUNK = 3072


def device(y, x, c):
    return (y * SIDE + x) * 2 + c


def routes():
    other = {"near": (1, 0, 3, 2), "wrap": (3, 2, 1, 0), "far": (2, 3, 0, 1)}
    out = {"core": [], **{axis + name: [] for axis in "st" for name in other}}
    for y in range(SIDE):
        for x in range(SIDE):
            for c in range(2):
                me = device(y, x, c)
                for name, to in other.items():
                    along_x, along_y = device(y, to[x], c), device(to[y], x, c)
                    out["s" + name].append((me, along_x if c == 0 else along_y))
                    out["t" + name].append((me, along_y if c == 0 else along_x))
                out["core"].append((me, device(y, x, 1 - c)))
    return out


ROUTES = routes()


def send(value, route, what):
    with jax.named_scope(what + "_" + route):
        return lax.ppermute(value, "dp", ROUTES[route])


def in_hbm(x):
    return pltpu.with_memory_space_constraint(x, pltpu.HBM)


def attend_kernel(
    counts, lengths_in, q_in, k_in, v_in, gain_in, down, attended, normed, down_held, lengths, q, k, v, gain, sems
):
    copies = [
        pltpu.make_async_copy(a, b, sems.at[i])
        for i, (a, b) in enumerate(
            (
                (lengths_in, lengths),
                (k_in, k),
                (q_in, q),
                (v_in, v),
                (gain_in, gain),
                (down, down_held),
            )
        )
    ]
    for copy in copies:
        copy.start()
    copies[0].wait()
    row = lax.broadcasted_iota(jnp.int32, (SLOTS, 1), 0)
    starts = jnp.zeros((SLOTS, 1), jnp.int32)
    ends = jnp.zeros((SLOTS, 1), jnp.int32)
    at = jnp.int32(0)
    for i in range(SLOTS):
        after = at + lengths[i]
        starts = jnp.where(row == i, at, starts)
        ends = jnp.where(row == i, after, ends)
        at = after
    position = lax.broadcasted_iota(jnp.int32, (SLOTS, POOL), 1)
    inside = (position >= starts) & (position < ends)
    offset = jnp.where(inside, jnp.float32(0.0), jnp.float32(-1e30))
    live = row < counts[0]
    squares = jnp.zeros((SLOTS, HD), jnp.float32)
    copies[1].wait()
    copies[2].wait()
    for kv in range(KVH):
        heads = range(kv * GROUP, (kv + 1) * GROUP)
        rows = jnp.concatenate([q[:, h * HD : (h + 1) * HD] for h in heads], axis=0)
        scores = lax.dot_general(
            rows,
            k[:, kv * HD : (kv + 1) * HD],
            (((1,), (1,)), ((), ())),
            preferred_element_type=jnp.float32,
        )
        masked = scores.reshape(GROUP, SLOTS, POOL) + offset[None]
        top = jnp.max(masked, axis=-1, keepdims=True)
        raised = jnp.exp((masked - top) * jnp.float32(HD ** (-0.5)))
        total = jnp.sum(raised, axis=-1, keepdims=True)
        if kv == 0:
            copies[3].wait()
        mixed = lax.dot_general(
            raised.astype(jnp.bfloat16).reshape(GROUP * SLOTS, POOL),
            v[:, kv * HD : (kv + 1) * HD],
            (((1,), (0,)), ((), ())),
            preferred_element_type=jnp.float32,
        )
        mixed = mixed.reshape(GROUP, SLOTS, HD) / total
        for g, h in enumerate(heads):
            part = jnp.where(live, mixed[g], jnp.float32(0.0)).astype(jnp.bfloat16)
            attended[:, h * HD : (h + 1) * HD] = part
            wide = part.astype(jnp.float32)
            squares = squares + wide * wide
    mean_square = jnp.sum(squares, axis=-1, keepdims=True) / D
    factor = lax.rsqrt(mean_square + 1e-05)
    copies[4].wait()
    normed[...] = (attended[...].astype(jnp.float32) * factor * gain[...]).astype(jnp.bfloat16)
    copies[5].wait()


def attend(queries, cache_keys, cache_values, lengths, counts, norm_gain, down_rows):
    vmem = pl.BlockSpec(memory_space=pltpu.VMEM)
    any_space = pl.BlockSpec(memory_space=pl.ANY)
    return pl.pallas_call(
        attend_kernel,
        out_shape=(
            jax.ShapeDtypeStruct((SLOTS, D), jnp.bfloat16),
            jax.ShapeDtypeStruct((SLOTS, D), jnp.bfloat16),
            jax.ShapeDtypeStruct((HIDDEN, D), jnp.bfloat16),
        ),
        in_specs=[pl.BlockSpec(memory_space=pltpu.SMEM)] + [any_space] * 6,
        out_specs=(vmem, vmem, vmem),
        scratch_shapes=[
            pltpu.SMEM((SLOTS,), jnp.int32),
            pltpu.VMEM((SLOTS, D), jnp.bfloat16),
            pltpu.VMEM((POOL, KVH * HD), jnp.bfloat16),
            pltpu.VMEM((POOL, KVH * HD), jnp.bfloat16),
            pltpu.VMEM((1, D), jnp.float32),
            pltpu.SemaphoreType.DMA((6,)),
        ],
        compiler_params=pltpu.CompilerParams(vmem_limit_bytes=16 * 2**20),
        name="attend",
    )(counts, *map(in_hbm, (lengths, queries, cache_keys, cache_values, norm_gain.reshape(1, D), down_rows)))


def fetch_kernel(weights, after, held, sem):
    copy = pltpu.make_async_copy(weights, held, sem)
    copy.start()
    copy.wait()


def fetch(weights, after):
    any_space = pl.BlockSpec(memory_space=pl.ANY)
    return pl.pallas_call(
        fetch_kernel,
        out_shape=jax.ShapeDtypeStruct((HIDDEN, D), jnp.bfloat16),
        in_specs=[any_space] * 2,
        out_specs=pl.BlockSpec(memory_space=pltpu.VMEM),
        scratch_shapes=[pltpu.SemaphoreType.DMA],
        compiler_params=pltpu.CompilerParams(vmem_limit_bytes=16 * 2**20),
        cost_estimate=pl.CostEstimate(flops=0, bytes_accessed=4 * HIDDEN * D, transcendentals=0),
        name="fetch",
    )(in_hbm(weights), after)


def ffn_kernel(n, *args):
    blocks, up, down, outs, (total, hidden) = args[:n], args[n : n + 2], args[n + 2 : n + 4], args[n + 4 : -2], args[-2:]
    total[...] = jnp.zeros_like(total)

    @pl.loop(0, D // CHUNK)
    def _(step):
        cols = pl.ds(pl.multiple_of(step * CHUNK, CHUNK), CHUNK)
        total[...] += lax.dot_general(
            jnp.concatenate([b[:, cols] for b in blocks], axis=0),
            jnp.concatenate([w[:, cols] for w in up], axis=0),
            (((1,), (1,)), ((), ())),
            preferred_element_type=jnp.float32,
        )

    value = total[...]
    hidden[...] = (value / (1.0 + jnp.exp(-value))).astype(jnp.bfloat16)

    @pl.loop(0, D // CHUNK)
    def _(step):
        cols = pl.ds(pl.multiple_of(step * CHUNK, CHUNK), CHUNK)
        product = jnp.dot(
            hidden[...],
            jnp.concatenate([w[:, cols] for w in down], axis=0),
            preferred_element_type=jnp.float32,
        ).astype(jnp.bfloat16)
        for i, out in enumerate(outs):
            out[:, cols] = product[i * PAIR : (i + 1) * PAIR]


def feed_forward(blocks, up, down):
    vmem = pl.BlockSpec(memory_space=pltpu.VMEM)
    n = len(blocks)
    rows = n * PAIR
    return pl.pallas_call(
        functools.partial(ffn_kernel, n),
        out_shape=[jax.ShapeDtypeStruct((PAIR, D), jnp.bfloat16)] * n,
        in_specs=[vmem] * (n + 4),
        out_specs=[vmem] * n,
        scratch_shapes=[
            pltpu.VMEM((rows, 2 * HIDDEN), jnp.float32),
            pltpu.VMEM((rows, 2 * HIDDEN), jnp.bfloat16),
        ],
        compiler_params=pltpu.CompilerParams(vmem_limit_bytes=16 * 2**20),
        cost_estimate=pl.CostEstimate(flops=8 * rows * HIDDEN * D, bytes_accessed=4 * rows * D, transcendentals=0),
        name="feed_forward",
    )(*blocks, *up, *down)


def f32(x):
    return x.astype(jnp.float32)


def pack_kernel(own, near, wrap, far, held, after, first, second, handed):
    first[:SLOTS] = wrap[...]
    first[SLOTS:] = far[...]
    second[:SLOTS] = own[...]
    second[SLOTS:] = near[...]


def pack(own, near, wrap, far, held, after):
    vmem = pl.BlockSpec(memory_space=pltpu.VMEM)
    block = jax.ShapeDtypeStruct((PAIR, D), jnp.bfloat16)
    return pl.pallas_call(
        pack_kernel,
        out_shape=[block, block, jax.ShapeDtypeStruct(held.shape, held.dtype)],
        in_specs=[vmem] * 5 + [pl.BlockSpec(memory_space=pl.ANY)],
        out_specs=[vmem] * 3,
        input_output_aliases={4: 2},
        compiler_params=pltpu.CompilerParams(vmem_limit_bytes=16 * 2**20),
        name="pack",
    )(own, near, wrap, far, held, after)


def merge_kernel(mine, arrived, *refs):
    waiting, (total, *later) = refs[: len(refs) // 2], refs[len(refs) // 2 :]
    total[...] = (mine[...].astype(jnp.float32) + arrived[...].astype(jnp.float32)).astype(jnp.bfloat16)
    for source, target in zip(waiting, later):
        target[...] = source[...]


def merge(mine, arrived, *waiting):
    vmem = pl.BlockSpec(memory_space=pltpu.VMEM)
    n = 1 + len(waiting)
    return pl.pallas_call(
        merge_kernel,
        out_shape=[jax.ShapeDtypeStruct((PAIR, D), jnp.bfloat16)] * n,
        in_specs=[vmem] * (n + 1),
        out_specs=[vmem] * n,
        compiler_params=pltpu.CompilerParams(vmem_limit_bytes=16 * 2**20),
        name="merge",
    )(mine, arrived, *waiting)


def on_device(
    queries, cache_keys, cache_values, lengths, counts, norm_gain, up_weight, down_weight
):
    up_own = up_weight.T
    up_other = send(up_own, "core", "up")
    attended, normed, down_held = attend(
        queries, cache_keys, cache_values, lengths, counts, norm_gain, down_weight
    )
    by_wrap, by_far, by_near = [send(normed, r, "gather") for r in ("swrap", "sfar", "snear")]
    first, second, down_held = pack(normed, by_near, by_wrap, by_far, down_held, up_other)
    down_other = send(down_held, "core", "down")
    up_held = fetch(up_own, second)
    first_w, second_n = send(first, "twrap", "gather"), send(second, "tnear", "gather")
    second_w, first_n = send(second, "twrap", "gather"), send(first, "tnear", "gather")
    first_f, second_f = send(first_w, "tnear", "gather2"), send(second_n, "twrap", "gather2")
    up, down = (up_held, up_other), (down_held, down_other)
    first_f, second_f = feed_forward([first_f, second_f], up, down)
    first, second, first_w, second_n, first_n, second_w = feed_forward(
        [first, second, first_w, second_n, first_n, second_w], up, down
    )
    far_first = send(first_f, "tnear", "reduce2")
    far_second = send(second_f, "twrap", "reduce2")
    near_second = send(second_w, "twrap", "reduce")
    first_w, first_n = merge(first_w, far_first, first_n)
    back_first = send(first_w, "twrap", "reduce")
    near_first = send(first_n, "tnear", "reduce")
    (second_n,) = merge(second_n, far_second)
    back_second = send(second_n, "tnear", "reduce")
    first = f32(first) + f32(near_first) + f32(back_first)
    second = f32(second) + f32(near_second) + f32(back_second)
    home_wrap = send(first[:SLOTS].astype(jnp.bfloat16), "swrap", "home")
    home_far = send(first[SLOTS:].astype(jnp.bfloat16), "sfar", "home")
    home_near = send(second[SLOTS:].astype(jnp.bfloat16), "snear", "home")
    projected = second[:SLOTS] + f32(home_near) + f32(home_wrap) + f32(home_far)
    return (f32(attended) + projected).astype(jnp.bfloat16)


def solution(mesh):
    in_specs = (
        P(("rep", "dp"), None),
        P(("rep", "dp"), None),
        P(("rep", "dp"), None),
        P(("rep", "dp")),
        P(("rep", "dp")),
        P(),
        P(None, "dp"),
        P("dp", None),
    )
    out_specs = P(("rep", "dp"), None)
    return jax.shard_map(
        on_device, mesh=mesh, in_specs=in_specs, out_specs=out_specs, check_vma=False
    )
```

```python
import functools

import jax
import jax.numpy as jnp
from jax import lax
from jax.experimental import pallas as pl
from jax.experimental.pallas import tpu as pltpu
from jax.sharding import PartitionSpec as P

HQ = 48
KVH = 4
HD = 128
GROUP = HQ // KVH
D = HQ * HD
SLOTS = 16
POOL = 1024
HIDDEN = 448
SIDE = 4
PAIR = 2 * SLOTS
CHUNK = 3072


def device(y, x, c):
    return (y * SIDE + x) * 2 + c


def routes():
    other = {"near": (1, 0, 3, 2), "wrap": (3, 2, 1, 0), "far": (2, 3, 0, 1)}
    out = {"core": [], **{axis + name: [] for axis in "st" for name in other}}
    for y in range(SIDE):
        for x in range(SIDE):
            for c in range(2):
                me = device(y, x, c)
                for name, to in other.items():
                    along_x, along_y = device(y, to[x], c), device(to[y], x, c)
                    out["s" + name].append((me, along_x if c == 0 else along_y))
                    out["t" + name].append((me, along_y if c == 0 else along_x))
                out["core"].append((me, device(y, x, 1 - c)))
    return out


ROUTES = routes()


def send(value, route, what):
    with jax.named_scope(what + "_" + route):
        return lax.ppermute(value, "dp", ROUTES[route])


def in_hbm(x):
    return pltpu.with_memory_space_constraint(x, pltpu.HBM)


def attend_kernel(
    counts, lengths_in, q_in, k_in, v_in, gain_in, down, attended, normed, down_held, lengths, q, k, v, gain, sems
):
    copies = [
        pltpu.make_async_copy(a, b, sems.at[i])
        for i, (a, b) in enumerate(
            (
                (lengths_in, lengths),
                (k_in, k),
                (q_in, q),
                (v_in, v),
                (gain_in, gain),
                (down, down_held),
            )
        )
    ]
    for copy in copies:
        copy.start()
    copies[0].wait()
    row = lax.broadcasted_iota(jnp.int32, (SLOTS, 1), 0)
    starts = jnp.zeros((SLOTS, 1), jnp.int32)
    ends = jnp.zeros((SLOTS, 1), jnp.int32)
    at = jnp.int32(0)
    for i in range(SLOTS):
        after = at + lengths[i]
        starts = jnp.where(row == i, at, starts)
        ends = jnp.where(row == i, after, ends)
        at = after
    position = lax.broadcasted_iota(jnp.int32, (SLOTS, POOL), 1)
    inside = (position >= starts) & (position < ends)
    offset = jnp.where(inside, jnp.float32(0.0), jnp.float32(-1e30))
    live = row < counts[0]
    squares = jnp.zeros((SLOTS, HD), jnp.float32)
    copies[1].wait()
    copies[2].wait()
    for kv in range(KVH):
        heads = range(kv * GROUP, (kv + 1) * GROUP)
        rows = jnp.concatenate([q[:, h * HD : (h + 1) * HD] for h in heads], axis=0)
        scores = lax.dot_general(
            rows,
            k[:, kv * HD : (kv + 1) * HD],
            (((1,), (1,)), ((), ())),
            preferred_element_type=jnp.float32,
        )
        masked = scores.reshape(GROUP, SLOTS, POOL) + offset[None]
        top = jnp.max(masked, axis=-1, keepdims=True)
        raised = jnp.exp((masked - top) * jnp.float32(HD ** (-0.5)))
        total = jnp.sum(raised, axis=-1, keepdims=True)
        if kv == 0:
            copies[3].wait()
        mixed = lax.dot_general(
            raised.astype(jnp.bfloat16).reshape(GROUP * SLOTS, POOL),
            v[:, kv * HD : (kv + 1) * HD],
            (((1,), (0,)), ((), ())),
            preferred_element_type=jnp.float32,
        )
        mixed = mixed.reshape(GROUP, SLOTS, HD) / total
        for g, h in enumerate(heads):
            part = jnp.where(live, mixed[g], jnp.float32(0.0)).astype(jnp.bfloat16)
            attended[:, h * HD : (h + 1) * HD] = part
            wide = part.astype(jnp.float32)
            squares = squares + wide * wide
    mean_square = jnp.sum(squares, axis=-1, keepdims=True) / D
    factor = lax.rsqrt(mean_square + 1e-05)
    copies[4].wait()
    normed[...] = (attended[...].astype(jnp.float32) * factor * gain[...]).astype(jnp.bfloat16)
    copies[5].wait()


def attend(queries, cache_keys, cache_values, lengths, counts, norm_gain, down_rows):
    vmem = pl.BlockSpec(memory_space=pltpu.VMEM)
    any_space = pl.BlockSpec(memory_space=pl.ANY)
    return pl.pallas_call(
        attend_kernel,
        out_shape=(
            jax.ShapeDtypeStruct((SLOTS, D), jnp.bfloat16),
            jax.ShapeDtypeStruct((SLOTS, D), jnp.bfloat16),
            jax.ShapeDtypeStruct((HIDDEN, D), jnp.bfloat16),
        ),
        in_specs=[pl.BlockSpec(memory_space=pltpu.SMEM)] + [any_space] * 6,
        out_specs=(vmem, vmem, vmem),
        scratch_shapes=[
            pltpu.SMEM((SLOTS,), jnp.int32),
            pltpu.VMEM((SLOTS, D), jnp.bfloat16),
            pltpu.VMEM((POOL, KVH * HD), jnp.bfloat16),
            pltpu.VMEM((POOL, KVH * HD), jnp.bfloat16),
            pltpu.VMEM((1, D), jnp.float32),
            pltpu.SemaphoreType.DMA((6,)),
        ],
        compiler_params=pltpu.CompilerParams(vmem_limit_bytes=16 * 2**20),
        name="attend",
    )(counts, *map(in_hbm, (lengths, queries, cache_keys, cache_values, norm_gain.reshape(1, D), down_rows)))


def fetch_kernel(weights, after, held, sem):
    copy = pltpu.make_async_copy(weights, held, sem)
    copy.start()
    copy.wait()


def fetch(weights, after):
    any_space = pl.BlockSpec(memory_space=pl.ANY)
    return pl.pallas_call(
        fetch_kernel,
        out_shape=jax.ShapeDtypeStruct((HIDDEN, D), jnp.bfloat16),
        in_specs=[any_space] * 2,
        out_specs=pl.BlockSpec(memory_space=pltpu.VMEM),
        scratch_shapes=[pltpu.SemaphoreType.DMA],
        compiler_params=pltpu.CompilerParams(vmem_limit_bytes=16 * 2**20),
        cost_estimate=pl.CostEstimate(flops=0, bytes_accessed=4 * HIDDEN * D, transcendentals=0),
        name="fetch",
    )(in_hbm(weights), after)


def up_kernel(*args):
    blocks, up, (hidden, total) = args[:8], args[8:10], args[10:]
    total[...] = jnp.zeros_like(total)

    @pl.loop(0, D // CHUNK)
    def _(step):
        cols = pl.ds(pl.multiple_of(step * CHUNK, CHUNK), CHUNK)
        total[...] += lax.dot_general(
            jnp.concatenate([w[:, cols] for w in up], axis=0),
            jnp.concatenate([b[:, cols] for b in blocks], axis=0),
            (((1,), (1,)), ((), ())),
            preferred_element_type=jnp.float32,
        )

    value = total[...]
    hidden[...] = (value / (1.0 + jnp.exp(-value))).astype(jnp.bfloat16).T


def project_up(blocks, up):
    vmem = pl.BlockSpec(memory_space=pltpu.VMEM)
    rows = len(blocks) * PAIR
    return pl.pallas_call(
        up_kernel,
        out_shape=jax.ShapeDtypeStruct((rows, 2 * HIDDEN), jnp.bfloat16),
        in_specs=[vmem] * 10,
        out_specs=vmem,
        scratch_shapes=[pltpu.VMEM((2 * HIDDEN, rows), jnp.float32)],
        compiler_params=pltpu.CompilerParams(vmem_limit_bytes=16 * 2**20),
        cost_estimate=pl.CostEstimate(flops=4 * rows * HIDDEN * D, bytes_accessed=2 * rows * D, transcendentals=0),
        name="up",
    )(*blocks, *up)


def down_kernel(begin, hidden, one, two, *outs):
    rows = pl.ds(begin * PAIR, len(outs) * PAIR)

    @pl.loop(0, D // CHUNK)
    def _(step):
        cols = pl.ds(pl.multiple_of(step * CHUNK, CHUNK), CHUNK)
        product = jnp.dot(
            hidden[rows, :],
            jnp.concatenate([one[:, cols], two[:, cols]], axis=0),
            preferred_element_type=jnp.float32,
        ).astype(jnp.bfloat16)
        for i, out in enumerate(outs):
            out[:, cols] = product[i * PAIR : (i + 1) * PAIR]


def project_down(hidden, down, begin, end):
    vmem = pl.BlockSpec(memory_space=pltpu.VMEM)
    n = end - begin
    return pl.pallas_call(
        functools.partial(down_kernel, begin),
        out_shape=[jax.ShapeDtypeStruct((PAIR, D), jnp.bfloat16)] * n,
        in_specs=[vmem] * 3,
        out_specs=[vmem] * n,
        compiler_params=pltpu.CompilerParams(vmem_limit_bytes=16 * 2**20),
        cost_estimate=pl.CostEstimate(
            flops=4 * n * PAIR * HIDDEN * D, bytes_accessed=2 * n * PAIR * D, transcendentals=0
        ),
        name="down",
    )(hidden, *down)


def f32(x):
    return x.astype(jnp.float32)


def pack_kernel(own, near, wrap, far, held, after, first, second, handed):
    first[:SLOTS] = own[...]
    first[SLOTS:] = near[...]
    second[:SLOTS] = wrap[...]
    second[SLOTS:] = far[...]


def pack(own, near, wrap, far, held, after):
    vmem = pl.BlockSpec(memory_space=pltpu.VMEM)
    block = jax.ShapeDtypeStruct((PAIR, D), jnp.bfloat16)
    return pl.pallas_call(
        pack_kernel,
        out_shape=[block, block, jax.ShapeDtypeStruct(held.shape, held.dtype)],
        in_specs=[vmem] * 5 + [pl.BlockSpec(memory_space=pl.ANY)],
        out_specs=[vmem] * 3,
        input_output_aliases={4: 2},
        compiler_params=pltpu.CompilerParams(vmem_limit_bytes=16 * 2**20),
        name="pack",
    )(own, near, wrap, far, held, after)


def merge_kernel(mine, arrived, *refs):
    waiting, (total, *later) = refs[: len(refs) // 2], refs[len(refs) // 2 :]
    total[...] = (mine[...].astype(jnp.float32) + arrived[...].astype(jnp.float32)).astype(jnp.bfloat16)
    for source, target in zip(waiting, later):
        target[...] = source[...]


def merge(mine, arrived, *waiting):
    vmem = pl.BlockSpec(memory_space=pltpu.VMEM)
    n = 1 + len(waiting)
    return pl.pallas_call(
        merge_kernel,
        out_shape=[jax.ShapeDtypeStruct((PAIR, D), jnp.bfloat16)] * n,
        in_specs=[vmem] * (n + 1),
        out_specs=[vmem] * n,
        compiler_params=pltpu.CompilerParams(vmem_limit_bytes=16 * 2**20),
        name="merge",
    )(mine, arrived, *waiting)


def finish_first_kernel(own, near, back, second, second_near, kept, leaving, second_sum):
    def total(rows):
        return sum(x[rows, :].astype(jnp.float32) for x in (own, near, back))

    kept[...] = total(slice(0, SLOTS))
    leaving[...] = total(slice(SLOTS, PAIR)).astype(jnp.bfloat16)
    second_sum[...] = second[...].astype(jnp.float32) + second_near[...].astype(jnp.float32)


def finish_first(*blocks):
    vmem = pl.BlockSpec(memory_space=pltpu.VMEM)
    return pl.pallas_call(
        finish_first_kernel,
        out_shape=[
            jax.ShapeDtypeStruct((SLOTS, D), jnp.float32),
            jax.ShapeDtypeStruct((SLOTS, D), jnp.bfloat16),
            jax.ShapeDtypeStruct((PAIR, D), jnp.float32),
        ],
        in_specs=[vmem] * 5,
        out_specs=[vmem] * 3,
        compiler_params=pltpu.CompilerParams(vmem_limit_bytes=16 * 2**20),
        name="finish_first",
    )(*blocks)


def finish_second_kernel(part, back, one, two):
    value = part[...] + back[...].astype(jnp.float32)
    one[...] = value[:SLOTS].astype(jnp.bfloat16)
    two[...] = value[SLOTS:].astype(jnp.bfloat16)


def finish_second(part, back):
    vmem = pl.BlockSpec(memory_space=pltpu.VMEM)
    return pl.pallas_call(
        finish_second_kernel,
        out_shape=[jax.ShapeDtypeStruct((SLOTS, D), jnp.bfloat16)] * 2,
        in_specs=[vmem] * 2,
        out_specs=[vmem] * 2,
        compiler_params=pltpu.CompilerParams(vmem_limit_bytes=16 * 2**20),
        name="finish_second",
    )(part, back)


def on_device(
    queries, cache_keys, cache_values, lengths, counts, norm_gain, up_weight, down_weight
):
    up_own = up_weight.T
    up_other = send(up_own, "core", "up")
    attended, normed, down_held = attend(
        queries, cache_keys, cache_values, lengths, counts, norm_gain, down_weight
    )
    by_wrap, by_far, by_near = [send(normed, r, "gather") for r in ("swrap", "sfar", "snear")]
    first, second, down_held = pack(normed, by_near, by_wrap, by_far, down_held, up_other)
    down_other = send(down_held, "core", "down")
    up_held = fetch(up_own, second)
    first_w, second_n = send(first, "twrap", "gather"), send(second, "tnear", "gather")
    second_w, first_n = send(second, "twrap", "gather"), send(first, "tnear", "gather")
    first_f, second_f = send(first_w, "tnear", "gather2"), send(second_n, "twrap", "gather2")
    hidden = project_up(
        [first, second, first_w, second_n, first_n, second_w, first_f, second_f], (up_held, up_other)
    )
    down = (down_held, down_other)
    first_f, second_f = project_down(hidden, down, 6, 8)
    first, second, first_w, second_n, first_n, second_w = project_down(hidden, down, 0, 6)
    far_first = send(first_f, "tnear", "reduce2")
    far_second = send(second_f, "twrap", "reduce2")
    near_first = send(first_n, "tnear", "reduce")
    near_second = send(second_w, "twrap", "reduce")
    (first_w,) = merge(first_w, far_first)
    back_first = send(first_w, "twrap", "reduce")
    (second_n,) = merge(second_n, far_second)
    back_second = send(second_n, "tnear", "reduce")
    own, first_out, second_part = finish_first(first, near_first, back_first, second, near_second)
    second_out = finish_second(second_part, back_second)
    home_near = send(first_out, "snear", "home")
    home_wrap = send(second_out[0], "swrap", "home")
    home_far = send(second_out[1], "sfar", "home")
    projected = own + f32(home_near) + f32(home_wrap) + f32(home_far)
    return (f32(attended) + projected).astype(jnp.bfloat16)


def solution(mesh):
    in_specs = (
        P(("rep", "dp"), None),
        P(("rep", "dp"), None),
        P(("rep", "dp"), None),
        P(("rep", "dp")),
        P(("rep", "dp")),
        P(),
        P(None, "dp"),
        P("dp", None),
    )
    out_specs = P(("rep", "dp"), None)
    return jax.shard_map(
        on_device, mesh=mesh, in_specs=in_specs, out_specs=out_specs, check_vma=False
    )
```

```python
import functools

import jax
import jax.numpy as jnp
from jax import lax
from jax.experimental import pallas as pl
from jax.experimental.pallas import tpu as pltpu
from jax.sharding import PartitionSpec as P

HQ = 48
KVH = 4
HD = 128
GROUP = HQ // KVH
D = HQ * HD
SLOTS = 16
POOL = 1024
HIDDEN = 448
SIDE = 4
PAIR = 2 * SLOTS
CHUNK = 3072


def device(y, x, c):
    return (y * SIDE + x) * 2 + c


def routes():
    other = {"near": (1, 0, 3, 2), "wrap": (3, 2, 1, 0), "far": (2, 3, 0, 1)}
    out = {"core": [], **{axis + name: [] for axis in "st" for name in other}}
    for y in range(SIDE):
        for x in range(SIDE):
            for c in range(2):
                me = device(y, x, c)
                for name, to in other.items():
                    along_x, along_y = device(y, to[x], c), device(to[y], x, c)
                    out["s" + name].append((me, along_x if c == 0 else along_y))
                    out["t" + name].append((me, along_y if c == 0 else along_x))
                out["core"].append((me, device(y, x, 1 - c)))
    return out


ROUTES = routes()


def send(value, route, what):
    with jax.named_scope(what + "_" + route):
        return lax.ppermute(value, "dp", ROUTES[route])


def in_hbm(x):
    return pltpu.with_memory_space_constraint(x, pltpu.HBM)


def attend_kernel(
    counts, lengths_in, q_in, k_in, v_in, gain_in, down, attended, normed, down_held, lengths, q, k, v, gain, sems
):
    copies = [
        pltpu.make_async_copy(a, b, sems.at[i])
        for i, (a, b) in enumerate(
            (
                (lengths_in, lengths),
                (k_in, k),
                (q_in, q),
                (v_in, v),
                (gain_in, gain),
                (down, down_held),
            )
        )
    ]
    for copy in copies:
        copy.start()
    copies[0].wait()
    row = lax.broadcasted_iota(jnp.int32, (SLOTS, 1), 0)
    starts = jnp.zeros((SLOTS, 1), jnp.int32)
    ends = jnp.zeros((SLOTS, 1), jnp.int32)
    at = jnp.int32(0)
    for i in range(SLOTS):
        after = at + lengths[i]
        starts = jnp.where(row == i, at, starts)
        ends = jnp.where(row == i, after, ends)
        at = after
    position = lax.broadcasted_iota(jnp.int32, (SLOTS, POOL), 1)
    inside = (position >= starts) & (position < ends)
    offset = jnp.where(inside, jnp.float32(0.0), jnp.float32(-1e30))
    live = row < counts[0]
    squares = jnp.zeros((SLOTS, HD), jnp.float32)
    copies[1].wait()
    copies[2].wait()
    for kv in range(KVH):
        heads = range(kv * GROUP, (kv + 1) * GROUP)
        rows = jnp.concatenate([q[:, h * HD : (h + 1) * HD] for h in heads], axis=0)
        scores = lax.dot_general(
            rows,
            k[:, kv * HD : (kv + 1) * HD],
            (((1,), (1,)), ((), ())),
            preferred_element_type=jnp.float32,
        )
        masked = scores.reshape(GROUP, SLOTS, POOL) + offset[None]
        top = jnp.max(masked, axis=-1, keepdims=True)
        raised = jnp.exp((masked - top) * jnp.float32(HD ** (-0.5)))
        total = jnp.sum(raised, axis=-1, keepdims=True)
        if kv == 0:
            copies[3].wait()
        mixed = lax.dot_general(
            raised.astype(jnp.bfloat16).reshape(GROUP * SLOTS, POOL),
            v[:, kv * HD : (kv + 1) * HD],
            (((1,), (0,)), ((), ())),
            preferred_element_type=jnp.float32,
        )
        mixed = mixed.reshape(GROUP, SLOTS, HD) / total
        for g, h in enumerate(heads):
            part = jnp.where(live, mixed[g], jnp.float32(0.0)).astype(jnp.bfloat16)
            attended[:, h * HD : (h + 1) * HD] = part
            wide = part.astype(jnp.float32)
            squares = squares + wide * wide
    mean_square = jnp.sum(squares, axis=-1, keepdims=True) / D
    factor = lax.rsqrt(mean_square + 1e-05)
    copies[4].wait()
    normed[...] = (attended[...].astype(jnp.float32) * factor * gain[...]).astype(jnp.bfloat16)
    copies[5].wait()


def attend(queries, cache_keys, cache_values, lengths, counts, norm_gain, down_rows):
    vmem = pl.BlockSpec(memory_space=pltpu.VMEM)
    any_space = pl.BlockSpec(memory_space=pl.ANY)
    return pl.pallas_call(
        attend_kernel,
        out_shape=(
            jax.ShapeDtypeStruct((SLOTS, D), jnp.bfloat16),
            jax.ShapeDtypeStruct((SLOTS, D), jnp.bfloat16),
            jax.ShapeDtypeStruct((HIDDEN, D), jnp.bfloat16),
        ),
        in_specs=[pl.BlockSpec(memory_space=pltpu.SMEM)] + [any_space] * 6,
        out_specs=(vmem, vmem, vmem),
        scratch_shapes=[
            pltpu.SMEM((SLOTS,), jnp.int32),
            pltpu.VMEM((SLOTS, D), jnp.bfloat16),
            pltpu.VMEM((POOL, KVH * HD), jnp.bfloat16),
            pltpu.VMEM((POOL, KVH * HD), jnp.bfloat16),
            pltpu.VMEM((1, D), jnp.float32),
            pltpu.SemaphoreType.DMA((6,)),
        ],
        compiler_params=pltpu.CompilerParams(vmem_limit_bytes=16 * 2**20),
        name="attend",
    )(counts, *map(in_hbm, (lengths, queries, cache_keys, cache_values, norm_gain.reshape(1, D), down_rows)))


def fetch_kernel(weights, after, held, sem):
    copy = pltpu.make_async_copy(weights, held, sem)
    copy.start()
    copy.wait()


def fetch(weights, after):
    any_space = pl.BlockSpec(memory_space=pl.ANY)
    return pl.pallas_call(
        fetch_kernel,
        out_shape=jax.ShapeDtypeStruct((HIDDEN, D), jnp.bfloat16),
        in_specs=[any_space] * 2,
        out_specs=pl.BlockSpec(memory_space=pltpu.VMEM),
        scratch_shapes=[pltpu.SemaphoreType.DMA],
        compiler_params=pltpu.CompilerParams(vmem_limit_bytes=16 * 2**20),
        cost_estimate=pl.CostEstimate(flops=0, bytes_accessed=4 * HIDDEN * D, transcendentals=0),
        name="fetch",
    )(in_hbm(weights), after)


def up_kernel(*args):
    blocks, up, (hidden, total) = args[:8], args[8:10], args[10:]
    total[...] = jnp.zeros_like(total)

    @pl.loop(0, D // CHUNK)
    def _(step):
        cols = pl.ds(pl.multiple_of(step * CHUNK, CHUNK), CHUNK)
        total[...] += lax.dot_general(
            jnp.concatenate([w[:, cols] for w in up], axis=0),
            jnp.concatenate([b[:, cols] for b in blocks], axis=0),
            (((1,), (1,)), ((), ())),
            preferred_element_type=jnp.float32,
        )

    value = total[...]
    hidden[...] = (value / (1.0 + jnp.exp(-value))).astype(jnp.bfloat16).T


def project_up(blocks, up):
    vmem = pl.BlockSpec(memory_space=pltpu.VMEM)
    rows = len(blocks) * PAIR
    return pl.pallas_call(
        up_kernel,
        out_shape=jax.ShapeDtypeStruct((rows, 2 * HIDDEN), jnp.bfloat16),
        in_specs=[vmem] * 10,
        out_specs=vmem,
        scratch_shapes=[pltpu.VMEM((2 * HIDDEN, rows), jnp.float32)],
        compiler_params=pltpu.CompilerParams(vmem_limit_bytes=16 * 2**20),
        cost_estimate=pl.CostEstimate(flops=4 * rows * HIDDEN * D, bytes_accessed=2 * rows * D, transcendentals=0),
        name="up",
    )(*blocks, *up)


def down_kernel(begin, hidden, one, two, *outs):
    rows = pl.ds(begin * PAIR, len(outs) * PAIR)

    @pl.loop(0, D // CHUNK)
    def _(step):
        cols = pl.ds(pl.multiple_of(step * CHUNK, CHUNK), CHUNK)
        product = jnp.dot(
            hidden[rows, :],
            jnp.concatenate([one[:, cols], two[:, cols]], axis=0),
            preferred_element_type=jnp.float32,
        ).astype(jnp.bfloat16)
        for i, out in enumerate(outs):
            out[:, cols] = product[i * PAIR : (i + 1) * PAIR]


def project_down(hidden, down, begin, end):
    vmem = pl.BlockSpec(memory_space=pltpu.VMEM)
    n = end - begin
    return pl.pallas_call(
        functools.partial(down_kernel, begin),
        out_shape=[jax.ShapeDtypeStruct((PAIR, D), jnp.bfloat16)] * n,
        in_specs=[vmem] * 3,
        out_specs=[vmem] * n,
        compiler_params=pltpu.CompilerParams(vmem_limit_bytes=16 * 2**20),
        cost_estimate=pl.CostEstimate(
            flops=4 * n * PAIR * HIDDEN * D, bytes_accessed=2 * n * PAIR * D, transcendentals=0
        ),
        name="down",
    )(hidden, *down)


def pack_kernel(own, near, wrap, far, held, after, early, late, handed):
    early[:SLOTS] = own[...]
    early[SLOTS:] = near[...]
    late[:SLOTS] = wrap[...]
    late[SLOTS:] = far[...]


def pack(own, near, wrap, far, held, after):
    vmem = pl.BlockSpec(memory_space=pltpu.VMEM)
    block = jax.ShapeDtypeStruct((PAIR, D), jnp.bfloat16)
    return pl.pallas_call(
        pack_kernel,
        out_shape=[block, block, jax.ShapeDtypeStruct(held.shape, held.dtype)],
        in_specs=[vmem] * 5 + [pl.BlockSpec(memory_space=pl.ANY)],
        out_specs=[vmem] * 3,
        input_output_aliases={4: 2},
        compiler_params=pltpu.CompilerParams(vmem_limit_bytes=16 * 2**20),
        name="pack",
    )(own, near, wrap, far, held, after)


def merge_kernel(n, mine, arrived, *refs):
    waiting, (total, *later) = refs[:n], refs[-n - 1 :]
    total[...] = (mine[...].astype(jnp.float32) + arrived[...].astype(jnp.float32)).astype(jnp.bfloat16)
    for source, target in zip(waiting, later):
        target[...] = source[...]


def merge(mine, arrived, *waiting, after=()):
    vmem = pl.BlockSpec(memory_space=pltpu.VMEM)
    n = len(waiting)
    return pl.pallas_call(
        functools.partial(merge_kernel, n),
        out_shape=[jax.ShapeDtypeStruct((PAIR, D), jnp.bfloat16)] * (1 + n),
        in_specs=[vmem] * (2 + n) + [pl.BlockSpec(memory_space=pl.ANY)] * len(after),
        out_specs=[vmem] * (1 + n),
        compiler_params=pltpu.CompilerParams(vmem_limit_bytes=16 * 2**20),
        name="merge",
    )(mine, arrived, *waiting, *after)


def finish_kernel(own, direct, back, *refs):
    one, two = refs[-2:]
    value = sum(x[...].astype(jnp.float32) for x in (own, direct, back))
    one[...] = value[:SLOTS].astype(one.dtype)
    two[...] = value[SLOTS:].astype(two.dtype)


def finish(own, direct, back, kept_type, after=()):
    vmem = pl.BlockSpec(memory_space=pltpu.VMEM)
    return pl.pallas_call(
        finish_kernel,
        out_shape=[jax.ShapeDtypeStruct((SLOTS, D), kept_type), jax.ShapeDtypeStruct((SLOTS, D), jnp.bfloat16)],
        in_specs=[vmem] * 3 + [pl.BlockSpec(memory_space=pl.ANY)] * len(after),
        out_specs=[vmem] * 2,
        compiler_params=pltpu.CompilerParams(vmem_limit_bytes=16 * 2**20),
        name="finish",
    )(own, direct, back, *after)


def collect_kernel(*refs):
    *parts, out = refs
    out[...] = sum(x[...].astype(jnp.float32) for x in parts)


def collect(*parts):
    vmem = pl.BlockSpec(memory_space=pltpu.VMEM)
    return pl.pallas_call(
        collect_kernel,
        out_shape=jax.ShapeDtypeStruct((SLOTS, D), jnp.float32),
        in_specs=[vmem] * len(parts),
        out_specs=vmem,
        compiler_params=pltpu.CompilerParams(vmem_limit_bytes=16 * 2**20),
        name="collect",
    )(*parts)


def on_device(
    queries, cache_keys, cache_values, lengths, counts, norm_gain, up_weight, down_weight
):
    up_own = up_weight.T
    up_other = send(up_own, "core", "up")
    attended, normed, down_held = attend(
        queries, cache_keys, cache_values, lengths, counts, norm_gain, down_weight
    )
    by_wrap, by_far, by_near = [send(normed, r, "gather") for r in ("swrap", "sfar", "snear")]
    early, late, down_held = pack(normed, by_near, by_wrap, by_far, down_held, up_other)
    down_other = send(down_held, "core", "down")
    early_n, late_w = send(early, "tnear", "gather"), send(late, "twrap", "gather")
    late_n, early_w = send(late, "tnear", "gather"), send(early, "twrap", "gather")
    early_f, late_f = send(early_n, "twrap", "gather2"), send(late_w, "tnear", "gather2")
    up_held = fetch(up_own, late)
    hidden = project_up(
        [early, late, early_n, late_w, early_w, late_n, early_f, late_f], (up_held, up_other)
    )
    down = (down_held, down_other)
    early_f, late_f = project_down(hidden, down, 6, 8)
    early, late, early_n, late_w, early_w, late_n = project_down(hidden, down, 0, 6)
    far_late = send(late_f, "twrap", "reduce2")
    far_early = send(early_f, "tnear", "reduce2")
    direct_late = send(late_w, "twrap", "reduce")
    (late_n,) = merge(late_n, far_late)
    back_late = send(late_n, "tnear", "reduce")
    early_w, early_n = merge(early_w, far_early, early_n, after=(late_n,))
    back_early = send(early_w, "twrap", "reduce")
    direct_early = send(early_n, "tnear", "reduce")
    home_wrap, home_far = finish(late, direct_late, back_late, jnp.bfloat16)
    own, home_near = finish(early, direct_early, back_early, jnp.float32, after=(home_wrap,))
    home_wrap, home_far = send(home_wrap, "swrap", "home"), send(home_far, "sfar", "home")
    home_near = send(home_near, "snear", "home")
    mixed = collect(attended, own, home_wrap, home_far)
    return (mixed + home_near.astype(jnp.float32)).astype(jnp.bfloat16)


def solution(mesh):
    in_specs = (
        P(("rep", "dp"), None),
        P(("rep", "dp"), None),
        P(("rep", "dp"), None),
        P(("rep", "dp")),
        P(("rep", "dp")),
        P(),
        P(None, "dp"),
        P("dp", None),
    )
    out_specs = P(("rep", "dp"), None)
    return jax.shard_map(
        on_device, mesh=mesh, in_specs=in_specs, out_specs=out_specs, check_vma=False
    )
```

```python
import functools
import math

import jax
import jax.numpy as jnp
from jax import lax
from jax.experimental import pallas as pl
from jax.experimental.pallas import tpu as pltpu
from jax.sharding import PartitionSpec as P

HQ = 48
KVH = 4
HD = 128
GROUP = HQ // KVH
D = HQ * HD
SLOTS = 16
POOL = 1024
HIDDEN = 448
SIDE = 4
PAIR = 2 * SLOTS
CHUNK = 3072


def device(y, x, c):
    return (y * SIDE + x) * 2 + c


def routes():
    other = {"near": (1, 0, 3, 2), "wrap": (3, 2, 1, 0), "far": (2, 3, 0, 1)}
    out = {"core": [], **{axis + name: [] for axis in "st" for name in other}}
    for y in range(SIDE):
        for x in range(SIDE):
            for c in range(2):
                me = device(y, x, c)
                for name, to in other.items():
                    along_x, along_y = device(y, to[x], c), device(to[y], x, c)
                    out["s" + name].append((me, along_x if c == 0 else along_y))
                    out["t" + name].append((me, along_y if c == 0 else along_x))
                out["core"].append((me, device(y, x, 1 - c)))
    return out


ROUTES = routes()


def send(value, route, what):
    with jax.named_scope(what + "_" + route):
        return lax.ppermute(value, "dp", ROUTES[route])


def in_hbm(x):
    return pltpu.with_memory_space_constraint(x, pltpu.HBM)


def attend_kernel(
    lengths_in, q_in, k_in, v_in, gain_in, down, attended, normed, down_held, lengths, q, k, v, gain, sems
):
    copies = [
        pltpu.make_async_copy(a, b, sems.at[i])
        for i, (a, b) in enumerate(
            (
                (lengths_in, lengths),
                (k_in, k),
                (q_in, q),
                (v_in, v),
                (gain_in, gain),
                (down, down_held),
            )
        )
    ]
    for copy in copies:
        copy.start()
    copies[0].wait()
    row = lax.broadcasted_iota(jnp.int32, (SLOTS, 1), 0)
    starts = jnp.zeros((SLOTS, 1), jnp.int32)
    ends = jnp.zeros((SLOTS, 1), jnp.int32)
    at = jnp.int32(0)
    for i in range(SLOTS):
        after = at + lengths[i]
        starts = jnp.where(row == i, at, starts)
        ends = jnp.where(row == i, after, ends)
        at = after
    position = lax.broadcasted_iota(jnp.int32, (SLOTS, POOL), 1)
    inside = (position >= starts) & (position < ends)
    offset = jnp.where(inside, jnp.float32(0.0), jnp.float32(-1e30))
    squares = jnp.zeros((SLOTS, HD), jnp.float32)
    ones = jnp.ones((POOL, HD), jnp.bfloat16)
    copies[1].wait()
    copies[2].wait()
    for kv in range(KVH):
        heads = range(kv * GROUP, (kv + 1) * GROUP)
        rows = jnp.concatenate([q[:, h * HD : (h + 1) * HD] for h in heads], axis=0)
        scores = lax.dot_general(
            rows,
            k[:, kv * HD : (kv + 1) * HD],
            (((1,), (1,)), ((), ())),
            preferred_element_type=jnp.float32,
        )
        masked = scores.reshape(GROUP, SLOTS, POOL) + offset[None]
        top = jnp.max(masked, axis=-1, keepdims=True)
        raised = jnp.exp2((masked - top) * jnp.float32(HD ** (-0.5) * math.log2(math.e)))
        if kv == 0:
            copies[3].wait()
        mixed = lax.dot_general(
            raised.astype(jnp.bfloat16).reshape(GROUP * SLOTS, POOL),
            jnp.concatenate([v[:, kv * HD : (kv + 1) * HD], ones], axis=1),
            (((1,), (0,)), ((), ())),
            preferred_element_type=jnp.float32,
        )
        mixed = (mixed[:, :HD] / mixed[:, HD:]).reshape(GROUP, SLOTS, HD)
        for g, h in enumerate(heads):
            part = mixed[g].astype(jnp.bfloat16)
            attended[:, h * HD : (h + 1) * HD] = part
            wide = part.astype(jnp.float32)
            squares = squares + wide * wide
    mean_square = jnp.sum(squares, axis=-1, keepdims=True) / D
    factor = lax.rsqrt(mean_square + 1e-05)
    copies[4].wait()
    normed[...] = (attended[...].astype(jnp.float32) * factor * gain[...]).astype(jnp.bfloat16)
    copies[5].wait()


def attend(queries, cache_keys, cache_values, lengths, norm_gain, down_rows):
    vmem = pl.BlockSpec(memory_space=pltpu.VMEM)
    any_space = pl.BlockSpec(memory_space=pl.ANY)
    return pl.pallas_call(
        attend_kernel,
        out_shape=(
            jax.ShapeDtypeStruct((SLOTS, D), jnp.bfloat16),
            jax.ShapeDtypeStruct((SLOTS, D), jnp.bfloat16),
            jax.ShapeDtypeStruct((HIDDEN, D), jnp.bfloat16),
        ),
        in_specs=[any_space] * 6,
        out_specs=(vmem, vmem, vmem),
        scratch_shapes=[
            pltpu.SMEM((SLOTS,), jnp.int32),
            pltpu.VMEM((SLOTS, D), jnp.bfloat16),
            pltpu.VMEM((POOL, KVH * HD), jnp.bfloat16),
            pltpu.VMEM((POOL, KVH * HD), jnp.bfloat16),
            pltpu.VMEM((1, D), jnp.float32),
            pltpu.SemaphoreType.DMA((6,)),
        ],
        compiler_params=pltpu.CompilerParams(vmem_limit_bytes=16 * 2**20),
        name="attend",
    )(*map(in_hbm, (lengths, queries, cache_keys, cache_values, norm_gain.reshape(1, D), down_rows)))


def fetch_kernel(weights, after, held, sem):
    copy = pltpu.make_async_copy(weights, held, sem)
    copy.start()
    copy.wait()


def fetch(weights, after):
    any_space = pl.BlockSpec(memory_space=pl.ANY)
    return pl.pallas_call(
        fetch_kernel,
        out_shape=jax.ShapeDtypeStruct((HIDDEN, D), jnp.bfloat16),
        in_specs=[any_space] * 2,
        out_specs=pl.BlockSpec(memory_space=pltpu.VMEM),
        scratch_shapes=[pltpu.SemaphoreType.DMA],
        compiler_params=pltpu.CompilerParams(vmem_limit_bytes=16 * 2**20),
        cost_estimate=pl.CostEstimate(flops=0, bytes_accessed=4 * HIDDEN * D, transcendentals=0),
        name="fetch",
    )(in_hbm(weights), after)


def up_kernel(*args):
    blocks, up, (hidden, total) = args[:8], args[8:10], args[10:]
    total[...] = jnp.zeros_like(total)

    @pl.loop(0, D // CHUNK)
    def _(step):
        cols = pl.ds(pl.multiple_of(step * CHUNK, CHUNK), CHUNK)
        total[...] += lax.dot_general(
            jnp.concatenate([w[:, cols] for w in up], axis=0),
            jnp.concatenate([b[:, cols] for b in blocks], axis=0),
            (((1,), (1,)), ((), ())),
            preferred_element_type=jnp.float32,
        )

    value = total[...]
    hidden[...] = (value / (1.0 + jnp.exp(-value))).astype(jnp.bfloat16).T


def project_up(blocks, up):
    vmem = pl.BlockSpec(memory_space=pltpu.VMEM)
    rows = len(blocks) * PAIR
    return pl.pallas_call(
        up_kernel,
        out_shape=jax.ShapeDtypeStruct((rows, 2 * HIDDEN), jnp.bfloat16),
        in_specs=[vmem] * 10,
        out_specs=vmem,
        scratch_shapes=[pltpu.VMEM((2 * HIDDEN, rows), jnp.float32)],
        compiler_params=pltpu.CompilerParams(vmem_limit_bytes=16 * 2**20),
        cost_estimate=pl.CostEstimate(flops=4 * rows * HIDDEN * D, bytes_accessed=2 * rows * D, transcendentals=0),
        name="up",
    )(*blocks, *up)


def down_kernel(begin, hidden, one, two, *outs):
    rows = pl.ds(begin * PAIR, len(outs) * PAIR)

    @pl.loop(0, D // CHUNK)
    def _(step):
        cols = pl.ds(pl.multiple_of(step * CHUNK, CHUNK), CHUNK)
        product = jnp.dot(
            hidden[rows, :],
            jnp.concatenate([one[:, cols], two[:, cols]], axis=0),
            preferred_element_type=jnp.float32,
        ).astype(jnp.bfloat16)
        for i, out in enumerate(outs):
            out[:, cols] = product[i * PAIR : (i + 1) * PAIR]


def project_down(hidden, down, begin, end):
    vmem = pl.BlockSpec(memory_space=pltpu.VMEM)
    n = end - begin
    return pl.pallas_call(
        functools.partial(down_kernel, begin),
        out_shape=[jax.ShapeDtypeStruct((PAIR, D), jnp.bfloat16)] * n,
        in_specs=[vmem] * 3,
        out_specs=[vmem] * n,
        compiler_params=pltpu.CompilerParams(vmem_limit_bytes=16 * 2**20),
        cost_estimate=pl.CostEstimate(
            flops=4 * n * PAIR * HIDDEN * D, bytes_accessed=2 * n * PAIR * D, transcendentals=0
        ),
        name="down",
    )(hidden, *down)


def pack_kernel(own, near, wrap, far, held, after, early, late, handed):
    early[:SLOTS] = own[...]
    early[SLOTS:] = near[...]
    late[:SLOTS] = wrap[...]
    late[SLOTS:] = far[...]


def pack(own, near, wrap, far, held, after):
    vmem = pl.BlockSpec(memory_space=pltpu.VMEM)
    block = jax.ShapeDtypeStruct((PAIR, D), jnp.bfloat16)
    return pl.pallas_call(
        pack_kernel,
        out_shape=[block, block, jax.ShapeDtypeStruct(held.shape, held.dtype)],
        in_specs=[vmem] * 5 + [pl.BlockSpec(memory_space=pl.ANY)],
        out_specs=[vmem] * 3,
        input_output_aliases={4: 2},
        compiler_params=pltpu.CompilerParams(vmem_limit_bytes=16 * 2**20),
        name="pack",
    )(own, near, wrap, far, held, after)


def merge_kernel(n, mine, arrived, *refs):
    waiting, (total, *later) = refs[:n], refs[-n - 1 :]
    total[...] = (mine[...].astype(jnp.float32) + arrived[...].astype(jnp.float32)).astype(jnp.bfloat16)
    for source, target in zip(waiting, later):
        target[...] = source[...]


def merge(mine, arrived, *waiting, after=()):
    vmem = pl.BlockSpec(memory_space=pltpu.VMEM)
    n = len(waiting)
    return pl.pallas_call(
        functools.partial(merge_kernel, n),
        out_shape=[jax.ShapeDtypeStruct((PAIR, D), jnp.bfloat16)] * (1 + n),
        in_specs=[vmem] * (2 + n) + [pl.BlockSpec(memory_space=pl.ANY)] * len(after),
        out_specs=[vmem] * (1 + n),
        compiler_params=pltpu.CompilerParams(vmem_limit_bytes=16 * 2**20),
        name="merge",
    )(mine, arrived, *waiting, *after)


def finish_kernel(own, direct, back, *refs):
    one, two = refs[-2:]
    value = sum(x[...].astype(jnp.float32) for x in (own, direct, back))
    one[...] = value[:SLOTS].astype(one.dtype)
    two[...] = value[SLOTS:].astype(two.dtype)


def finish(own, direct, back, kept_type, after=()):
    vmem = pl.BlockSpec(memory_space=pltpu.VMEM)
    return pl.pallas_call(
        finish_kernel,
        out_shape=[jax.ShapeDtypeStruct((SLOTS, D), kept_type), jax.ShapeDtypeStruct((SLOTS, D), jnp.bfloat16)],
        in_specs=[vmem] * 3 + [pl.BlockSpec(memory_space=pl.ANY)] * len(after),
        out_specs=[vmem] * 2,
        compiler_params=pltpu.CompilerParams(vmem_limit_bytes=16 * 2**20),
        name="finish",
    )(own, direct, back, *after)


def collect_kernel(*refs):
    *parts, out = refs
    out[...] = sum(x[...].astype(jnp.float32) for x in parts)


def collect(*parts):
    vmem = pl.BlockSpec(memory_space=pltpu.VMEM)
    return pl.pallas_call(
        collect_kernel,
        out_shape=jax.ShapeDtypeStruct((SLOTS, D), jnp.float32),
        in_specs=[vmem] * len(parts),
        out_specs=vmem,
        compiler_params=pltpu.CompilerParams(vmem_limit_bytes=16 * 2**20),
        name="collect",
    )(*parts)


def on_device(
    queries, cache_keys, cache_values, lengths, counts, norm_gain, up_weight, down_weight
):
    up_own = up_weight.T
    up_other = send(up_own, "core", "up")
    attended, normed, down_held = attend(
        queries, cache_keys, cache_values, lengths, norm_gain, down_weight
    )
    by_wrap, by_far, by_near = [send(normed, r, "gather") for r in ("swrap", "sfar", "snear")]
    early, late, down_held = pack(normed, by_near, by_wrap, by_far, down_held, up_other)
    down_other = send(down_held, "core", "down")
    early_n, late_w = send(early, "tnear", "gather"), send(late, "twrap", "gather")
    late_n, early_w = send(late, "tnear", "gather"), send(early, "twrap", "gather")
    early_f, late_f = send(early_n, "twrap", "gather2"), send(late_w, "tnear", "gather2")
    up_held = fetch(up_own, late)
    hidden = project_up(
        [early, late, early_n, late_w, early_w, late_n, early_f, late_f], (up_held, up_other)
    )
    down = (down_held, down_other)
    early_f, late_f = project_down(hidden, down, 6, 8)
    early, late, early_n, late_w, early_w, late_n = project_down(hidden, down, 0, 6)
    far_late = send(late_f, "twrap", "reduce2")
    far_early = send(early_f, "tnear", "reduce2")
    direct_late = send(late_w, "twrap", "reduce")
    (late_n,) = merge(late_n, far_late)
    back_late = send(late_n, "tnear", "reduce")
    direct_early = send(early_n, "tnear", "reduce")
    (early_w,) = merge(early_w, far_early, after=(late_n,))
    back_early = send(early_w, "twrap", "reduce")
    home_wrap, home_far = finish(late, direct_late, back_late, jnp.bfloat16, after=(direct_early,))
    own, home_near = finish(early, direct_early, back_early, jnp.float32, after=(home_wrap,))
    home_wrap, home_far = send(home_wrap, "swrap", "home"), send(home_far, "sfar", "home")
    home_near = send(home_near, "snear", "home")
    mixed = collect(attended, own, home_wrap, home_far)
    live = jnp.arange(SLOTS, dtype=jnp.int32)[:, None] < counts[0]
    return jnp.where(live, mixed + home_near.astype(jnp.float32), jnp.float32(0.0)).astype(jnp.bfloat16)


def solution(mesh):
    in_specs = (
        P(("rep", "dp"), None),
        P(("rep", "dp"), None),
        P(("rep", "dp"), None),
        P(("rep", "dp")),
        P(("rep", "dp")),
        P(),
        P(None, "dp"),
        P("dp", None),
    )
    out_specs = P(("rep", "dp"), None)
    return jax.shard_map(
        on_device, mesh=mesh, in_specs=in_specs, out_specs=out_specs, check_vma=False
    )
```

```python
import functools
import math

import jax
import jax.numpy as jnp
from jax import lax
from jax.experimental import pallas as pl
from jax.experimental.pallas import tpu as pltpu
from jax.sharding import PartitionSpec as P

HQ = 48
KVH = 4
HD = 128
GROUP = HQ // KVH
D = HQ * HD
SLOTS = 16
POOL = 1024
HIDDEN = 448
SIDE = 4
PAIR = 2 * SLOTS
CHUNK = 3072


def device(y, x, c):
    return (y * SIDE + x) * 2 + c


def routes():
    other = {"near": (1, 0, 3, 2), "wrap": (3, 2, 1, 0), "far": (2, 3, 0, 1)}
    out = {"core": [], **{axis + name: [] for axis in "st" for name in other}}
    for y in range(SIDE):
        for x in range(SIDE):
            for c in range(2):
                me = device(y, x, c)
                for name, to in other.items():
                    along_x, along_y = device(y, to[x], c), device(to[y], x, c)
                    out["s" + name].append((me, along_x if c == 0 else along_y))
                    out["t" + name].append((me, along_y if c == 0 else along_x))
                out["core"].append((me, device(y, x, 1 - c)))
    return out


ROUTES = routes()


def send(value, route, what):
    with jax.named_scope(what + "_" + route):
        return lax.ppermute(value, "dp", ROUTES[route])


def in_hbm(x):
    return pltpu.with_memory_space_constraint(x, pltpu.HBM)


def attend_kernel(
    lengths_in, q_in, k_in, v_in, gain_in, down, attended, normed, down_held, lengths, q, k, v, gain, sems
):
    copies = [
        pltpu.make_async_copy(a, b, sems.at[i])
        for i, (a, b) in enumerate(
            (
                (lengths_in, lengths),
                (k_in, k),
                (q_in, q),
                (v_in, v),
                (gain_in, gain),
                (down, down_held),
            )
        )
    ]
    for copy in copies:
        copy.start()
    copies[0].wait()
    row = lax.broadcasted_iota(jnp.int32, (SLOTS, 1), 0)
    starts = jnp.zeros((SLOTS, 1), jnp.int32)
    ends = jnp.zeros((SLOTS, 1), jnp.int32)
    at = jnp.int32(0)
    for i in range(SLOTS):
        after = at + lengths[i]
        starts = jnp.where(row == i, at, starts)
        ends = jnp.where(row == i, after, ends)
        at = after
    position = lax.broadcasted_iota(jnp.int32, (SLOTS, POOL), 1)
    inside = (position >= starts) & (position < ends)
    offset = jnp.where(inside, jnp.float32(0.0), jnp.float32(-1e30))
    squares = jnp.zeros((SLOTS, HD), jnp.float32)
    ones = jnp.ones((POOL, HD), jnp.bfloat16)
    copies[1].wait()
    copies[2].wait()
    for kv in range(KVH):
        heads = range(kv * GROUP, (kv + 1) * GROUP)
        rows = jnp.concatenate([q[:, h * HD : (h + 1) * HD] for h in heads], axis=0)
        scores = lax.dot_general(
            rows,
            k[:, kv * HD : (kv + 1) * HD],
            (((1,), (1,)), ((), ())),
            preferred_element_type=jnp.float32,
        )
        masked = scores.reshape(GROUP, SLOTS, POOL) + offset[None]
        top = jnp.max(masked, axis=-1, keepdims=True)
        raised = jnp.exp2((masked - top) * jnp.float32(HD ** (-0.5) * math.log2(math.e)))
        if kv == 0:
            copies[3].wait()
        mixed = lax.dot_general(
            raised.astype(jnp.bfloat16).reshape(GROUP * SLOTS, POOL),
            jnp.concatenate([v[:, kv * HD : (kv + 1) * HD], ones], axis=1),
            (((1,), (0,)), ((), ())),
            preferred_element_type=jnp.float32,
        )
        mixed = (mixed[:, :HD] / mixed[:, HD:]).reshape(GROUP, SLOTS, HD)
        for g, h in enumerate(heads):
            part = mixed[g].astype(jnp.bfloat16)
            attended[:, h * HD : (h + 1) * HD] = part
            wide = part.astype(jnp.float32)
            squares = squares + wide * wide
    mean_square = jnp.sum(squares, axis=-1, keepdims=True) / D
    factor = lax.rsqrt(mean_square + 1e-05)
    copies[4].wait()
    normed[...] = (attended[...].astype(jnp.float32) * factor * gain[...]).astype(jnp.bfloat16)
    copies[5].wait()


def attend(queries, cache_keys, cache_values, lengths, norm_gain, down_rows):
    vmem = pl.BlockSpec(memory_space=pltpu.VMEM)
    any_space = pl.BlockSpec(memory_space=pl.ANY)
    return pl.pallas_call(
        attend_kernel,
        out_shape=(
            jax.ShapeDtypeStruct((SLOTS, D), jnp.bfloat16),
            jax.ShapeDtypeStruct((SLOTS, D), jnp.bfloat16),
            jax.ShapeDtypeStruct((HIDDEN, D), jnp.bfloat16),
        ),
        in_specs=[any_space] * 6,
        out_specs=(vmem, vmem, vmem),
        scratch_shapes=[
            pltpu.SMEM((SLOTS,), jnp.int32),
            pltpu.VMEM((SLOTS, D), jnp.bfloat16),
            pltpu.VMEM((POOL, KVH * HD), jnp.bfloat16),
            pltpu.VMEM((POOL, KVH * HD), jnp.bfloat16),
            pltpu.VMEM((1, D), jnp.float32),
            pltpu.SemaphoreType.DMA((6,)),
        ],
        compiler_params=pltpu.CompilerParams(vmem_limit_bytes=16 * 2**20),
        name="attend",
    )(*map(in_hbm, (lengths, queries, cache_keys, cache_values, norm_gain.reshape(1, D), down_rows)))


def fetch_kernel(weights, after, held, sem):
    copy = pltpu.make_async_copy(weights, held, sem)
    copy.start()
    copy.wait()


def fetch(weights, after):
    any_space = pl.BlockSpec(memory_space=pl.ANY)
    return pl.pallas_call(
        fetch_kernel,
        out_shape=jax.ShapeDtypeStruct((HIDDEN, D), jnp.bfloat16),
        in_specs=[any_space] * 2,
        out_specs=pl.BlockSpec(memory_space=pltpu.VMEM),
        scratch_shapes=[pltpu.SemaphoreType.DMA],
        compiler_params=pltpu.CompilerParams(vmem_limit_bytes=16 * 2**20),
        cost_estimate=pl.CostEstimate(flops=10**11, bytes_accessed=4 * HIDDEN * D, transcendentals=0),
        name="fetch",
    )(in_hbm(weights), after)


def up_kernel(*args):
    blocks, up, (hidden, total) = args[:8], args[8:10], args[10:]
    total[...] = jnp.zeros_like(total)

    @pl.loop(0, D // CHUNK)
    def _(step):
        cols = pl.ds(pl.multiple_of(step * CHUNK, CHUNK), CHUNK)
        total[...] += lax.dot_general(
            jnp.concatenate([w[:, cols] for w in up], axis=0),
            jnp.concatenate([b[:, cols] for b in blocks], axis=0),
            (((1,), (1,)), ((), ())),
            preferred_element_type=jnp.float32,
        )

    value = total[...]
    hidden[...] = (value / (1.0 + jnp.exp(-value))).astype(jnp.bfloat16).T


def project_up(blocks, up):
    vmem = pl.BlockSpec(memory_space=pltpu.VMEM)
    rows = len(blocks) * PAIR
    return pl.pallas_call(
        up_kernel,
        out_shape=jax.ShapeDtypeStruct((rows, 2 * HIDDEN), jnp.bfloat16),
        in_specs=[vmem] * 10,
        out_specs=vmem,
        scratch_shapes=[pltpu.VMEM((2 * HIDDEN, rows), jnp.float32)],
        compiler_params=pltpu.CompilerParams(vmem_limit_bytes=16 * 2**20),
        cost_estimate=pl.CostEstimate(flops=4 * rows * HIDDEN * D, bytes_accessed=2 * rows * D, transcendentals=0),
        name="up",
    )(*blocks, *up)


def down_kernel(begin, hidden, one, two, *outs):
    rows = pl.ds(begin * PAIR, len(outs) * PAIR)

    @pl.loop(0, D // CHUNK)
    def _(step):
        cols = pl.ds(pl.multiple_of(step * CHUNK, CHUNK), CHUNK)
        product = jnp.dot(
            hidden[rows, :],
            jnp.concatenate([one[:, cols], two[:, cols]], axis=0),
            preferred_element_type=jnp.float32,
        ).astype(jnp.bfloat16)
        for i, out in enumerate(outs):
            out[:, cols] = product[i * PAIR : (i + 1) * PAIR]


def project_down(hidden, down, begin, end):
    vmem = pl.BlockSpec(memory_space=pltpu.VMEM)
    n = end - begin
    return pl.pallas_call(
        functools.partial(down_kernel, begin),
        out_shape=[jax.ShapeDtypeStruct((PAIR, D), jnp.bfloat16)] * n,
        in_specs=[vmem] * 3,
        out_specs=[vmem] * n,
        compiler_params=pltpu.CompilerParams(vmem_limit_bytes=16 * 2**20),
        cost_estimate=pl.CostEstimate(
            flops=4 * n * PAIR * HIDDEN * D, bytes_accessed=2 * n * PAIR * D, transcendentals=0
        ),
        name="down",
    )(hidden, *down)


def pack_kernel(one, two, block):
    block[:SLOTS] = one[...]
    block[SLOTS:] = two[...]


def pack(one, two):
    vmem = pl.BlockSpec(memory_space=pltpu.VMEM)
    return pl.pallas_call(
        pack_kernel,
        out_shape=jax.ShapeDtypeStruct((PAIR, D), jnp.bfloat16),
        in_specs=[vmem] * 2,
        out_specs=vmem,
        compiler_params=pltpu.CompilerParams(vmem_limit_bytes=16 * 2**20),
        name="pack",
    )(one, two)


def hand_kernel(*refs):
    pass


def hand(held, *after):
    vmem = pl.BlockSpec(memory_space=pltpu.VMEM)
    return pl.pallas_call(
        hand_kernel,
        out_shape=jax.ShapeDtypeStruct(held.shape, held.dtype),
        in_specs=[vmem] + [pl.BlockSpec(memory_space=pl.ANY)] * len(after),
        out_specs=vmem,
        input_output_aliases={0: 0},
        compiler_params=pltpu.CompilerParams(vmem_limit_bytes=16 * 2**20),
        name="hand",
    )(held, *after)


def merge_kernel(n, mine, arrived, *refs):
    waiting, (total, *later) = refs[:n], refs[-n - 1 :]
    total[...] = (mine[...].astype(jnp.float32) + arrived[...].astype(jnp.float32)).astype(jnp.bfloat16)
    for source, target in zip(waiting, later):
        target[...] = source[...]


def merge(mine, arrived, *waiting, after=()):
    vmem = pl.BlockSpec(memory_space=pltpu.VMEM)
    n = len(waiting)
    return pl.pallas_call(
        functools.partial(merge_kernel, n),
        out_shape=[jax.ShapeDtypeStruct((PAIR, D), jnp.bfloat16)] * (1 + n),
        in_specs=[vmem] * (2 + n) + [pl.BlockSpec(memory_space=pl.ANY)] * len(after),
        out_specs=[vmem] * (1 + n),
        compiler_params=pltpu.CompilerParams(vmem_limit_bytes=16 * 2**20),
        name="merge",
    )(mine, arrived, *waiting, *after)


def finish_kernel(own, direct, back, *refs):
    one, two = refs[-2:]
    value = sum(x[...].astype(jnp.float32) for x in (own, direct, back))
    one[...] = value[:SLOTS].astype(one.dtype)
    two[...] = value[SLOTS:].astype(two.dtype)


def finish(own, direct, back, kept_type, after=()):
    vmem = pl.BlockSpec(memory_space=pltpu.VMEM)
    return pl.pallas_call(
        finish_kernel,
        out_shape=[jax.ShapeDtypeStruct((SLOTS, D), kept_type), jax.ShapeDtypeStruct((SLOTS, D), jnp.bfloat16)],
        in_specs=[vmem] * 3 + [pl.BlockSpec(memory_space=pl.ANY)] * len(after),
        out_specs=[vmem] * 2,
        compiler_params=pltpu.CompilerParams(vmem_limit_bytes=16 * 2**20),
        name="finish",
    )(own, direct, back, *after)


def collect_kernel(*refs):
    *parts, out = refs
    out[...] = sum(x[...].astype(jnp.float32) for x in parts)


def collect(*parts):
    vmem = pl.BlockSpec(memory_space=pltpu.VMEM)
    return pl.pallas_call(
        collect_kernel,
        out_shape=jax.ShapeDtypeStruct((SLOTS, D), jnp.float32),
        in_specs=[vmem] * len(parts),
        out_specs=vmem,
        compiler_params=pltpu.CompilerParams(vmem_limit_bytes=16 * 2**20),
        name="collect",
    )(*parts)


def on_device(
    queries, cache_keys, cache_values, lengths, counts, norm_gain, up_weight, down_weight
):
    up_own = up_weight.T
    up_other = send(up_own, "core", "up")
    attended, normed, down_held = attend(
        queries, cache_keys, cache_values, lengths, norm_gain, down_weight
    )
    by_wrap, by_far, by_near = [send(normed, r, "gather") for r in ("swrap", "sfar", "snear")]
    early = pack(normed, by_near)
    late = pack(by_wrap, by_far)
    early_n, late_w = send(early, "tnear", "gather"), send(late, "twrap", "gather")
    late_n, early_w = send(late, "tnear", "gather"), send(early, "twrap", "gather")
    early_n = hand(early_n, early_w)
    early_f, late_f = send(early_n, "twrap", "gather2"), send(late_w, "tnear", "gather2")
    down_held = hand(down_held, up_other)
    down_other = send(down_held, "core", "down")
    up_held = fetch(up_own, late)
    hidden = project_up(
        [early, late, early_n, late_w, early_w, late_n, early_f, late_f], (up_held, up_other)
    )
    down = (down_held, down_other)
    early_f, late_f = project_down(hidden, down, 6, 8)
    early, late, early_n, late_w, early_w, late_n = project_down(hidden, down, 0, 6)
    far_late = send(late_f, "twrap", "reduce2")
    far_early = send(early_f, "tnear", "reduce2")
    direct_late = send(late_w, "twrap", "reduce")
    (late_n,) = merge(late_n, far_late)
    back_late = send(late_n, "tnear", "reduce")
    direct_early = send(early_n, "tnear", "reduce")
    (early_w,) = merge(early_w, far_early, after=(late_n,))
    back_early = send(early_w, "twrap", "reduce")
    home_wrap, home_far = finish(late, direct_late, back_late, jnp.bfloat16, after=(direct_early,))
    own, home_near = finish(early, direct_early, back_early, jnp.float32, after=(home_wrap,))
    home_wrap, home_far = send(home_wrap, "swrap", "home"), send(home_far, "sfar", "home")
    home_near = send(home_near, "snear", "home")
    mixed = collect(attended, own, home_wrap, home_far)
    live = jnp.arange(SLOTS, dtype=jnp.int32)[:, None] < counts[0]
    return jnp.where(live, mixed + home_near.astype(jnp.float32), jnp.float32(0.0)).astype(jnp.bfloat16)


def solution(mesh):
    in_specs = (
        P(("rep", "dp"), None),
        P(("rep", "dp"), None),
        P(("rep", "dp"), None),
        P(("rep", "dp")),
        P(("rep", "dp")),
        P(),
        P(None, "dp"),
        P("dp", None),
    )
    out_specs = P(("rep", "dp"), None)
    return jax.shard_map(
        on_device, mesh=mesh, in_specs=in_specs, out_specs=out_specs, check_vma=False
    )
```

```python
import functools
import math

import jax
import jax.numpy as jnp
from jax import lax
from jax.experimental import pallas as pl
from jax.experimental.pallas import tpu as pltpu
from jax.sharding import PartitionSpec as P

HQ = 48
KVH = 4
HD = 128
GROUP = HQ // KVH
D = HQ * HD
SLOTS = 16
POOL = 1024
HIDDEN = 448
SIDE = 4
PAIR = 2 * SLOTS
CHUNK = 3072


def device(y, x, c):
    return (y * SIDE + x) * 2 + c


def routes():
    other = {"near": (1, 0, 3, 2), "wrap": (3, 2, 1, 0), "far": (2, 3, 0, 1)}
    out = {"core": [], **{axis + name: [] for axis in "st" for name in other}}
    for y in range(SIDE):
        for x in range(SIDE):
            for c in range(2):
                me = device(y, x, c)
                for name, to in other.items():
                    along_x, along_y = device(y, to[x], c), device(to[y], x, c)
                    out["s" + name].append((me, along_x if c == 0 else along_y))
                    out["t" + name].append((me, along_y if c == 0 else along_x))
                out["core"].append((me, device(y, x, 1 - c)))
    return out


ROUTES = routes()


def send(value, route, what):
    with jax.named_scope(what + "_" + route):
        return lax.ppermute(value, "dp", ROUTES[route])


def in_hbm(x):
    return pltpu.with_memory_space_constraint(x, pltpu.HBM)


def attend_kernel(
    lengths_in, q_in, k_in, v_in, gain_in, down, attended, normed, down_held, lengths, q, k, v, gain, sems
):
    copies = [
        pltpu.make_async_copy(a, b, sems.at[i])
        for i, (a, b) in enumerate(
            (
                (lengths_in, lengths),
                (k_in, k),
                (q_in, q),
                (v_in, v),
                (gain_in, gain),
                (down, down_held),
            )
        )
    ]
    for copy in copies:
        copy.start()
    copies[0].wait()
    row = lax.broadcasted_iota(jnp.int32, (SLOTS, 1), 0)
    starts = jnp.zeros((SLOTS, 1), jnp.int32)
    ends = jnp.zeros((SLOTS, 1), jnp.int32)
    at = jnp.int32(0)
    for i in range(SLOTS):
        after = at + lengths[i]
        starts = jnp.where(row == i, at, starts)
        ends = jnp.where(row == i, after, ends)
        at = after
    position = lax.broadcasted_iota(jnp.int32, (SLOTS, POOL), 1)
    inside = (position >= starts) & (position < ends)
    offset = jnp.where(inside, jnp.float32(0.0), jnp.float32(-1e30))
    squares = jnp.zeros((SLOTS, HD), jnp.float32)
    ones = jnp.ones((POOL, HD), jnp.bfloat16)
    copies[1].wait()
    copies[2].wait()
    for kv in range(KVH):
        heads = range(kv * GROUP, (kv + 1) * GROUP)
        rows = jnp.concatenate([q[:, h * HD : (h + 1) * HD] for h in heads], axis=0)
        scores = lax.dot_general(
            rows,
            k[:, kv * HD : (kv + 1) * HD],
            (((1,), (1,)), ((), ())),
            preferred_element_type=jnp.float32,
        )
        masked = scores.reshape(GROUP, SLOTS, POOL) + offset[None]
        top = jnp.max(masked, axis=-1, keepdims=True)
        raised = jnp.exp2((masked - top) * jnp.float32(HD ** (-0.5) * math.log2(math.e)))
        if kv == 0:
            copies[3].wait()
        mixed = lax.dot_general(
            raised.astype(jnp.bfloat16).reshape(GROUP * SLOTS, POOL),
            jnp.concatenate([v[:, kv * HD : (kv + 1) * HD], ones], axis=1),
            (((1,), (0,)), ((), ())),
            preferred_element_type=jnp.float32,
        )
        mixed = (mixed[:, :HD] / mixed[:, HD:]).reshape(GROUP, SLOTS, HD)
        for g, h in enumerate(heads):
            part = mixed[g].astype(jnp.bfloat16)
            attended[:, h * HD : (h + 1) * HD] = part
            wide = part.astype(jnp.float32)
            squares = squares + wide * wide
    mean_square = jnp.sum(squares, axis=-1, keepdims=True) / D
    factor = lax.rsqrt(mean_square + 1e-05)
    copies[4].wait()
    normed[...] = (attended[...].astype(jnp.float32) * factor * gain[...]).astype(jnp.bfloat16)
    copies[5].wait()


def attend(queries, cache_keys, cache_values, lengths, norm_gain, down_rows):
    vmem = pl.BlockSpec(memory_space=pltpu.VMEM)
    any_space = pl.BlockSpec(memory_space=pl.ANY)
    return pl.pallas_call(
        attend_kernel,
        out_shape=(
            jax.ShapeDtypeStruct((SLOTS, D), jnp.bfloat16),
            jax.ShapeDtypeStruct((SLOTS, D), jnp.bfloat16),
            jax.ShapeDtypeStruct((HIDDEN, D), jnp.bfloat16),
        ),
        in_specs=[any_space] * 6,
        out_specs=(vmem, vmem, vmem),
        scratch_shapes=[
            pltpu.SMEM((SLOTS,), jnp.int32),
            pltpu.VMEM((SLOTS, D), jnp.bfloat16),
            pltpu.VMEM((POOL, KVH * HD), jnp.bfloat16),
            pltpu.VMEM((POOL, KVH * HD), jnp.bfloat16),
            pltpu.VMEM((1, D), jnp.float32),
            pltpu.SemaphoreType.DMA((6,)),
        ],
        compiler_params=pltpu.CompilerParams(vmem_limit_bytes=16 * 2**20),
        name="attend",
    )(*map(in_hbm, (lengths, queries, cache_keys, cache_values, norm_gain.reshape(1, D), down_rows)))


def fetch_kernel(weights, after, held, sem):
    copy = pltpu.make_async_copy(weights, held, sem)
    copy.start()
    copy.wait()


def fetch(weights, after):
    any_space = pl.BlockSpec(memory_space=pl.ANY)
    return pl.pallas_call(
        fetch_kernel,
        out_shape=jax.ShapeDtypeStruct((HIDDEN, D), jnp.bfloat16),
        in_specs=[any_space] * 2,
        out_specs=pl.BlockSpec(memory_space=pltpu.VMEM),
        scratch_shapes=[pltpu.SemaphoreType.DMA],
        compiler_params=pltpu.CompilerParams(vmem_limit_bytes=16 * 2**20),
        cost_estimate=pl.CostEstimate(flops=10**11, bytes_accessed=4 * HIDDEN * D, transcendentals=0),
        name="fetch",
    )(in_hbm(weights), after)


def up_kernel(*args):
    blocks, up, (hidden, total) = args[:8], args[8:10], args[10:]
    total[...] = jnp.zeros_like(total)

    @pl.loop(0, D // CHUNK)
    def _(step):
        cols = pl.ds(pl.multiple_of(step * CHUNK, CHUNK), CHUNK)
        total[...] += lax.dot_general(
            jnp.concatenate([w[:, cols] for w in up], axis=0),
            jnp.concatenate([b[:, cols] for b in blocks], axis=0),
            (((1,), (1,)), ((), ())),
            preferred_element_type=jnp.float32,
        )

    value = total[...]
    hidden[...] = (value / (1.0 + jnp.exp(-value))).astype(jnp.bfloat16).T


def project_up(blocks, up):
    vmem = pl.BlockSpec(memory_space=pltpu.VMEM)
    rows = len(blocks) * PAIR
    return pl.pallas_call(
        up_kernel,
        out_shape=jax.ShapeDtypeStruct((rows, 2 * HIDDEN), jnp.bfloat16),
        in_specs=[vmem] * 10,
        out_specs=vmem,
        scratch_shapes=[pltpu.VMEM((2 * HIDDEN, rows), jnp.float32)],
        compiler_params=pltpu.CompilerParams(vmem_limit_bytes=16 * 2**20),
        cost_estimate=pl.CostEstimate(flops=4 * rows * HIDDEN * D, bytes_accessed=2 * rows * D, transcendentals=0),
        name="up",
    )(*blocks, *up)


def down_kernel(begin, hidden, one, two, *outs):
    rows = pl.ds(begin * PAIR, len(outs) * PAIR)

    @pl.loop(0, D // CHUNK)
    def _(step):
        cols = pl.ds(pl.multiple_of(step * CHUNK, CHUNK), CHUNK)
        product = jnp.dot(
            hidden[rows, :],
            jnp.concatenate([one[:, cols], two[:, cols]], axis=0),
            preferred_element_type=jnp.float32,
        ).astype(jnp.bfloat16)
        for i, out in enumerate(outs):
            out[:, cols] = product[i * PAIR : (i + 1) * PAIR]


def project_down(hidden, down, begin, end):
    vmem = pl.BlockSpec(memory_space=pltpu.VMEM)
    n = end - begin
    return pl.pallas_call(
        functools.partial(down_kernel, begin),
        out_shape=[jax.ShapeDtypeStruct((PAIR, D), jnp.bfloat16)] * n,
        in_specs=[vmem] * 3,
        out_specs=[vmem] * n,
        compiler_params=pltpu.CompilerParams(vmem_limit_bytes=16 * 2**20),
        cost_estimate=pl.CostEstimate(
            flops=4 * n * PAIR * HIDDEN * D, bytes_accessed=2 * n * PAIR * D, transcendentals=0
        ),
        name="down",
    )(hidden, *down)


def pack_kernel(one, two, block):
    block[:SLOTS] = one[...]
    block[SLOTS:] = two[...]


def pack(one, two):
    vmem = pl.BlockSpec(memory_space=pltpu.VMEM)
    return pl.pallas_call(
        pack_kernel,
        out_shape=jax.ShapeDtypeStruct((PAIR, D), jnp.bfloat16),
        in_specs=[vmem] * 2,
        out_specs=vmem,
        compiler_params=pltpu.CompilerParams(vmem_limit_bytes=16 * 2**20),
        name="pack",
    )(one, two)


def hand_kernel(*refs):
    pass


def hand(held, *after):
    vmem = pl.BlockSpec(memory_space=pltpu.VMEM)
    return pl.pallas_call(
        hand_kernel,
        out_shape=jax.ShapeDtypeStruct(held.shape, held.dtype),
        in_specs=[vmem] + [pl.BlockSpec(memory_space=pl.ANY)] * len(after),
        out_specs=vmem,
        input_output_aliases={0: 0},
        compiler_params=pltpu.CompilerParams(vmem_limit_bytes=16 * 2**20),
        name="hand",
    )(held, *after)


def merge_kernel(n, mine, arrived, *refs):
    waiting, (total, *later) = refs[:n], refs[-n - 1 :]
    total[...] = (mine[...].astype(jnp.float32) + arrived[...].astype(jnp.float32)).astype(jnp.bfloat16)
    for source, target in zip(waiting, later):
        target[...] = source[...]


def merge(mine, arrived, *waiting, after=()):
    vmem = pl.BlockSpec(memory_space=pltpu.VMEM)
    n = len(waiting)
    return pl.pallas_call(
        functools.partial(merge_kernel, n),
        out_shape=[jax.ShapeDtypeStruct((PAIR, D), jnp.bfloat16)] * (1 + n),
        in_specs=[vmem] * (2 + n) + [pl.BlockSpec(memory_space=pl.ANY)] * len(after),
        out_specs=[vmem] * (1 + n),
        compiler_params=pltpu.CompilerParams(vmem_limit_bytes=16 * 2**20),
        name="merge",
    )(mine, arrived, *waiting, *after)


def finish_kernel(own, direct, back, *refs):
    one, two = refs[-2:]
    value = sum(x[...].astype(jnp.float32) for x in (own, direct, back))
    one[...] = value[:SLOTS].astype(one.dtype)
    two[...] = value[SLOTS:].astype(two.dtype)


def finish(own, direct, back, kept_type, after=()):
    vmem = pl.BlockSpec(memory_space=pltpu.VMEM)
    return pl.pallas_call(
        finish_kernel,
        out_shape=[jax.ShapeDtypeStruct((SLOTS, D), kept_type), jax.ShapeDtypeStruct((SLOTS, D), jnp.bfloat16)],
        in_specs=[vmem] * 3 + [pl.BlockSpec(memory_space=pl.ANY)] * len(after),
        out_specs=[vmem] * 2,
        compiler_params=pltpu.CompilerParams(vmem_limit_bytes=16 * 2**20),
        name="finish",
    )(own, direct, back, *after)


def collect_kernel(*refs):
    *parts, out = refs
    out[...] = sum(x[...].astype(jnp.float32) for x in parts)


def collect(*parts):
    vmem = pl.BlockSpec(memory_space=pltpu.VMEM)
    return pl.pallas_call(
        collect_kernel,
        out_shape=jax.ShapeDtypeStruct((SLOTS, D), jnp.float32),
        in_specs=[vmem] * len(parts),
        out_specs=vmem,
        compiler_params=pltpu.CompilerParams(vmem_limit_bytes=16 * 2**20),
        name="collect",
    )(*parts)


def on_device(
    queries, cache_keys, cache_values, lengths, counts, norm_gain, up_weight, down_weight
):
    up_own = up_weight.T
    up_other = send(up_own, "core", "up")
    attended, normed, down_held = attend(
        queries, cache_keys, cache_values, lengths, norm_gain, down_weight
    )
    by_wrap, by_far, by_near = [send(normed, r, "gather") for r in ("swrap", "sfar", "snear")]
    early = pack(normed, by_near)
    late = pack(by_wrap, by_far)
    early_n, late_w = send(early, "tnear", "gather"), send(late, "twrap", "gather")
    late_n, early_w = send(late, "tnear", "gather"), send(early, "twrap", "gather")
    early_n = hand(early_n, early_w)
    early_f, late_f = send(early_n, "twrap", "gather2"), send(late_w, "tnear", "gather2")
    down_held = hand(down_held, up_other)
    down_other = send(down_held, "core", "down")
    up_held = fetch(up_own, late)
    hidden = project_up(
        [early, late, early_n, late_w, early_w, late_n, early_f, late_f], (up_held, up_other)
    )
    down = (down_held, down_other)
    early_f, late_f = project_down(hidden, down, 6, 8)
    early, late, early_n, late_w, early_w, late_n = project_down(hidden, down, 0, 6)
    far_late = send(late_f, "twrap", "reduce2")
    far_early = send(early_f, "tnear", "reduce2")
    direct_late = send(late_w, "twrap", "reduce")
    direct_early = send(early_n, "tnear", "reduce")
    (early_w,) = merge(early_w, far_early)
    back_early = send(early_w, "twrap", "reduce")
    (late_n,) = merge(late_n, far_late, after=(early_w,))
    back_late = send(late_n, "tnear", "reduce")
    own, home_near = finish(early, direct_early, back_early, jnp.float32, after=(direct_late,))
    home_wrap, home_far = finish(late, direct_late, back_late, jnp.bfloat16, after=(own,))
    home_wrap, home_far = send(home_wrap, "swrap", "home"), send(home_far, "sfar", "home")
    home_near = send(home_near, "snear", "home")
    mixed = collect(attended, own, home_wrap, home_far)
    live = jnp.arange(SLOTS, dtype=jnp.int32)[:, None] < counts[0]
    return jnp.where(live, mixed + home_near.astype(jnp.float32), jnp.float32(0.0)).astype(jnp.bfloat16)


def solution(mesh):
    in_specs = (
        P(("rep", "dp"), None),
        P(("rep", "dp"), None),
        P(("rep", "dp"), None),
        P(("rep", "dp")),
        P(("rep", "dp")),
        P(),
        P(None, "dp"),
        P("dp", None),
    )
    out_specs = P(("rep", "dp"), None)
    return jax.shard_map(
        on_device, mesh=mesh, in_specs=in_specs, out_specs=out_specs, check_vma=False
    )
```

```python
import functools
import math

import jax
import jax.numpy as jnp
from jax import lax
from jax.experimental import pallas as pl
from jax.experimental.pallas import tpu as pltpu
from jax.sharding import PartitionSpec as P

HQ = 48
KVH = 4
HD = 128
GROUP = HQ // KVH
D = HQ * HD
SLOTS = 16
POOL = 1024
HIDDEN = 448
SIDE = 4
PAIR = 2 * SLOTS
CHUNK = 3072


def device(y, x, c):
    return (y * SIDE + x) * 2 + c


def routes():
    other = {"near": (1, 0, 3, 2), "wrap": (3, 2, 1, 0), "far": (2, 3, 0, 1)}
    out = {"core": [], **{axis + name: [] for axis in "st" for name in other}}
    for y in range(SIDE):
        for x in range(SIDE):
            for c in range(2):
                me = device(y, x, c)
                for name, to in other.items():
                    along_x, along_y = device(y, to[x], c), device(to[y], x, c)
                    out["s" + name].append((me, along_x if c == 0 else along_y))
                    out["t" + name].append((me, along_y if c == 0 else along_x))
                out["core"].append((me, device(y, x, 1 - c)))
    return out


ROUTES = routes()


def send(value, route, what):
    with jax.named_scope(what + "_" + route):
        return lax.ppermute(value, "dp", ROUTES[route])


def in_hbm(x):
    return pltpu.with_memory_space_constraint(x, pltpu.HBM)


def attend_kernel(
    lengths_in, q_in, k_in, v_in, gain_in, down, attended, normed, down_held, lengths, q, k, v, gain, sems
):
    copies = [
        pltpu.make_async_copy(a, b, sems.at[i])
        for i, (a, b) in enumerate(
            (
                (lengths_in, lengths),
                (k_in, k),
                (q_in, q),
                (v_in, v),
                (gain_in, gain),
                (down, down_held),
            )
        )
    ]
    for copy in copies:
        copy.start()
    copies[0].wait()
    row = lax.broadcasted_iota(jnp.int32, (SLOTS, 1), 0)
    starts = jnp.zeros((SLOTS, 1), jnp.int32)
    ends = jnp.zeros((SLOTS, 1), jnp.int32)
    at = jnp.int32(0)
    for i in range(SLOTS):
        after = at + lengths[i]
        starts = jnp.where(row == i, at, starts)
        ends = jnp.where(row == i, after, ends)
        at = after
    position = lax.broadcasted_iota(jnp.int32, (SLOTS, POOL), 1)
    inside = (position >= starts) & (position < ends)
    offset = jnp.where(inside, jnp.float32(0.0), jnp.float32(-1e30))
    squares = jnp.zeros((SLOTS, HD), jnp.float32)
    ones = jnp.ones((POOL, HD), jnp.bfloat16)
    copies[1].wait()
    copies[2].wait()
    for kv in range(KVH):
        heads = range(kv * GROUP, (kv + 1) * GROUP)
        rows = jnp.concatenate([q[:, h * HD : (h + 1) * HD] for h in heads], axis=0)
        scores = lax.dot_general(
            rows,
            k[:, kv * HD : (kv + 1) * HD],
            (((1,), (1,)), ((), ())),
            preferred_element_type=jnp.float32,
        )
        masked = scores.reshape(GROUP, SLOTS, POOL) + offset[None]
        top = jnp.max(masked, axis=-1, keepdims=True)
        raised = jnp.exp2((masked - top) * jnp.float32(HD ** (-0.5) * math.log2(math.e)))
        if kv == 0:
            copies[3].wait()
        mixed = lax.dot_general(
            raised.astype(jnp.bfloat16).reshape(GROUP * SLOTS, POOL),
            jnp.concatenate([v[:, kv * HD : (kv + 1) * HD], ones], axis=1),
            (((1,), (0,)), ((), ())),
            preferred_element_type=jnp.float32,
        )
        mixed = (mixed[:, :HD] / mixed[:, HD:]).reshape(GROUP, SLOTS, HD)
        for g, h in enumerate(heads):
            part = mixed[g].astype(jnp.bfloat16)
            attended[:, h * HD : (h + 1) * HD] = part
            wide = part.astype(jnp.float32)
            squares = squares + wide * wide
    mean_square = jnp.sum(squares, axis=-1, keepdims=True) / D
    factor = lax.rsqrt(mean_square + 1e-05)
    copies[4].wait()
    normed[...] = (attended[...].astype(jnp.float32) * factor * gain[...]).astype(jnp.bfloat16)
    copies[5].wait()


def attend(queries, cache_keys, cache_values, lengths, norm_gain, down_rows):
    vmem = pl.BlockSpec(memory_space=pltpu.VMEM)
    any_space = pl.BlockSpec(memory_space=pl.ANY)
    return pl.pallas_call(
        attend_kernel,
        out_shape=(
            jax.ShapeDtypeStruct((SLOTS, D), jnp.bfloat16),
            jax.ShapeDtypeStruct((SLOTS, D), jnp.bfloat16),
            jax.ShapeDtypeStruct((HIDDEN, D), jnp.bfloat16),
        ),
        in_specs=[any_space] * 6,
        out_specs=(vmem, vmem, vmem),
        scratch_shapes=[
            pltpu.SMEM((SLOTS,), jnp.int32),
            pltpu.VMEM((SLOTS, D), jnp.bfloat16),
            pltpu.VMEM((POOL, KVH * HD), jnp.bfloat16),
            pltpu.VMEM((POOL, KVH * HD), jnp.bfloat16),
            pltpu.VMEM((1, D), jnp.float32),
            pltpu.SemaphoreType.DMA((6,)),
        ],
        compiler_params=pltpu.CompilerParams(vmem_limit_bytes=16 * 2**20),
        name="attend",
    )(*map(in_hbm, (lengths, queries, cache_keys, cache_values, norm_gain.reshape(1, D), down_rows)))


def fetch_kernel(weights, after, held, sem):
    copy = pltpu.make_async_copy(weights, held, sem)
    copy.start()
    copy.wait()


def fetch(weights, after):
    any_space = pl.BlockSpec(memory_space=pl.ANY)
    return pl.pallas_call(
        fetch_kernel,
        out_shape=jax.ShapeDtypeStruct((HIDDEN, D), jnp.bfloat16),
        in_specs=[any_space] * 2,
        out_specs=pl.BlockSpec(memory_space=pltpu.VMEM),
        scratch_shapes=[pltpu.SemaphoreType.DMA],
        compiler_params=pltpu.CompilerParams(vmem_limit_bytes=16 * 2**20),
        cost_estimate=pl.CostEstimate(flops=10**11, bytes_accessed=4 * HIDDEN * D, transcendentals=0),
        name="fetch",
    )(in_hbm(weights), after)


def up_kernel(*args):
    blocks, up, (hidden, total) = args[:8], args[8:10], args[10:]
    lows, highs = slice(0, SLOTS), slice(SLOTS, PAIR)
    order = [(part, half) for part in (0, 1) for half in (lows, highs)]
    total[...] = jnp.zeros_like(total)

    @pl.loop(0, D // CHUNK)
    def _(step):
        cols = pl.ds(pl.multiple_of(step * CHUNK, CHUNK), CHUNK)
        total[...] += lax.dot_general(
            jnp.concatenate([w[:, cols] for w in up], axis=0),
            jnp.concatenate([blocks[2 * t + part][half, cols] for part, half in order for t in range(SIDE)], axis=0),
            (((1,), (1,)), ((), ())),
            preferred_element_type=jnp.float32,
        )

    value = total[...]
    hidden[...] = (value / (1.0 + jnp.exp(-value))).astype(jnp.bfloat16).T


def project_up(blocks, up):
    vmem = pl.BlockSpec(memory_space=pltpu.VMEM)
    rows = len(blocks) * PAIR
    return pl.pallas_call(
        up_kernel,
        out_shape=jax.ShapeDtypeStruct((rows, 2 * HIDDEN), jnp.bfloat16),
        in_specs=[vmem] * 10,
        out_specs=vmem,
        scratch_shapes=[pltpu.VMEM((2 * HIDDEN, rows), jnp.float32)],
        compiler_params=pltpu.CompilerParams(vmem_limit_bytes=16 * 2**20),
        cost_estimate=pl.CostEstimate(flops=4 * rows * HIDDEN * D, bytes_accessed=2 * rows * D, transcendentals=0),
        name="up",
    )(*blocks, *up)


def down_kernel(begin, hidden, one, two, *outs):
    rows = pl.ds(begin * PAIR, len(outs) * PAIR)

    @pl.loop(0, D // CHUNK)
    def _(step):
        cols = pl.ds(pl.multiple_of(step * CHUNK, CHUNK), CHUNK)
        product = jnp.dot(
            hidden[rows, :],
            jnp.concatenate([one[:, cols], two[:, cols]], axis=0),
            preferred_element_type=jnp.float32,
        ).astype(jnp.bfloat16)
        for i, out in enumerate(outs):
            out[:, cols] = product[i * PAIR : (i + 1) * PAIR]


def project_down(hidden, down, begin, end):
    vmem = pl.BlockSpec(memory_space=pltpu.VMEM)
    n = end - begin
    return pl.pallas_call(
        functools.partial(down_kernel, begin),
        out_shape=[jax.ShapeDtypeStruct((PAIR, D), jnp.bfloat16)] * n,
        in_specs=[vmem] * 3,
        out_specs=[vmem] * n,
        compiler_params=pltpu.CompilerParams(vmem_limit_bytes=16 * 2**20),
        cost_estimate=pl.CostEstimate(
            flops=4 * n * PAIR * HIDDEN * D, bytes_accessed=2 * n * PAIR * D, transcendentals=0
        ),
        name="down",
    )(hidden, *down)


def pack_kernel(one, two, block):
    block[:SLOTS] = one[...]
    block[SLOTS:] = two[...]


def pack(one, two):
    vmem = pl.BlockSpec(memory_space=pltpu.VMEM)
    return pl.pallas_call(
        pack_kernel,
        out_shape=jax.ShapeDtypeStruct((PAIR, D), jnp.bfloat16),
        in_specs=[vmem] * 2,
        out_specs=vmem,
        compiler_params=pltpu.CompilerParams(vmem_limit_bytes=16 * 2**20),
        name="pack",
    )(one, two)


def hand_kernel(*refs):
    pass


def hand(held, *after):
    vmem = pl.BlockSpec(memory_space=pltpu.VMEM)
    return pl.pallas_call(
        hand_kernel,
        out_shape=jax.ShapeDtypeStruct(held.shape, held.dtype),
        in_specs=[vmem] + [pl.BlockSpec(memory_space=pl.ANY)] * len(after),
        out_specs=vmem,
        input_output_aliases={0: 0},
        compiler_params=pltpu.CompilerParams(vmem_limit_bytes=16 * 2**20),
        name="hand",
    )(held, *after)


def merge_kernel(n, mine, arrived, *refs):
    waiting, (total, *later) = refs[:n], refs[-n - 1 :]
    total[...] = (mine[...].astype(jnp.float32) + arrived[...].astype(jnp.float32)).astype(jnp.bfloat16)
    for source, target in zip(waiting, later):
        target[...] = source[...]


def merge(mine, arrived, *waiting, after=()):
    vmem = pl.BlockSpec(memory_space=pltpu.VMEM)
    n = len(waiting)
    return pl.pallas_call(
        functools.partial(merge_kernel, n),
        out_shape=[jax.ShapeDtypeStruct((PAIR, D), jnp.bfloat16)] * (1 + n),
        in_specs=[vmem] * (2 + n) + [pl.BlockSpec(memory_space=pl.ANY)] * len(after),
        out_specs=[vmem] * (1 + n),
        compiler_params=pltpu.CompilerParams(vmem_limit_bytes=16 * 2**20),
        name="merge",
    )(mine, arrived, *waiting, *after)


def finish_kernel(own, direct, back, *refs):
    one, two = refs[-2:]
    value = sum(x[...].astype(jnp.float32) for x in (own, direct, back))
    one[...] = value[:SLOTS].astype(one.dtype)
    two[...] = value[SLOTS:].astype(two.dtype)


def finish(own, direct, back, kept_type, after=()):
    vmem = pl.BlockSpec(memory_space=pltpu.VMEM)
    return pl.pallas_call(
        finish_kernel,
        out_shape=[jax.ShapeDtypeStruct((SLOTS, D), kept_type), jax.ShapeDtypeStruct((SLOTS, D), jnp.bfloat16)],
        in_specs=[vmem] * 3 + [pl.BlockSpec(memory_space=pl.ANY)] * len(after),
        out_specs=[vmem] * 2,
        compiler_params=pltpu.CompilerParams(vmem_limit_bytes=16 * 2**20),
        name="finish",
    )(own, direct, back, *after)


def collect_kernel(*refs):
    *parts, out = refs
    out[...] = sum(x[...].astype(jnp.float32) for x in parts)


def collect(*parts):
    vmem = pl.BlockSpec(memory_space=pltpu.VMEM)
    return pl.pallas_call(
        collect_kernel,
        out_shape=jax.ShapeDtypeStruct((SLOTS, D), jnp.float32),
        in_specs=[vmem] * len(parts),
        out_specs=vmem,
        compiler_params=pltpu.CompilerParams(vmem_limit_bytes=16 * 2**20),
        name="collect",
    )(*parts)


def on_device(
    queries, cache_keys, cache_values, lengths, counts, norm_gain, up_weight, down_weight
):
    up_own = up_weight.T
    up_other = send(up_own, "core", "up")
    attended, normed, down_held = attend(
        queries, cache_keys, cache_values, lengths, norm_gain, down_weight
    )
    by_wrap, by_far, by_near = [send(normed, r, "gather") for r in ("swrap", "sfar", "snear")]
    early = pack(normed, by_near)
    late = pack(by_wrap, by_far)
    early_n, late_w = send(early, "tnear", "gather"), send(late, "twrap", "gather")
    late_n, early_w = send(late, "tnear", "gather"), send(early, "twrap", "gather")
    early_n = hand(early_n, early_w)
    early_f, late_f = send(early_n, "twrap", "gather2"), send(late_w, "tnear", "gather2")
    down_held = hand(down_held, up_other)
    down_other = send(down_held, "core", "down")
    up_held = fetch(up_own, late)
    hidden = project_up(
        [early, late, early_n, late_n, early_w, late_w, early_f, late_f], (up_held, up_other)
    )
    down = (down_held, down_other)
    early_f, late_f = project_down(hidden, down, 6, 8)
    early, late, early_n, late_n, early_w, late_w = project_down(hidden, down, 0, 6)
    far_late = send(late_f, "swrap", "reduce2")
    far_early = send(early_f, "snear", "reduce2")
    direct_late = send(late_w, "swrap", "reduce")
    (late_n,) = merge(late_n, far_late)
    back_late = send(late_n, "snear", "reduce")
    direct_early = send(early_n, "snear", "reduce")
    (early_w,) = merge(early_w, far_early, after=(late_n,))
    back_early = send(early_w, "swrap", "reduce")
    home_wrap, home_far = finish(late, direct_late, back_late, jnp.bfloat16, after=(direct_early,))
    own, home_near = finish(early, direct_early, back_early, jnp.float32, after=(home_wrap,))
    home_wrap, home_far = send(home_wrap, "twrap", "home"), send(home_far, "tfar", "home")
    home_near = send(home_near, "tnear", "home")
    mixed = collect(attended, own, home_wrap, home_far)
    live = jnp.arange(SLOTS, dtype=jnp.int32)[:, None] < counts[0]
    return jnp.where(live, mixed + home_near.astype(jnp.float32), jnp.float32(0.0)).astype(jnp.bfloat16)


def solution(mesh):
    in_specs = (
        P(("rep", "dp"), None),
        P(("rep", "dp"), None),
        P(("rep", "dp"), None),
        P(("rep", "dp")),
        P(("rep", "dp")),
        P(),
        P(None, "dp"),
        P("dp", None),
    )
    out_specs = P(("rep", "dp"), None)
    return jax.shard_map(
        on_device, mesh=mesh, in_specs=in_specs, out_specs=out_specs, check_vma=False
    )
```

```python
import functools
import math

import jax
import jax.numpy as jnp
from jax import lax
from jax.experimental import pallas as pl
from jax.experimental.pallas import tpu as pltpu
from jax.sharding import PartitionSpec as P

HQ = 48
KVH = 4
HD = 128
GROUP = HQ // KVH
D = HQ * HD
SLOTS = 16
POOL = 1024
HIDDEN = 448
SIDE = 4
PAIR = 2 * SLOTS
CHUNK = 3072


def device(y, x, c):
    return (y * SIDE + x) * 2 + c


def routes():
    other = {"near": (1, 0, 3, 2), "wrap": (3, 2, 1, 0), "far": (2, 3, 0, 1)}
    out = {"core": [], **{axis + name: [] for axis in "st" for name in other}}
    for y in range(SIDE):
        for x in range(SIDE):
            for c in range(2):
                me = device(y, x, c)
                for name, to in other.items():
                    along_x, along_y = device(y, to[x], c), device(to[y], x, c)
                    out["s" + name].append((me, along_x if c == 0 else along_y))
                    out["t" + name].append((me, along_y if c == 0 else along_x))
                out["core"].append((me, device(y, x, 1 - c)))
    return out


ROUTES = routes()


def send(value, route, what):
    with jax.named_scope(what + "_" + route):
        return lax.ppermute(value, "dp", ROUTES[route])


def in_hbm(x):
    return pltpu.with_memory_space_constraint(x, pltpu.HBM)


def attend_kernel(
    lengths_in, q_in, k_in, v_in, gain_in, down, attended, normed, down_held, lengths, q, k, v, gain, sems
):
    copies = [
        pltpu.make_async_copy(a, b, sems.at[i])
        for i, (a, b) in enumerate(
            (
                (lengths_in, lengths),
                (k_in, k),
                (q_in, q),
                (v_in, v),
                (gain_in, gain),
                (down, down_held),
            )
        )
    ]
    for copy in copies:
        copy.start()
    copies[0].wait()
    row = lax.broadcasted_iota(jnp.int32, (SLOTS, 1), 0)
    starts = jnp.zeros((SLOTS, 1), jnp.int32)
    ends = jnp.zeros((SLOTS, 1), jnp.int32)
    at = jnp.int32(0)
    for i in range(SLOTS):
        after = at + lengths[i]
        starts = jnp.where(row == i, at, starts)
        ends = jnp.where(row == i, after, ends)
        at = after
    position = lax.broadcasted_iota(jnp.int32, (SLOTS, POOL), 1)
    inside = (position >= starts) & (position < ends)
    offset = jnp.where(inside, jnp.float32(0.0), jnp.float32(-1e30))
    squares = jnp.zeros((SLOTS, HD), jnp.float32)
    ones = jnp.ones((POOL, HD), jnp.bfloat16)
    copies[1].wait()
    copies[2].wait()
    for kv in range(KVH):
        heads = range(kv * GROUP, (kv + 1) * GROUP)
        rows = jnp.concatenate([q[:, h * HD : (h + 1) * HD] for h in heads], axis=0)
        scores = lax.dot_general(
            rows,
            k[:, kv * HD : (kv + 1) * HD],
            (((1,), (1,)), ((), ())),
            preferred_element_type=jnp.float32,
        )
        masked = scores.reshape(GROUP, SLOTS, POOL) + offset[None]
        top = jnp.max(masked, axis=-1, keepdims=True)
        raised = jnp.exp2((masked - top) * jnp.float32(HD ** (-0.5) * math.log2(math.e)))
        if kv == 0:
            copies[3].wait()
        mixed = lax.dot_general(
            raised.astype(jnp.bfloat16).reshape(GROUP * SLOTS, POOL),
            jnp.concatenate([v[:, kv * HD : (kv + 1) * HD], ones], axis=1),
            (((1,), (0,)), ((), ())),
            preferred_element_type=jnp.float32,
        )
        mixed = (mixed[:, :HD] / mixed[:, HD:]).reshape(GROUP, SLOTS, HD)
        for g, h in enumerate(heads):
            part = mixed[g].astype(jnp.bfloat16)
            attended[:, h * HD : (h + 1) * HD] = part
            wide = part.astype(jnp.float32)
            squares = squares + wide * wide
    mean_square = jnp.sum(squares, axis=-1, keepdims=True) / D
    factor = lax.rsqrt(mean_square + 1e-05)
    copies[4].wait()
    normed[...] = (attended[...].astype(jnp.float32) * factor * gain[...]).astype(jnp.bfloat16)
    copies[5].wait()


def attend(queries, cache_keys, cache_values, lengths, norm_gain, down_rows):
    vmem = pl.BlockSpec(memory_space=pltpu.VMEM)
    any_space = pl.BlockSpec(memory_space=pl.ANY)
    return pl.pallas_call(
        attend_kernel,
        out_shape=(
            jax.ShapeDtypeStruct((SLOTS, D), jnp.bfloat16),
            jax.ShapeDtypeStruct((SLOTS, D), jnp.bfloat16),
            jax.ShapeDtypeStruct((HIDDEN, D), jnp.bfloat16),
        ),
        in_specs=[any_space] * 6,
        out_specs=(vmem, vmem, vmem),
        scratch_shapes=[
            pltpu.SMEM((SLOTS,), jnp.int32),
            pltpu.VMEM((SLOTS, D), jnp.bfloat16),
            pltpu.VMEM((POOL, KVH * HD), jnp.bfloat16),
            pltpu.VMEM((POOL, KVH * HD), jnp.bfloat16),
            pltpu.VMEM((1, D), jnp.float32),
            pltpu.SemaphoreType.DMA((6,)),
        ],
        compiler_params=pltpu.CompilerParams(vmem_limit_bytes=16 * 2**20),
        name="attend",
    )(*map(in_hbm, (lengths, queries, cache_keys, cache_values, norm_gain.reshape(1, D), down_rows)))


def fetch_kernel(weights, after, held, sem):
    copy = pltpu.make_async_copy(weights, held, sem)
    copy.start()
    copy.wait()


def fetch(weights, after):
    any_space = pl.BlockSpec(memory_space=pl.ANY)
    return pl.pallas_call(
        fetch_kernel,
        out_shape=jax.ShapeDtypeStruct((HIDDEN, D), jnp.bfloat16),
        in_specs=[any_space] * 2,
        out_specs=pl.BlockSpec(memory_space=pltpu.VMEM),
        scratch_shapes=[pltpu.SemaphoreType.DMA],
        compiler_params=pltpu.CompilerParams(vmem_limit_bytes=16 * 2**20),
        cost_estimate=pl.CostEstimate(flops=10**11, bytes_accessed=4 * HIDDEN * D, transcendentals=0),
        name="fetch",
    )(in_hbm(weights), after)


def up_kernel(*args):
    blocks, up, (hidden, total) = args[:8], args[8:10], args[10:]
    lows, highs = slice(0, SLOTS), slice(SLOTS, PAIR)
    order = [(part, half) for part in (0, 1) for half in (lows, highs)]
    total[...] = jnp.zeros_like(total)

    @pl.loop(0, D // CHUNK)
    def _(step):
        cols = pl.ds(pl.multiple_of(step * CHUNK, CHUNK), CHUNK)
        total[...] += lax.dot_general(
            jnp.concatenate([w[:, cols] for w in up], axis=0),
            jnp.concatenate([blocks[2 * t + part][half, cols] for part, half in order for t in range(SIDE)], axis=0),
            (((1,), (1,)), ((), ())),
            preferred_element_type=jnp.float32,
        )

    value = total[...]
    hidden[...] = (value / (1.0 + jnp.exp(-value))).astype(jnp.bfloat16).T


def project_up(blocks, up):
    vmem = pl.BlockSpec(memory_space=pltpu.VMEM)
    rows = len(blocks) * PAIR
    return pl.pallas_call(
        up_kernel,
        out_shape=jax.ShapeDtypeStruct((rows, 2 * HIDDEN), jnp.bfloat16),
        in_specs=[vmem] * 10,
        out_specs=vmem,
        scratch_shapes=[pltpu.VMEM((2 * HIDDEN, rows), jnp.float32)],
        compiler_params=pltpu.CompilerParams(vmem_limit_bytes=16 * 2**20),
        cost_estimate=pl.CostEstimate(flops=4 * rows * HIDDEN * D, bytes_accessed=2 * rows * D, transcendentals=0),
        name="up",
    )(*blocks, *up)


def down_kernel(begin, hidden, one, two, *outs):
    rows = pl.ds(begin * PAIR, len(outs) * PAIR)

    @pl.loop(0, D // CHUNK)
    def _(step):
        cols = pl.ds(pl.multiple_of(step * CHUNK, CHUNK), CHUNK)
        product = jnp.dot(
            hidden[rows, :],
            jnp.concatenate([one[:, cols], two[:, cols]], axis=0),
            preferred_element_type=jnp.float32,
        ).astype(jnp.bfloat16)
        for i, out in enumerate(outs):
            out[:, cols] = product[i * PAIR : (i + 1) * PAIR]


def project_down(hidden, down, begin, end):
    vmem = pl.BlockSpec(memory_space=pltpu.VMEM)
    n = end - begin
    return pl.pallas_call(
        functools.partial(down_kernel, begin),
        out_shape=[jax.ShapeDtypeStruct((PAIR, D), jnp.bfloat16)] * n,
        in_specs=[vmem] * 3,
        out_specs=[vmem] * n,
        compiler_params=pltpu.CompilerParams(vmem_limit_bytes=16 * 2**20),
        cost_estimate=pl.CostEstimate(
            flops=4 * n * PAIR * HIDDEN * D, bytes_accessed=2 * n * PAIR * D, transcendentals=0
        ),
        name="down",
    )(hidden, *down)


def pack_kernel(one, two, block):
    block[:SLOTS] = one[...]
    block[SLOTS:] = two[...]


def pack(one, two):
    vmem = pl.BlockSpec(memory_space=pltpu.VMEM)
    return pl.pallas_call(
        pack_kernel,
        out_shape=jax.ShapeDtypeStruct((PAIR, D), jnp.bfloat16),
        in_specs=[vmem] * 2,
        out_specs=vmem,
        compiler_params=pltpu.CompilerParams(vmem_limit_bytes=16 * 2**20),
        name="pack",
    )(one, two)


def hand_kernel(*refs):
    pass


def hand(held, *after):
    vmem = pl.BlockSpec(memory_space=pltpu.VMEM)
    return pl.pallas_call(
        hand_kernel,
        out_shape=jax.ShapeDtypeStruct(held.shape, held.dtype),
        in_specs=[vmem] + [pl.BlockSpec(memory_space=pl.ANY)] * len(after),
        out_specs=vmem,
        input_output_aliases={0: 0},
        compiler_params=pltpu.CompilerParams(vmem_limit_bytes=16 * 2**20),
        name="hand",
    )(held, *after)


def merge_kernel(n, mine, arrived, *refs):
    waiting, (total, *later) = refs[:n], refs[-n - 1 :]
    total[...] = (mine[...].astype(jnp.float32) + arrived[...].astype(jnp.float32)).astype(jnp.bfloat16)
    for source, target in zip(waiting, later):
        target[...] = source[...]


def merge(mine, arrived, *waiting, after=()):
    vmem = pl.BlockSpec(memory_space=pltpu.VMEM)
    n = len(waiting)
    return pl.pallas_call(
        functools.partial(merge_kernel, n),
        out_shape=[jax.ShapeDtypeStruct((PAIR, D), jnp.bfloat16)] * (1 + n),
        in_specs=[vmem] * (2 + n) + [pl.BlockSpec(memory_space=pl.ANY)] * len(after),
        out_specs=[vmem] * (1 + n),
        compiler_params=pltpu.CompilerParams(vmem_limit_bytes=16 * 2**20),
        name="merge",
    )(mine, arrived, *waiting, *after)


def finish_kernel(own, direct, back, *refs):
    one, two = refs[-2:]
    value = sum(x[...].astype(jnp.float32) for x in (own, direct, back))
    one[...] = value[:SLOTS].astype(one.dtype)
    two[...] = value[SLOTS:].astype(two.dtype)


def finish(own, direct, back, kept_type, after=()):
    vmem = pl.BlockSpec(memory_space=pltpu.VMEM)
    return pl.pallas_call(
        finish_kernel,
        out_shape=[jax.ShapeDtypeStruct((SLOTS, D), kept_type), jax.ShapeDtypeStruct((SLOTS, D), jnp.bfloat16)],
        in_specs=[vmem] * 3 + [pl.BlockSpec(memory_space=pl.ANY)] * len(after),
        out_specs=[vmem] * 2,
        compiler_params=pltpu.CompilerParams(vmem_limit_bytes=16 * 2**20),
        name="finish",
    )(own, direct, back, *after)


def collect_kernel(*refs):
    *parts, out = refs
    out[...] = sum(x[...].astype(jnp.float32) for x in parts)


def collect(*parts):
    vmem = pl.BlockSpec(memory_space=pltpu.VMEM)
    return pl.pallas_call(
        collect_kernel,
        out_shape=jax.ShapeDtypeStruct((SLOTS, D), jnp.float32),
        in_specs=[vmem] * len(parts),
        out_specs=vmem,
        compiler_params=pltpu.CompilerParams(vmem_limit_bytes=16 * 2**20),
        name="collect",
    )(*parts)


def on_device(
    queries, cache_keys, cache_values, lengths, counts, norm_gain, up_weight, down_weight
):
    up_own = up_weight.T
    up_other = send(up_own, "core", "up")
    attended, normed, down_held = attend(
        queries, cache_keys, cache_values, lengths, norm_gain, down_weight
    )
    by_wrap, by_far, by_near = [send(normed, r, "gather") for r in ("swrap", "sfar", "snear")]
    early = pack(normed, by_near)
    late = pack(by_wrap, by_far)
    early_n, late_w = send(early, "tnear", "gather"), send(late, "twrap", "gather")
    late_n, early_w = send(late, "tnear", "gather"), send(early, "twrap", "gather")
    early_n = hand(early_n, early_w)
    early_f, late_f = send(early_n, "twrap", "gather2"), send(late_w, "tnear", "gather2")
    down_held = hand(down_held, up_other)
    down_other = send(down_held, "core", "down")
    up_held = fetch(up_own, late)
    hidden = project_up(
        [early, late, early_n, late_n, early_w, late_w, early_f, late_f], (up_held, up_other)
    )
    down = (down_held, down_other)
    early_f, late_f = project_down(hidden, down, 6, 8)
    early, late, early_n, late_n, early_w, late_w = project_down(hidden, down, 0, 6)
    far_late = send(late_f, "snear", "reduce2")
    far_early = send(early_f, "swrap", "reduce2")
    direct_late = send(late_n, "snear", "reduce")
    direct_early = send(early_w, "swrap", "reduce")
    (late_w,) = merge(late_w, far_late)
    back_late = send(late_w, "swrap", "reduce")
    (early_n,) = merge(early_n, far_early, after=(late_w,))
    back_early = send(early_n, "snear", "reduce")
    home_wrap, home_far = finish(late, direct_late, back_late, jnp.bfloat16, after=(direct_early,))
    own, home_near = finish(early, direct_early, back_early, jnp.float32, after=(home_wrap,))
    home_wrap, home_far = send(home_wrap, "twrap", "home"), send(home_far, "tfar", "home")
    home_near = send(home_near, "tnear", "home")
    mixed = collect(attended, own, home_wrap, home_far)
    live = jnp.arange(SLOTS, dtype=jnp.int32)[:, None] < counts[0]
    return jnp.where(live, mixed + home_near.astype(jnp.float32), jnp.float32(0.0)).astype(jnp.bfloat16)


def solution(mesh):
    in_specs = (
        P(("rep", "dp"), None),
        P(("rep", "dp"), None),
        P(("rep", "dp"), None),
        P(("rep", "dp")),
        P(("rep", "dp")),
        P(),
        P(None, "dp"),
        P("dp", None),
    )
    out_specs = P(("rep", "dp"), None)
    return jax.shard_map(
        on_device, mesh=mesh, in_specs=in_specs, out_specs=out_specs, check_vma=False
    )
```

```python
import functools
import math

import jax
import jax.numpy as jnp
from jax import lax
from jax.experimental import pallas as pl
from jax.experimental.pallas import tpu as pltpu
from jax.sharding import PartitionSpec as P

HQ = 48
KVH = 4
HD = 128
GROUP = HQ // KVH
D = HQ * HD
SLOTS = 16
POOL = 1024
HIDDEN = 448
SIDE = 4
PAIR = 2 * SLOTS
CHUNK = 3072


def device(y, x, c):
    return (y * SIDE + x) * 2 + c


def routes():
    other = {"near": (1, 0, 3, 2), "wrap": (3, 2, 1, 0), "far": (2, 3, 0, 1)}
    out = {"core": [], **{axis + name: [] for axis in "st" for name in other}}
    for y in range(SIDE):
        for x in range(SIDE):
            for c in range(2):
                me = device(y, x, c)
                for name, to in other.items():
                    along_x, along_y = device(y, to[x], c), device(to[y], x, c)
                    out["s" + name].append((me, along_x if c == 0 else along_y))
                    out["t" + name].append((me, along_y if c == 0 else along_x))
                out["core"].append((me, device(y, x, 1 - c)))
    return out


ROUTES = routes()


def send(value, route, what):
    with jax.named_scope(what + "_" + route):
        return lax.ppermute(value, "dp", ROUTES[route])


def in_hbm(x):
    return pltpu.with_memory_space_constraint(x, pltpu.HBM)


def attend_kernel(
    lengths_in, q_in, k_in, v_in, gain_in, down, attended, normed, down_held, lengths, q, k, v, gain, sems
):
    copies = [
        pltpu.make_async_copy(a, b, sems.at[i])
        for i, (a, b) in enumerate(
            (
                (lengths_in, lengths),
                (k_in, k),
                (q_in, q),
                (v_in, v),
                (gain_in, gain),
                (down, down_held),
            )
        )
    ]
    for copy in copies:
        copy.start()
    copies[0].wait()
    column = lax.broadcasted_iota(jnp.int32, (1, HD), 1)
    starts = jnp.zeros((1, HD), jnp.int32)
    ends = jnp.zeros((1, HD), jnp.int32)
    at = jnp.int32(0)
    for i in range(SLOTS):
        after = at + lengths[i]
        starts = jnp.where(column == i, at, starts)
        ends = jnp.where(column == i, after, ends)
        at = after
    position = lax.broadcasted_iota(jnp.int32, (POOL, HD), 0)
    inside = (position >= starts) & (position < ends)
    offset = jnp.where(inside, jnp.float32(0.0), jnp.float32(-1e30)).astype(jnp.bfloat16)
    row = lax.broadcasted_iota(jnp.int32, (SLOTS, HD), 0)
    slot = lax.broadcasted_iota(jnp.int32, (SLOTS, HD), 1)
    own_slot = jnp.where(row == slot, jnp.float32(1.0), jnp.float32(0.0)).astype(jnp.bfloat16)
    own_slot = jnp.concatenate([own_slot] * GROUP, axis=0)
    squares = jnp.zeros((SLOTS, HD), jnp.float32)
    ones = jnp.ones((POOL, HD), jnp.bfloat16)
    copies[1].wait()
    copies[2].wait()
    for kv in range(KVH):
        heads = range(kv * GROUP, (kv + 1) * GROUP)
        rows = jnp.concatenate([q[:, h * HD : (h + 1) * HD] for h in heads], axis=0)
        scores = lax.dot_general(
            jnp.concatenate([rows, own_slot], axis=1),
            jnp.concatenate([k[:, kv * HD : (kv + 1) * HD], offset], axis=1),
            (((1,), (1,)), ((), ())),
            preferred_element_type=jnp.float32,
        )
        top = jnp.max(scores, axis=-1, keepdims=True)
        raised = jnp.exp2((scores - top) * jnp.float32(HD ** (-0.5) * math.log2(math.e)))
        if kv == 0:
            copies[3].wait()
        mixed = lax.dot_general(
            raised.astype(jnp.bfloat16),
            jnp.concatenate([v[:, kv * HD : (kv + 1) * HD], ones], axis=1),
            (((1,), (0,)), ((), ())),
            preferred_element_type=jnp.float32,
        )
        mixed = (mixed[:, :HD] / mixed[:, HD:]).reshape(GROUP, SLOTS, HD)
        for g, h in enumerate(heads):
            part = mixed[g].astype(jnp.bfloat16)
            attended[:, h * HD : (h + 1) * HD] = part
            wide = part.astype(jnp.float32)
            squares = squares + wide * wide
    mean_square = jnp.sum(squares, axis=-1, keepdims=True) / D
    factor = lax.rsqrt(mean_square + 1e-05)
    copies[4].wait()
    normed[...] = (attended[...].astype(jnp.float32) * factor * gain[...]).astype(jnp.bfloat16)
    copies[5].wait()


def attend(queries, cache_keys, cache_values, lengths, norm_gain, down_rows):
    vmem = pl.BlockSpec(memory_space=pltpu.VMEM)
    any_space = pl.BlockSpec(memory_space=pl.ANY)
    return pl.pallas_call(
        attend_kernel,
        out_shape=(
            jax.ShapeDtypeStruct((SLOTS, D), jnp.bfloat16),
            jax.ShapeDtypeStruct((SLOTS, D), jnp.bfloat16),
            jax.ShapeDtypeStruct((HIDDEN, D), jnp.bfloat16),
        ),
        in_specs=[any_space] * 6,
        out_specs=(vmem, vmem, vmem),
        scratch_shapes=[
            pltpu.SMEM((SLOTS,), jnp.int32),
            pltpu.VMEM((SLOTS, D), jnp.bfloat16),
            pltpu.VMEM((POOL, KVH * HD), jnp.bfloat16),
            pltpu.VMEM((POOL, KVH * HD), jnp.bfloat16),
            pltpu.VMEM((1, D), jnp.float32),
            pltpu.SemaphoreType.DMA((6,)),
        ],
        compiler_params=pltpu.CompilerParams(vmem_limit_bytes=16 * 2**20),
        name="attend",
    )(*map(in_hbm, (lengths, queries, cache_keys, cache_values, norm_gain.reshape(1, D), down_rows)))


def fetch_kernel(weights, after, held, sem):
    copy = pltpu.make_async_copy(weights, held, sem)
    copy.start()
    copy.wait()


def fetch(weights, after):
    any_space = pl.BlockSpec(memory_space=pl.ANY)
    return pl.pallas_call(
        fetch_kernel,
        out_shape=jax.ShapeDtypeStruct((HIDDEN, D), jnp.bfloat16),
        in_specs=[any_space] * 2,
        out_specs=pl.BlockSpec(memory_space=pltpu.VMEM),
        scratch_shapes=[pltpu.SemaphoreType.DMA],
        compiler_params=pltpu.CompilerParams(vmem_limit_bytes=16 * 2**20),
        cost_estimate=pl.CostEstimate(flops=10**11, bytes_accessed=4 * HIDDEN * D, transcendentals=0),
        name="fetch",
    )(in_hbm(weights), after)


def up_kernel(*args):
    blocks, up, hidden = args[:8], args[8:10], args[10]
    lows, highs = slice(0, SLOTS), slice(SLOTS, PAIR)
    order = [(part, half) for part in (0, 1) for half in (lows, highs)]
    rows = jnp.concatenate([blocks[2 * t + part][half, :] for part, half in order for t in range(SIDE)], axis=0)
    value = lax.dot_general(
        jnp.concatenate([w[...] for w in up], axis=0),
        rows,
        (((1,), (1,)), ((), ())),
        preferred_element_type=jnp.float32,
    )
    hidden[...] = (value / (1.0 + jnp.exp(-value))).astype(jnp.bfloat16).T


def project_up(blocks, up):
    vmem = pl.BlockSpec(memory_space=pltpu.VMEM)
    rows = len(blocks) * PAIR
    return pl.pallas_call(
        up_kernel,
        out_shape=jax.ShapeDtypeStruct((rows, 2 * HIDDEN), jnp.bfloat16),
        in_specs=[vmem] * 10,
        out_specs=vmem,
        compiler_params=pltpu.CompilerParams(vmem_limit_bytes=16 * 2**20),
        cost_estimate=pl.CostEstimate(flops=4 * rows * HIDDEN * D, bytes_accessed=2 * rows * D, transcendentals=0),
        name="up",
    )(*blocks, *up)


def down_kernel(begin, hidden, one, two, *outs):
    rows = pl.ds(begin * PAIR, len(outs) * PAIR)

    @pl.loop(0, D // CHUNK)
    def _(step):
        cols = pl.ds(pl.multiple_of(step * CHUNK, CHUNK), CHUNK)
        product = jnp.dot(
            hidden[rows, :],
            jnp.concatenate([one[:, cols], two[:, cols]], axis=0),
            preferred_element_type=jnp.float32,
        ).astype(jnp.bfloat16)
        for i, out in enumerate(outs):
            out[:, cols] = product[i * PAIR : (i + 1) * PAIR]


def project_down(hidden, down, begin, end):
    vmem = pl.BlockSpec(memory_space=pltpu.VMEM)
    n = end - begin
    return pl.pallas_call(
        functools.partial(down_kernel, begin),
        out_shape=[jax.ShapeDtypeStruct((PAIR, D), jnp.bfloat16)] * n,
        in_specs=[vmem] * 3,
        out_specs=[vmem] * n,
        compiler_params=pltpu.CompilerParams(vmem_limit_bytes=16 * 2**20),
        cost_estimate=pl.CostEstimate(
            flops=4 * n * PAIR * HIDDEN * D, bytes_accessed=2 * n * PAIR * D, transcendentals=0
        ),
        name="down",
    )(hidden, *down)


def pack_kernel(one, two, block):
    block[:SLOTS] = one[...]
    block[SLOTS:] = two[...]


def pack(one, two):
    vmem = pl.BlockSpec(memory_space=pltpu.VMEM)
    return pl.pallas_call(
        pack_kernel,
        out_shape=jax.ShapeDtypeStruct((PAIR, D), jnp.bfloat16),
        in_specs=[vmem] * 2,
        out_specs=vmem,
        compiler_params=pltpu.CompilerParams(vmem_limit_bytes=16 * 2**20),
        name="pack",
    )(one, two)


def hand_kernel(*refs):
    pass


def hand(held, *after):
    vmem = pl.BlockSpec(memory_space=pltpu.VMEM)
    return pl.pallas_call(
        hand_kernel,
        out_shape=jax.ShapeDtypeStruct(held.shape, held.dtype),
        in_specs=[vmem] + [pl.BlockSpec(memory_space=pl.ANY)] * len(after),
        out_specs=vmem,
        input_output_aliases={0: 0},
        compiler_params=pltpu.CompilerParams(vmem_limit_bytes=16 * 2**20),
        name="hand",
    )(held, *after)


def merge_kernel(n, mine, arrived, *refs):
    waiting, (total, *later) = refs[:n], refs[-n - 1 :]
    total[...] = (mine[...].astype(jnp.float32) + arrived[...].astype(jnp.float32)).astype(jnp.bfloat16)
    for source, target in zip(waiting, later):
        target[...] = source[...]


def merge(mine, arrived, *waiting, after=()):
    vmem = pl.BlockSpec(memory_space=pltpu.VMEM)
    n = len(waiting)
    return pl.pallas_call(
        functools.partial(merge_kernel, n),
        out_shape=[jax.ShapeDtypeStruct((PAIR, D), jnp.bfloat16)] * (1 + n),
        in_specs=[vmem] * (2 + n) + [pl.BlockSpec(memory_space=pl.ANY)] * len(after),
        out_specs=[vmem] * (1 + n),
        compiler_params=pltpu.CompilerParams(vmem_limit_bytes=16 * 2**20),
        name="merge",
    )(mine, arrived, *waiting, *after)


def finish_kernel(own, direct, back, *refs):
    one, two = refs[-2:]
    value = sum(x[...].astype(jnp.float32) for x in (own, direct, back))
    one[...] = value[:SLOTS].astype(one.dtype)
    two[...] = value[SLOTS:].astype(two.dtype)


def finish(own, direct, back, kept_type, after=()):
    vmem = pl.BlockSpec(memory_space=pltpu.VMEM)
    return pl.pallas_call(
        finish_kernel,
        out_shape=[jax.ShapeDtypeStruct((SLOTS, D), kept_type), jax.ShapeDtypeStruct((SLOTS, D), jnp.bfloat16)],
        in_specs=[vmem] * 3 + [pl.BlockSpec(memory_space=pl.ANY)] * len(after),
        out_specs=[vmem] * 2,
        compiler_params=pltpu.CompilerParams(vmem_limit_bytes=16 * 2**20),
        name="finish",
    )(own, direct, back, *after)


def collect_kernel(*refs):
    *parts, out = refs
    out[...] = sum(x[...].astype(jnp.float32) for x in parts)


def collect(*parts):
    vmem = pl.BlockSpec(memory_space=pltpu.VMEM)
    return pl.pallas_call(
        collect_kernel,
        out_shape=jax.ShapeDtypeStruct((SLOTS, D), jnp.float32),
        in_specs=[vmem] * len(parts),
        out_specs=vmem,
        compiler_params=pltpu.CompilerParams(vmem_limit_bytes=16 * 2**20),
        name="collect",
    )(*parts)


def on_device(
    queries, cache_keys, cache_values, lengths, counts, norm_gain, up_weight, down_weight
):
    up_own = up_weight.T
    up_other = send(up_own, "core", "up")
    attended, normed, down_held = attend(
        queries, cache_keys, cache_values, lengths, norm_gain, down_weight
    )
    by_wrap, by_far, by_near = [send(normed, r, "gather") for r in ("swrap", "sfar", "snear")]
    early = pack(normed, by_near)
    late = pack(by_wrap, by_far)
    early_n, late_w = send(early, "tnear", "gather"), send(late, "twrap", "gather")
    late_n, early_w = send(late, "tnear", "gather"), send(early, "twrap", "gather")
    early_n = hand(early_n, early_w)
    early_f, late_f = send(early_n, "twrap", "gather2"), send(late_w, "tnear", "gather2")
    down_held = hand(down_held, up_other)
    down_other = send(down_held, "core", "down")
    up_held = fetch(up_own, late)
    hidden = project_up(
        [early, late, early_n, late_n, early_w, late_w, early_f, late_f], (up_held, up_other)
    )
    down = (down_held, down_other)
    early_f, late_f = project_down(hidden, down, 6, 8)
    early, late, early_n, late_n, early_w, late_w = project_down(hidden, down, 0, 6)
    far_late = send(late_f, "snear", "reduce2")
    far_early = send(early_f, "swrap", "reduce2")
    direct_late = send(late_n, "snear", "reduce")
    direct_early = send(early_w, "swrap", "reduce")
    (late_w,) = merge(late_w, far_late)
    back_late = send(late_w, "swrap", "reduce")
    (early_n,) = merge(early_n, far_early, after=(late_w,))
    back_early = send(early_n, "snear", "reduce")
    home_wrap, home_far = finish(late, direct_late, back_late, jnp.bfloat16, after=(direct_early,))
    own, home_near = finish(early, direct_early, back_early, jnp.float32, after=(home_wrap,))
    home_wrap, home_far = send(home_wrap, "twrap", "home"), send(home_far, "tfar", "home")
    home_near = send(home_near, "tnear", "home")
    mixed = collect(attended, own, home_wrap, home_far)
    live = jnp.arange(SLOTS, dtype=jnp.int32)[:, None] < counts[0]
    return jnp.where(live, mixed + home_near.astype(jnp.float32), jnp.float32(0.0)).astype(jnp.bfloat16)


def solution(mesh):
    in_specs = (
        P(("rep", "dp"), None),
        P(("rep", "dp"), None),
        P(("rep", "dp"), None),
        P(("rep", "dp")),
        P(("rep", "dp")),
        P(),
        P(None, "dp"),
        P("dp", None),
    )
    out_specs = P(("rep", "dp"), None)
    return jax.shard_map(
        on_device, mesh=mesh, in_specs=in_specs, out_specs=out_specs, check_vma=False
    )
```

```python
import functools
import math

import jax
import jax.numpy as jnp
from jax import lax
from jax.experimental import pallas as pl
from jax.experimental.pallas import tpu as pltpu
from jax.sharding import PartitionSpec as P

HQ = 48
KVH = 4
HD = 128
GROUP = HQ // KVH
D = HQ * HD
SLOTS = 16
POOL = 1024
HIDDEN = 448
SIDE = 4
PAIR = 2 * SLOTS


def device(y, x, c):
    return (y * SIDE + x) * 2 + c


def routes():
    other = {"near": (1, 0, 3, 2), "wrap": (3, 2, 1, 0), "far": (2, 3, 0, 1)}
    out = {"core": [], **{axis + name: [] for axis in "st" for name in other}}
    for y in range(SIDE):
        for x in range(SIDE):
            for c in range(2):
                me = device(y, x, c)
                for name, to in other.items():
                    along_x, along_y = device(y, to[x], c), device(to[y], x, c)
                    out["s" + name].append((me, along_x if c == 0 else along_y))
                    out["t" + name].append((me, along_y if c == 0 else along_x))
                out["core"].append((me, device(y, x, 1 - c)))
    return out


ROUTES = routes()


def send(value, route, what):
    with jax.named_scope(what + "_" + route):
        return lax.ppermute(value, "dp", ROUTES[route])


def in_hbm(x):
    return pltpu.with_memory_space_constraint(x, pltpu.HBM)


def attend_kernel(
    lengths_in, q_in, k_in, v_in, gain_in, down, attended, normed, down_held, lengths, q, k, v, gain, sems
):
    copies = [
        pltpu.make_async_copy(a, b, sems.at[i])
        for i, (a, b) in enumerate(
            (
                (lengths_in, lengths),
                (k_in, k),
                (q_in, q),
                (v_in, v),
                (gain_in, gain),
                (down, down_held),
            )
        )
    ]
    for copy in copies:
        copy.start()
    copies[0].wait()
    row = lax.broadcasted_iota(jnp.int32, (SLOTS, 1), 0)
    starts = jnp.zeros((SLOTS, 1), jnp.int32)
    ends = jnp.zeros((SLOTS, 1), jnp.int32)
    at = jnp.int32(0)
    for i in range(SLOTS):
        after = at + lengths[i]
        starts = jnp.where(row == i, at, starts)
        ends = jnp.where(row == i, after, ends)
        at = after
    position = lax.broadcasted_iota(jnp.int32, (SLOTS, POOL), 1)
    inside = (position >= starts) & (position < ends)
    offset = jnp.where(inside, jnp.float32(0.0), jnp.float32(-1e30))
    squares = jnp.zeros((SLOTS, HD), jnp.float32)
    ones = jnp.ones((POOL, HD), jnp.bfloat16)
    copies[1].wait()
    copies[2].wait()
    for kv in range(KVH):
        heads = range(kv * GROUP, (kv + 1) * GROUP)
        rows = jnp.concatenate([q[:, h * HD : (h + 1) * HD] for h in heads], axis=0)
        scores = lax.dot_general(
            rows,
            k[:, kv * HD : (kv + 1) * HD],
            (((1,), (1,)), ((), ())),
            preferred_element_type=jnp.float32,
        )
        masked = scores.reshape(GROUP, SLOTS, POOL) + offset[None]
        top = jnp.max(masked, axis=-1, keepdims=True)
        raised = jnp.exp2((masked - top) * jnp.float32(HD ** (-0.5) * math.log2(math.e)))
        if kv == 0:
            copies[3].wait()
        mixed = lax.dot_general(
            raised.astype(jnp.bfloat16).reshape(GROUP * SLOTS, POOL),
            jnp.concatenate([v[:, kv * HD : (kv + 1) * HD], ones], axis=1),
            (((1,), (0,)), ((), ())),
            preferred_element_type=jnp.float32,
        )
        mixed = (mixed[:, :HD] / mixed[:, HD:]).reshape(GROUP, SLOTS, HD)
        for g, h in enumerate(heads):
            part = mixed[g].astype(jnp.bfloat16)
            attended[:, h * HD : (h + 1) * HD] = part
            wide = part.astype(jnp.float32)
            squares = squares + wide * wide
    mean_square = jnp.sum(squares, axis=-1, keepdims=True) / D
    factor = lax.rsqrt(mean_square + 1e-05)
    copies[4].wait()
    normed[...] = (attended[...].astype(jnp.float32) * factor * gain[...]).astype(jnp.bfloat16)
    copies[5].wait()


def attend(queries, cache_keys, cache_values, lengths, norm_gain, down_rows):
    vmem = pl.BlockSpec(memory_space=pltpu.VMEM)
    any_space = pl.BlockSpec(memory_space=pl.ANY)
    return pl.pallas_call(
        attend_kernel,
        out_shape=(
            jax.ShapeDtypeStruct((SLOTS, D), jnp.bfloat16),
            jax.ShapeDtypeStruct((SLOTS, D), jnp.bfloat16),
            jax.ShapeDtypeStruct((HIDDEN, D), jnp.bfloat16),
        ),
        in_specs=[any_space] * 6,
        out_specs=(vmem, vmem, vmem),
        scratch_shapes=[
            pltpu.SMEM((SLOTS,), jnp.int32),
            pltpu.VMEM((SLOTS, D), jnp.bfloat16),
            pltpu.VMEM((POOL, KVH * HD), jnp.bfloat16),
            pltpu.VMEM((POOL, KVH * HD), jnp.bfloat16),
            pltpu.VMEM((1, D), jnp.float32),
            pltpu.SemaphoreType.DMA((6,)),
        ],
        compiler_params=pltpu.CompilerParams(vmem_limit_bytes=16 * 2**20),
        name="attend",
    )(*map(in_hbm, (lengths, queries, cache_keys, cache_values, norm_gain.reshape(1, D), down_rows)))


def fetch_kernel(weights, after, held, sem):
    copy = pltpu.make_async_copy(weights, held, sem)
    copy.start()
    copy.wait()


def fetch(weights, after):
    any_space = pl.BlockSpec(memory_space=pl.ANY)
    return pl.pallas_call(
        fetch_kernel,
        out_shape=jax.ShapeDtypeStruct((HIDDEN, D), jnp.bfloat16),
        in_specs=[any_space] * 2,
        out_specs=pl.BlockSpec(memory_space=pltpu.VMEM),
        scratch_shapes=[pltpu.SemaphoreType.DMA],
        compiler_params=pltpu.CompilerParams(vmem_limit_bytes=16 * 2**20),
        cost_estimate=pl.CostEstimate(flops=10**11, bytes_accessed=4 * HIDDEN * D, transcendentals=0),
        name="fetch",
    )(in_hbm(weights), after)


def up_kernel(*args):
    blocks, up, hidden = args[:8], args[8:10], args[10]
    lows, highs = slice(0, SLOTS), slice(SLOTS, PAIR)
    order = [(part, half) for part in (0, 1) for half in (lows, highs)]
    rows = jnp.concatenate([blocks[2 * t + part][half, :] for part, half in order for t in range(SIDE)], axis=0)
    value = lax.dot_general(
        jnp.concatenate([w[...] for w in up], axis=0),
        rows,
        (((1,), (1,)), ((), ())),
        preferred_element_type=jnp.float32,
    )
    hidden[...] = (value / (1.0 + jnp.exp(-value))).astype(jnp.bfloat16).T


def project_up(blocks, up):
    vmem = pl.BlockSpec(memory_space=pltpu.VMEM)
    rows = len(blocks) * PAIR
    return pl.pallas_call(
        up_kernel,
        out_shape=jax.ShapeDtypeStruct((rows, 2 * HIDDEN), jnp.bfloat16),
        in_specs=[vmem] * 10,
        out_specs=vmem,
        compiler_params=pltpu.CompilerParams(vmem_limit_bytes=16 * 2**20),
        cost_estimate=pl.CostEstimate(flops=4 * rows * HIDDEN * D, bytes_accessed=2 * rows * D, transcendentals=0),
        name="up",
    )(*blocks, *up)


def down_kernel(begin, hidden, one, two, *outs):
    product = jnp.dot(
        hidden[begin * PAIR : (begin + len(outs)) * PAIR, :],
        jnp.concatenate([one[...], two[...]], axis=0),
        preferred_element_type=jnp.float32,
    ).astype(jnp.bfloat16)
    for i, out in enumerate(outs):
        out[...] = product[i * PAIR : (i + 1) * PAIR]


def project_down(hidden, down, begin, end):
    vmem = pl.BlockSpec(memory_space=pltpu.VMEM)
    n = end - begin
    return pl.pallas_call(
        functools.partial(down_kernel, begin),
        out_shape=[jax.ShapeDtypeStruct((PAIR, D), jnp.bfloat16)] * n,
        in_specs=[vmem] * 3,
        out_specs=[vmem] * n,
        compiler_params=pltpu.CompilerParams(vmem_limit_bytes=16 * 2**20),
        cost_estimate=pl.CostEstimate(
            flops=4 * n * PAIR * HIDDEN * D, bytes_accessed=2 * n * PAIR * D, transcendentals=0
        ),
        name="down",
    )(hidden, *down)


def pack_kernel(one, two, block):
    block[:SLOTS] = one[...]
    block[SLOTS:] = two[...]


def pack(one, two):
    vmem = pl.BlockSpec(memory_space=pltpu.VMEM)
    return pl.pallas_call(
        pack_kernel,
        out_shape=jax.ShapeDtypeStruct((PAIR, D), jnp.bfloat16),
        in_specs=[vmem] * 2,
        out_specs=vmem,
        compiler_params=pltpu.CompilerParams(vmem_limit_bytes=16 * 2**20),
        name="pack",
    )(one, two)


def hand_kernel(*refs):
    pass


def hand(held, *after):
    vmem = pl.BlockSpec(memory_space=pltpu.VMEM)
    return pl.pallas_call(
        hand_kernel,
        out_shape=jax.ShapeDtypeStruct(held.shape, held.dtype),
        in_specs=[vmem] + [pl.BlockSpec(memory_space=pl.ANY)] * len(after),
        out_specs=vmem,
        input_output_aliases={0: 0},
        compiler_params=pltpu.CompilerParams(vmem_limit_bytes=16 * 2**20),
        name="hand",
    )(held, *after)


def merge_kernel(n, mine, arrived, *refs):
    waiting, (total, *later) = refs[:n], refs[-n - 1 :]
    total[...] = (mine[...].astype(jnp.float32) + arrived[...].astype(jnp.float32)).astype(jnp.bfloat16)
    for source, target in zip(waiting, later):
        target[...] = source[...]


def merge(mine, arrived, *waiting, after=()):
    vmem = pl.BlockSpec(memory_space=pltpu.VMEM)
    n = len(waiting)
    return pl.pallas_call(
        functools.partial(merge_kernel, n),
        out_shape=[jax.ShapeDtypeStruct((PAIR, D), jnp.bfloat16)] * (1 + n),
        in_specs=[vmem] * (2 + n) + [pl.BlockSpec(memory_space=pl.ANY)] * len(after),
        out_specs=[vmem] * (1 + n),
        compiler_params=pltpu.CompilerParams(vmem_limit_bytes=16 * 2**20),
        name="merge",
    )(mine, arrived, *waiting, *after)


def finish_kernel(own, direct, back, *refs):
    one, two = refs[-2:]
    value = sum(x[...].astype(jnp.float32) for x in (own, direct, back))
    one[...] = value[:SLOTS].astype(one.dtype)
    two[...] = value[SLOTS:].astype(two.dtype)


def finish(own, direct, back, kept_type, after=()):
    vmem = pl.BlockSpec(memory_space=pltpu.VMEM)
    return pl.pallas_call(
        finish_kernel,
        out_shape=[jax.ShapeDtypeStruct((SLOTS, D), kept_type), jax.ShapeDtypeStruct((SLOTS, D), jnp.bfloat16)],
        in_specs=[vmem] * 3 + [pl.BlockSpec(memory_space=pl.ANY)] * len(after),
        out_specs=[vmem] * 2,
        compiler_params=pltpu.CompilerParams(vmem_limit_bytes=16 * 2**20),
        name="finish",
    )(own, direct, back, *after)


def collect_kernel(*refs):
    *parts, out = refs
    out[...] = sum(x[...].astype(jnp.float32) for x in parts)


def collect(*parts):
    vmem = pl.BlockSpec(memory_space=pltpu.VMEM)
    return pl.pallas_call(
        collect_kernel,
        out_shape=jax.ShapeDtypeStruct((SLOTS, D), jnp.float32),
        in_specs=[vmem] * len(parts),
        out_specs=vmem,
        compiler_params=pltpu.CompilerParams(vmem_limit_bytes=16 * 2**20),
        name="collect",
    )(*parts)


def on_device(
    queries, cache_keys, cache_values, lengths, counts, norm_gain, up_weight, down_weight
):
    up_own = up_weight.T
    up_other = send(up_own, "core", "up")
    attended, normed, down_held = attend(
        queries, cache_keys, cache_values, lengths, norm_gain, down_weight
    )
    by_wrap, by_far, by_near = [send(normed, r, "gather") for r in ("swrap", "sfar", "snear")]
    early = pack(normed, by_near)
    late = pack(by_wrap, by_far)
    early_n, late_w = send(early, "tnear", "gather"), send(late, "twrap", "gather")
    late_n, early_w = send(late, "tnear", "gather"), send(early, "twrap", "gather")
    early_n = hand(early_n, early_w)
    early_f, late_f = send(early_n, "twrap", "gather2"), send(late_w, "tnear", "gather2")
    down_held = hand(down_held, up_other)
    down_other = send(down_held, "core", "down")
    up_held = fetch(up_own, late)
    hidden = project_up(
        [early, late, early_n, late_n, early_w, late_w, early_f, late_f], (up_held, up_other)
    )
    down = (down_held, down_other)
    early_f, late_f = project_down(hidden, down, 6, 8)
    early, late, early_n, late_n, early_w, late_w = project_down(hidden, down, 0, 6)
    far_late = send(late_f, "snear", "reduce2")
    far_early = send(early_f, "swrap", "reduce2")
    direct_late = send(late_n, "snear", "reduce")
    direct_early = send(early_w, "swrap", "reduce")
    (late_w,) = merge(late_w, far_late)
    back_late = send(late_w, "swrap", "reduce")
    (early_n,) = merge(early_n, far_early, after=(late_w,))
    back_early = send(early_n, "snear", "reduce")
    home_wrap, home_far = finish(late, direct_late, back_late, jnp.bfloat16, after=(direct_early,))
    own, home_near = finish(early, direct_early, back_early, jnp.float32, after=(home_wrap,))
    home_wrap, home_far = send(home_wrap, "twrap", "home"), send(home_far, "tfar", "home")
    home_near = send(home_near, "tnear", "home")
    mixed = collect(attended, own, home_wrap, home_far)
    live = jnp.arange(SLOTS, dtype=jnp.int32)[:, None] < counts[0]
    return jnp.where(live, mixed + home_near.astype(jnp.float32), jnp.float32(0.0)).astype(jnp.bfloat16)


def solution(mesh):
    in_specs = (
        P(("rep", "dp"), None),
        P(("rep", "dp"), None),
        P(("rep", "dp"), None),
        P(("rep", "dp")),
        P(("rep", "dp")),
        P(),
        P(None, "dp"),
        P("dp", None),
    )
    out_specs = P(("rep", "dp"), None)
    return jax.shard_map(
        on_device, mesh=mesh, in_specs=in_specs, out_specs=out_specs, check_vma=False
    )
```

```python
import functools
import math

import jax
import jax.numpy as jnp
from jax import lax
from jax.experimental import pallas as pl
from jax.experimental.pallas import tpu as pltpu
from jax.sharding import PartitionSpec as P

HQ = 48
KVH = 4
HD = 128
GROUP = HQ // KVH
D = HQ * HD
SLOTS = 16
POOL = 1024
HIDDEN = 448
SIDE = 4
PAIR = 2 * SLOTS


def device(y, x, c):
    return (y * SIDE + x) * 2 + c


def routes():
    other = {"near": (1, 0, 3, 2), "wrap": (3, 2, 1, 0), "far": (2, 3, 0, 1)}
    out = {"core": [], **{axis + name: [] for axis in "st" for name in other}}
    for y in range(SIDE):
        for x in range(SIDE):
            for c in range(2):
                me = device(y, x, c)
                for name, to in other.items():
                    along_x, along_y = device(y, to[x], c), device(to[y], x, c)
                    out["s" + name].append((me, along_x if c == 0 else along_y))
                    out["t" + name].append((me, along_y if c == 0 else along_x))
                out["core"].append((me, device(y, x, 1 - c)))
    return out


ROUTES = routes()


def send(value, route, what):
    with jax.named_scope(what + "_" + route):
        return lax.ppermute(value, "dp", ROUTES[route])


def in_hbm(x):
    return pltpu.with_memory_space_constraint(x, pltpu.HBM)


def attend_kernel(
    lengths_in, q_in, k_in, v_in, gain_in, down, attended, normed, down_held, lengths, q, k, v, gain, sems
):
    copies = [
        pltpu.make_async_copy(a, b, sems.at[i])
        for i, (a, b) in enumerate(
            (
                (lengths_in, lengths),
                (k_in, k),
                (q_in, q),
                (v_in, v),
                (gain_in, gain),
                (down, down_held),
            )
        )
    ]
    for copy in copies:
        copy.start()
    copies[0].wait()
    row = lax.broadcasted_iota(jnp.int32, (SLOTS, 1), 0)
    starts = jnp.zeros((SLOTS, 1), jnp.int32)
    ends = jnp.zeros((SLOTS, 1), jnp.int32)
    at = jnp.int32(0)
    for i in range(SLOTS):
        after = at + lengths[i]
        starts = jnp.where(row == i, at, starts)
        ends = jnp.where(row == i, after, ends)
        at = after
    position = lax.broadcasted_iota(jnp.int32, (SLOTS, POOL), 1)
    inside = (position >= starts) & (position < ends)
    offset = jnp.where(inside, jnp.float32(0.0), jnp.float32(-1e30))
    squares = jnp.zeros((SLOTS, HD), jnp.float32)
    ones = jnp.ones((POOL, HD), jnp.bfloat16)
    copies[1].wait()
    copies[2].wait()
    for kv in range(KVH):
        heads = range(kv * GROUP, (kv + 1) * GROUP)
        rows = jnp.concatenate([q[:, h * HD : (h + 1) * HD] for h in heads], axis=0)
        scores = lax.dot_general(
            rows,
            k[:, kv * HD : (kv + 1) * HD],
            (((1,), (1,)), ((), ())),
            preferred_element_type=jnp.float32,
        )
        masked = scores.reshape(GROUP, SLOTS, POOL) + offset[None]
        top = jnp.max(masked, axis=-1, keepdims=True)
        raised = jnp.exp2((masked - top) * jnp.float32(HD ** (-0.5) * math.log2(math.e)))
        if kv == 0:
            copies[3].wait()
        mixed = lax.dot_general(
            raised.astype(jnp.bfloat16).reshape(GROUP * SLOTS, POOL),
            jnp.concatenate([v[:, kv * HD : (kv + 1) * HD], ones], axis=1),
            (((1,), (0,)), ((), ())),
            preferred_element_type=jnp.float32,
        )
        mixed = (mixed[:, :HD] / mixed[:, HD:]).reshape(GROUP, SLOTS, HD)
        for g, h in enumerate(heads):
            part = mixed[g].astype(jnp.bfloat16)
            attended[:, h * HD : (h + 1) * HD] = part
            wide = part.astype(jnp.float32)
            squares = squares + wide * wide
    mean_square = jnp.sum(squares, axis=-1, keepdims=True) / D
    factor = lax.rsqrt(mean_square + 1e-05)
    copies[4].wait()
    normed[...] = (attended[...].astype(jnp.float32) * factor * gain[...]).astype(jnp.bfloat16)
    copies[5].wait()


def attend(queries, cache_keys, cache_values, lengths, norm_gain, down_rows):
    vmem = pl.BlockSpec(memory_space=pltpu.VMEM)
    any_space = pl.BlockSpec(memory_space=pl.ANY)
    return pl.pallas_call(
        attend_kernel,
        out_shape=(
            jax.ShapeDtypeStruct((SLOTS, D), jnp.bfloat16),
            jax.ShapeDtypeStruct((SLOTS, D), jnp.bfloat16),
            jax.ShapeDtypeStruct((HIDDEN, D), jnp.bfloat16),
        ),
        in_specs=[any_space] * 6,
        out_specs=(vmem, vmem, vmem),
        scratch_shapes=[
            pltpu.SMEM((SLOTS,), jnp.int32),
            pltpu.VMEM((SLOTS, D), jnp.bfloat16),
            pltpu.VMEM((POOL, KVH * HD), jnp.bfloat16),
            pltpu.VMEM((POOL, KVH * HD), jnp.bfloat16),
            pltpu.VMEM((1, D), jnp.float32),
            pltpu.SemaphoreType.DMA((6,)),
        ],
        compiler_params=pltpu.CompilerParams(vmem_limit_bytes=16 * 2**20),
        name="attend",
    )(*map(in_hbm, (lengths, queries, cache_keys, cache_values, norm_gain.reshape(1, D), down_rows)))


def fetch_kernel(weights, after, held, sem):
    copy = pltpu.make_async_copy(weights, held, sem)
    copy.start()
    copy.wait()


def fetch(weights, after):
    any_space = pl.BlockSpec(memory_space=pl.ANY)
    return pl.pallas_call(
        fetch_kernel,
        out_shape=jax.ShapeDtypeStruct((HIDDEN, D), jnp.bfloat16),
        in_specs=[any_space] * 2,
        out_specs=pl.BlockSpec(memory_space=pltpu.VMEM),
        scratch_shapes=[pltpu.SemaphoreType.DMA],
        compiler_params=pltpu.CompilerParams(vmem_limit_bytes=16 * 2**20),
        cost_estimate=pl.CostEstimate(flops=10**11, bytes_accessed=4 * HIDDEN * D, transcendentals=0),
        name="fetch",
    )(in_hbm(weights), after)


def up_kernel(*args):
    blocks, up, hidden = args[:8], args[8:10], args[10]
    lows, highs = slice(0, SLOTS), slice(SLOTS, PAIR)
    order = [(part, half) for part in (0, 1) for half in (lows, highs)]
    rows = jnp.concatenate([blocks[2 * t + part][half, :] for part, half in order for t in range(SIDE)], axis=0)
    value = lax.dot_general(
        jnp.concatenate([w[...] for w in up], axis=0),
        rows,
        (((1,), (1,)), ((), ())),
        preferred_element_type=jnp.float32,
    )
    hidden[...] = (value / (1.0 + jnp.exp(-value))).astype(jnp.bfloat16).T


def project_up(blocks, up):
    vmem = pl.BlockSpec(memory_space=pltpu.VMEM)
    rows = len(blocks) * PAIR
    return pl.pallas_call(
        up_kernel,
        out_shape=jax.ShapeDtypeStruct((rows, 2 * HIDDEN), jnp.bfloat16),
        in_specs=[vmem] * 10,
        out_specs=vmem,
        compiler_params=pltpu.CompilerParams(vmem_limit_bytes=16 * 2**20),
        cost_estimate=pl.CostEstimate(flops=4 * rows * HIDDEN * D, bytes_accessed=2 * rows * D, transcendentals=0),
        name="up",
    )(*blocks, *up)


def down_kernel(begin, hidden, one, two, *outs):
    product = jnp.dot(
        hidden[begin * PAIR : (begin + len(outs)) * PAIR, :],
        jnp.concatenate([one[...], two[...]], axis=0),
        preferred_element_type=jnp.float32,
    ).astype(jnp.bfloat16)
    for i, out in enumerate(outs):
        out[...] = product[i * PAIR : (i + 1) * PAIR]


def project_down(hidden, down, begin, end):
    vmem = pl.BlockSpec(memory_space=pltpu.VMEM)
    n = end - begin
    return pl.pallas_call(
        functools.partial(down_kernel, begin),
        out_shape=[jax.ShapeDtypeStruct((PAIR, D), jnp.bfloat16)] * n,
        in_specs=[vmem] * 3,
        out_specs=[vmem] * n,
        compiler_params=pltpu.CompilerParams(vmem_limit_bytes=16 * 2**20),
        cost_estimate=pl.CostEstimate(
            flops=4 * n * PAIR * HIDDEN * D, bytes_accessed=2 * n * PAIR * D, transcendentals=0
        ),
        name="down",
    )(hidden, *down)


def pack_kernel(one, two, block):
    block[:SLOTS] = one[...]
    block[SLOTS:] = two[...]


def pack(one, two):
    vmem = pl.BlockSpec(memory_space=pltpu.VMEM)
    return pl.pallas_call(
        pack_kernel,
        out_shape=jax.ShapeDtypeStruct((PAIR, D), jnp.bfloat16),
        in_specs=[vmem] * 2,
        out_specs=vmem,
        compiler_params=pltpu.CompilerParams(vmem_limit_bytes=16 * 2**20),
        name="pack",
    )(one, two)


def hand_kernel(*refs):
    pass


def hand(held, *after):
    vmem = pl.BlockSpec(memory_space=pltpu.VMEM)
    return pl.pallas_call(
        hand_kernel,
        out_shape=jax.ShapeDtypeStruct(held.shape, held.dtype),
        in_specs=[vmem] + [pl.BlockSpec(memory_space=pl.ANY)] * len(after),
        out_specs=vmem,
        input_output_aliases={0: 0},
        compiler_params=pltpu.CompilerParams(vmem_limit_bytes=16 * 2**20),
        name="hand",
    )(held, *after)


def merge_kernel(n, mine, arrived, *refs):
    waiting, (total, *later) = refs[:n], refs[-n - 1 :]
    total[...] = (mine[...].astype(jnp.float32) + arrived[...].astype(jnp.float32)).astype(jnp.bfloat16)
    for source, target in zip(waiting, later):
        target[...] = source[...]


def merge(mine, arrived, *waiting, after=()):
    vmem = pl.BlockSpec(memory_space=pltpu.VMEM)
    n = len(waiting)
    return pl.pallas_call(
        functools.partial(merge_kernel, n),
        out_shape=[jax.ShapeDtypeStruct((PAIR, D), jnp.bfloat16)] * (1 + n),
        in_specs=[vmem] * (2 + n) + [pl.BlockSpec(memory_space=pl.ANY)] * len(after),
        out_specs=[vmem] * (1 + n),
        compiler_params=pltpu.CompilerParams(vmem_limit_bytes=16 * 2**20),
        name="merge",
    )(mine, arrived, *waiting, *after)


def finish_kernel(own, direct, back, *refs):
    one, two = refs[-2:]
    value = sum(x[...].astype(jnp.float32) for x in (own, direct, back))
    one[...] = value[:SLOTS].astype(one.dtype)
    two[...] = value[SLOTS:].astype(two.dtype)


def finish(own, direct, back, kept_type, after=()):
    vmem = pl.BlockSpec(memory_space=pltpu.VMEM)
    return pl.pallas_call(
        finish_kernel,
        out_shape=[jax.ShapeDtypeStruct((SLOTS, D), kept_type), jax.ShapeDtypeStruct((SLOTS, D), jnp.bfloat16)],
        in_specs=[vmem] * 3 + [pl.BlockSpec(memory_space=pl.ANY)] * len(after),
        out_specs=[vmem] * 2,
        compiler_params=pltpu.CompilerParams(vmem_limit_bytes=16 * 2**20),
        name="finish",
    )(own, direct, back, *after)


def collect_kernel(*refs):
    *parts, out = refs
    out[...] = sum(x[...].astype(jnp.float32) for x in parts)


def collect(*parts):
    vmem = pl.BlockSpec(memory_space=pltpu.VMEM)
    return pl.pallas_call(
        collect_kernel,
        out_shape=jax.ShapeDtypeStruct((SLOTS, D), jnp.float32),
        in_specs=[vmem] * len(parts),
        out_specs=vmem,
        compiler_params=pltpu.CompilerParams(vmem_limit_bytes=16 * 2**20),
        name="collect",
    )(*parts)


def on_device(
    queries, cache_keys, cache_values, lengths, counts, norm_gain, up_weight, down_weight
):
    up_own = up_weight.T
    up_other = send(up_own, "core", "up")
    attended, normed, down_held = attend(
        queries, cache_keys, cache_values, lengths, norm_gain, down_weight
    )
    by_wrap, by_far, by_near = [send(normed, r, "gather") for r in ("swrap", "sfar", "snear")]
    early = pack(normed, by_near)
    late = pack(by_wrap, by_far)
    early_n, late_w = send(early, "tnear", "gather"), send(late, "twrap", "gather")
    late_n, early_w = send(late, "tnear", "gather"), send(early, "twrap", "gather")
    early_n = hand(early_n, early_w)
    early_f, late_f = send(early_n, "twrap", "gather2"), send(late_w, "tnear", "gather2")
    down_held = hand(down_held, up_other)
    down_other = send(down_held, "core", "down")
    up_held = fetch(up_own, late)
    hidden = project_up(
        [early, late, early_n, late_n, early_w, late_w, early_f, late_f], (up_held, up_other)
    )
    down = (down_held, down_other)
    early_f, late_f = project_down(hidden, down, 6, 8)
    early, late, early_n, late_n, early_w, late_w = project_down(hidden, down, 0, 6)
    far_late = send(late_f, "snear", "reduce2")
    far_early = send(early_f, "swrap", "reduce2")
    direct_late = send(late_n, "snear", "reduce")
    direct_early = send(early_w, "swrap", "reduce")
    (late_w,) = merge(late_w, far_late)
    back_late = send(late_w, "swrap", "reduce")
    (early_n,) = merge(early_n, far_early, after=(late_w,))
    back_early = send(early_n, "snear", "reduce")
    home_wrap, home_far = finish(late, direct_late, back_late, jnp.bfloat16, after=(direct_early,))
    own, home_near = finish(early, direct_early, back_early, jnp.float32, after=(home_wrap,))
    home_wrap, home_far = send(home_wrap, "twrap", "home"), send(home_far, "tfar", "home")
    home_near = send(home_near, "tnear", "home")
    mixed = collect(attended, own, home_far, home_wrap)
    live = jnp.arange(SLOTS, dtype=jnp.int32)[:, None] < counts[0]
    return jnp.where(live, mixed + home_near.astype(jnp.float32), jnp.float32(0.0)).astype(jnp.bfloat16)


def solution(mesh):
    in_specs = (
        P(("rep", "dp"), None),
        P(("rep", "dp"), None),
        P(("rep", "dp"), None),
        P(("rep", "dp")),
        P(("rep", "dp")),
        P(),
        P(None, "dp"),
        P("dp", None),
    )
    out_specs = P(("rep", "dp"), None)
    return jax.shard_map(
        on_device, mesh=mesh, in_specs=in_specs, out_specs=out_specs, check_vma=False
    )
```

```python
import functools
import math

import jax
import jax.numpy as jnp
from jax import lax
from jax.experimental import pallas as pl
from jax.experimental.pallas import tpu as pltpu
from jax.sharding import PartitionSpec as P

HQ = 48
KVH = 4
HD = 128
GROUP = HQ // KVH
D = HQ * HD
SLOTS = 16
POOL = 1024
HIDDEN = 448
SIDE = 4
PAIR = 2 * SLOTS


def device(y, x, c):
    return (y * SIDE + x) * 2 + c


def routes():
    other = {"near": (1, 0, 3, 2), "wrap": (3, 2, 1, 0), "far": (2, 3, 0, 1)}
    out = {"core": [], **{axis + name: [] for axis in "st" for name in other}}
    for y in range(SIDE):
        for x in range(SIDE):
            for c in range(2):
                me = device(y, x, c)
                for name, to in other.items():
                    along_x, along_y = device(y, to[x], c), device(to[y], x, c)
                    out["s" + name].append((me, along_x if c == 0 else along_y))
                    out["t" + name].append((me, along_y if c == 0 else along_x))
                out["core"].append((me, device(y, x, 1 - c)))
    return out


ROUTES = routes()


def send(value, route, what):
    with jax.named_scope(what + "_" + route):
        return lax.ppermute(value, "dp", ROUTES[route])


def in_hbm(x):
    return pltpu.with_memory_space_constraint(x, pltpu.HBM)


def attend_kernel(
    lengths_in, q_in, k_in, v_in, gain_in, down, attended, normed, down_held, lengths, q, k, v, gain, sems
):
    copies = [
        pltpu.make_async_copy(a, b, sems.at[i])
        for i, (a, b) in enumerate(
            (
                (lengths_in, lengths),
                (k_in, k),
                (q_in, q),
                (v_in, v),
                (gain_in, gain),
                (down, down_held),
            )
        )
    ]
    for copy in copies:
        copy.start()
    copies[0].wait()
    row = lax.broadcasted_iota(jnp.int32, (SLOTS, 1), 0)
    starts = jnp.zeros((SLOTS, 1), jnp.int32)
    ends = jnp.zeros((SLOTS, 1), jnp.int32)
    at = jnp.int32(0)
    for i in range(SLOTS):
        after = at + lengths[i]
        starts = jnp.where(row == i, at, starts)
        ends = jnp.where(row == i, after, ends)
        at = after
    position = lax.broadcasted_iota(jnp.int32, (SLOTS, POOL), 1)
    inside = (position >= starts) & (position < ends)
    offset = jnp.where(inside, jnp.float32(0.0), jnp.float32(-1e30))
    squares = jnp.zeros((SLOTS, HD), jnp.float32)
    ones = jnp.ones((POOL, HD), jnp.bfloat16)
    copies[1].wait()
    copies[2].wait()
    for kv in range(KVH):
        heads = range(kv * GROUP, (kv + 1) * GROUP)
        rows = jnp.concatenate([q[:, h * HD : (h + 1) * HD] for h in heads], axis=0)
        scores = lax.dot_general(
            rows,
            k[:, kv * HD : (kv + 1) * HD],
            (((1,), (1,)), ((), ())),
            preferred_element_type=jnp.float32,
        )
        masked = scores.reshape(GROUP, SLOTS, POOL) + offset[None]
        top = jnp.max(masked, axis=-1, keepdims=True)
        raised = jnp.exp2((masked - top) * jnp.float32(HD ** (-0.5) * math.log2(math.e)))
        if kv == 0:
            copies[3].wait()
        mixed = lax.dot_general(
            raised.astype(jnp.bfloat16).reshape(GROUP * SLOTS, POOL),
            jnp.concatenate([v[:, kv * HD : (kv + 1) * HD], ones], axis=1),
            (((1,), (0,)), ((), ())),
            preferred_element_type=jnp.float32,
        )
        mixed = (mixed[:, :HD] / mixed[:, HD:]).reshape(GROUP, SLOTS, HD)
        for g, h in enumerate(heads):
            part = mixed[g].astype(jnp.bfloat16)
            attended[:, h * HD : (h + 1) * HD] = part
            wide = part.astype(jnp.float32)
            squares = squares + wide * wide
    mean_square = jnp.sum(squares, axis=-1, keepdims=True) / D
    factor = lax.rsqrt(mean_square + 1e-05)
    copies[4].wait()
    normed[...] = (attended[...].astype(jnp.float32) * factor * gain[...]).astype(jnp.bfloat16)
    copies[5].wait()


def attend(queries, cache_keys, cache_values, lengths, norm_gain, down_rows):
    vmem = pl.BlockSpec(memory_space=pltpu.VMEM)
    any_space = pl.BlockSpec(memory_space=pl.ANY)
    return pl.pallas_call(
        attend_kernel,
        out_shape=(
            jax.ShapeDtypeStruct((SLOTS, D), jnp.bfloat16),
            jax.ShapeDtypeStruct((SLOTS, D), jnp.bfloat16),
            jax.ShapeDtypeStruct((HIDDEN, D), jnp.bfloat16),
        ),
        in_specs=[any_space] * 6,
        out_specs=(vmem, vmem, vmem),
        scratch_shapes=[
            pltpu.SMEM((SLOTS,), jnp.int32),
            pltpu.VMEM((SLOTS, D), jnp.bfloat16),
            pltpu.VMEM((POOL, KVH * HD), jnp.bfloat16),
            pltpu.VMEM((POOL, KVH * HD), jnp.bfloat16),
            pltpu.VMEM((1, D), jnp.float32),
            pltpu.SemaphoreType.DMA((6,)),
        ],
        compiler_params=pltpu.CompilerParams(vmem_limit_bytes=16 * 2**20),
        name="attend",
    )(*map(in_hbm, (lengths, queries, cache_keys, cache_values, norm_gain.reshape(1, D), down_rows)))


def fetch_kernel(weights, after, held, sem):
    copy = pltpu.make_async_copy(weights, held, sem)
    copy.start()
    copy.wait()


def fetch(weights, after):
    any_space = pl.BlockSpec(memory_space=pl.ANY)
    return pl.pallas_call(
        fetch_kernel,
        out_shape=jax.ShapeDtypeStruct((HIDDEN, D), jnp.bfloat16),
        in_specs=[any_space] * 2,
        out_specs=pl.BlockSpec(memory_space=pltpu.VMEM),
        scratch_shapes=[pltpu.SemaphoreType.DMA],
        compiler_params=pltpu.CompilerParams(vmem_limit_bytes=16 * 2**20),
        cost_estimate=pl.CostEstimate(flops=10**11, bytes_accessed=4 * HIDDEN * D, transcendentals=0),
        name="fetch",
    )(in_hbm(weights), after)


def up_kernel(*args):
    blocks, up, hidden = args[:8], args[8:10], args[10]
    lows, highs = slice(0, SLOTS), slice(SLOTS, PAIR)
    order = [(part, half) for part in (0, 1) for half in (lows, highs)]
    rows = jnp.concatenate([blocks[2 * t + part][half, :] for part, half in order for t in range(SIDE)], axis=0)
    value = lax.dot_general(
        jnp.concatenate([w[...] for w in up], axis=0),
        rows,
        (((1,), (1,)), ((), ())),
        preferred_element_type=jnp.float32,
    )
    hidden[...] = (value / (1.0 + jnp.exp(-value))).astype(jnp.bfloat16).T


def project_up(blocks, up):
    vmem = pl.BlockSpec(memory_space=pltpu.VMEM)
    rows = len(blocks) * PAIR
    return pl.pallas_call(
        up_kernel,
        out_shape=jax.ShapeDtypeStruct((rows, 2 * HIDDEN), jnp.bfloat16),
        in_specs=[vmem] * 10,
        out_specs=vmem,
        compiler_params=pltpu.CompilerParams(vmem_limit_bytes=16 * 2**20),
        cost_estimate=pl.CostEstimate(flops=4 * rows * HIDDEN * D, bytes_accessed=2 * rows * D, transcendentals=0),
        name="up",
    )(*blocks, *up)


def down_kernel(begin, hidden, one, two, *outs):
    product = jnp.dot(
        hidden[begin * PAIR : (begin + len(outs)) * PAIR, :],
        jnp.concatenate([one[...], two[...]], axis=0),
        preferred_element_type=jnp.float32,
    ).astype(jnp.bfloat16)
    for i, out in enumerate(outs):
        out[...] = product[i * PAIR : (i + 1) * PAIR]


def project_down(hidden, down, begin, end):
    vmem = pl.BlockSpec(memory_space=pltpu.VMEM)
    n = end - begin
    return pl.pallas_call(
        functools.partial(down_kernel, begin),
        out_shape=[jax.ShapeDtypeStruct((PAIR, D), jnp.bfloat16)] * n,
        in_specs=[vmem] * 3,
        out_specs=[vmem] * n,
        compiler_params=pltpu.CompilerParams(vmem_limit_bytes=16 * 2**20),
        cost_estimate=pl.CostEstimate(
            flops=4 * n * PAIR * HIDDEN * D, bytes_accessed=2 * n * PAIR * D, transcendentals=0
        ),
        name="down",
    )(hidden, *down)


def pack_kernel(one, two, block):
    block[:SLOTS] = one[...]
    block[SLOTS:] = two[...]


def pack(one, two):
    vmem = pl.BlockSpec(memory_space=pltpu.VMEM)
    return pl.pallas_call(
        pack_kernel,
        out_shape=jax.ShapeDtypeStruct((PAIR, D), jnp.bfloat16),
        in_specs=[vmem] * 2,
        out_specs=vmem,
        compiler_params=pltpu.CompilerParams(vmem_limit_bytes=16 * 2**20),
        name="pack",
    )(one, two)


def hand_kernel(*refs):
    pass


def hand(held, *after):
    vmem = pl.BlockSpec(memory_space=pltpu.VMEM)
    return pl.pallas_call(
        hand_kernel,
        out_shape=jax.ShapeDtypeStruct(held.shape, held.dtype),
        in_specs=[vmem] + [pl.BlockSpec(memory_space=pl.ANY)] * len(after),
        out_specs=vmem,
        input_output_aliases={0: 0},
        compiler_params=pltpu.CompilerParams(vmem_limit_bytes=16 * 2**20),
        name="hand",
    )(held, *after)


def merge_kernel(n, mine, arrived, *refs):
    waiting, (total, *later) = refs[:n], refs[-n - 1 :]
    total[...] = (mine[...].astype(jnp.float32) + arrived[...].astype(jnp.float32)).astype(jnp.bfloat16)
    for source, target in zip(waiting, later):
        target[...] = source[...]


def merge(mine, arrived, *waiting, after=()):
    vmem = pl.BlockSpec(memory_space=pltpu.VMEM)
    n = len(waiting)
    return pl.pallas_call(
        functools.partial(merge_kernel, n),
        out_shape=[jax.ShapeDtypeStruct((PAIR, D), jnp.bfloat16)] * (1 + n),
        in_specs=[vmem] * (2 + n) + [pl.BlockSpec(memory_space=pl.ANY)] * len(after),
        out_specs=[vmem] * (1 + n),
        compiler_params=pltpu.CompilerParams(vmem_limit_bytes=16 * 2**20),
        name="merge",
    )(mine, arrived, *waiting, *after)


def finish_kernel(own, direct, back, *refs):
    one, two = refs[-2:]
    value = sum(x[...].astype(jnp.float32) for x in (own, direct, back))
    one[...] = value[:SLOTS].astype(one.dtype)
    two[...] = value[SLOTS:].astype(two.dtype)


def finish(own, direct, back, kept_type, after=()):
    vmem = pl.BlockSpec(memory_space=pltpu.VMEM)
    return pl.pallas_call(
        finish_kernel,
        out_shape=[jax.ShapeDtypeStruct((SLOTS, D), kept_type), jax.ShapeDtypeStruct((SLOTS, D), jnp.bfloat16)],
        in_specs=[vmem] * 3 + [pl.BlockSpec(memory_space=pl.ANY)] * len(after),
        out_specs=[vmem] * 2,
        compiler_params=pltpu.CompilerParams(vmem_limit_bytes=16 * 2**20),
        name="finish",
    )(own, direct, back, *after)


def collect_kernel(*refs):
    *parts, out = refs
    out[...] = sum(x[...].astype(jnp.float32) for x in parts)


def collect(*parts):
    vmem = pl.BlockSpec(memory_space=pltpu.VMEM)
    return pl.pallas_call(
        collect_kernel,
        out_shape=jax.ShapeDtypeStruct((SLOTS, D), jnp.float32),
        in_specs=[vmem] * len(parts),
        out_specs=vmem,
        compiler_params=pltpu.CompilerParams(vmem_limit_bytes=16 * 2**20),
        name="collect",
    )(*parts)


def on_device(
    queries, cache_keys, cache_values, lengths, counts, norm_gain, up_weight, down_weight
):
    up_own = up_weight.T
    up_other = send(up_own, "core", "up")
    attended, normed, down_held = attend(
        queries, cache_keys, cache_values, lengths, norm_gain, down_weight
    )
    by_wrap, by_far, by_near = [send(normed, r, "gather") for r in ("swrap", "sfar", "snear")]
    early = pack(normed, by_near)
    late = pack(by_wrap, by_far)
    early_n, late_w = send(early, "tnear", "gather"), send(late, "twrap", "gather")
    late_n, early_w = send(late, "tnear", "gather"), send(early, "twrap", "gather")
    early_w = hand(early_w, early_n)
    early_f, late_f = send(early_w, "tnear", "gather2"), send(late_n, "twrap", "gather2")
    down_held = hand(down_held, up_other)
    down_other = send(down_held, "core", "down")
    up_held = fetch(up_own, late)
    hidden = project_up(
        [early, late, early_n, late_n, early_w, late_w, early_f, late_f], (up_held, up_other)
    )
    down = (down_held, down_other)
    early_f, late_f = project_down(hidden, down, 6, 8)
    early, late, early_n, late_n, early_w, late_w = project_down(hidden, down, 0, 6)
    far_late = send(late_f, "snear", "reduce2")
    far_early = send(early_f, "swrap", "reduce2")
    direct_late = send(late_n, "snear", "reduce")
    direct_early = send(early_w, "swrap", "reduce")
    (late_w,) = merge(late_w, far_late)
    back_late = send(late_w, "swrap", "reduce")
    (early_n,) = merge(early_n, far_early, after=(late_w,))
    back_early = send(early_n, "snear", "reduce")
    home_wrap, home_far = finish(late, direct_late, back_late, jnp.bfloat16, after=(direct_early,))
    own, home_near = finish(early, direct_early, back_early, jnp.float32, after=(home_wrap,))
    home_wrap, home_far = send(home_wrap, "twrap", "home"), send(home_far, "tfar", "home")
    home_near = send(home_near, "tnear", "home")
    mixed = collect(attended, own, home_far, home_wrap)
    live = jnp.arange(SLOTS, dtype=jnp.int32)[:, None] < counts[0]
    return jnp.where(live, mixed + home_near.astype(jnp.float32), jnp.float32(0.0)).astype(jnp.bfloat16)


def solution(mesh):
    in_specs = (
        P(("rep", "dp"), None),
        P(("rep", "dp"), None),
        P(("rep", "dp"), None),
        P(("rep", "dp")),
        P(("rep", "dp")),
        P(),
        P(None, "dp"),
        P("dp", None),
    )
    out_specs = P(("rep", "dp"), None)
    return jax.shard_map(
        on_device, mesh=mesh, in_specs=in_specs, out_specs=out_specs, check_vma=False
    )
```

```python
import functools
import math

import jax
import jax.numpy as jnp
from jax import lax
from jax.experimental import pallas as pl
from jax.experimental.pallas import tpu as pltpu
from jax.sharding import PartitionSpec as P

HQ = 48
KVH = 4
HD = 128
GROUP = HQ // KVH
D = HQ * HD
SLOTS = 16
POOL = 1024
HIDDEN = 448
SIDE = 4
PAIR = 2 * SLOTS


def device(y, x, c):
    return (y * SIDE + x) * 2 + c


def routes():
    other = {"near": (1, 0, 3, 2), "wrap": (3, 2, 1, 0), "far": (2, 3, 0, 1)}
    out = {"core": [], **{axis + name: [] for axis in "st" for name in other}}
    for y in range(SIDE):
        for x in range(SIDE):
            for c in range(2):
                me = device(y, x, c)
                for name, to in other.items():
                    along_x, along_y = device(y, to[x], c), device(to[y], x, c)
                    out["s" + name].append((me, along_x if c == 0 else along_y))
                    out["t" + name].append((me, along_y if c == 0 else along_x))
                out["core"].append((me, device(y, x, 1 - c)))
    return out


ROUTES = routes()


def send(value, route, what):
    with jax.named_scope(what + "_" + route):
        return lax.ppermute(value, "dp", ROUTES[route])


def in_hbm(x):
    return pltpu.with_memory_space_constraint(x, pltpu.HBM)


def attend_kernel(
    lengths_in, q_in, k_in, v_in, gain_in, down, attended, normed, down_held, lengths, q, k, v, gain, sems
):
    copies = [
        pltpu.make_async_copy(a, b, sems.at[i])
        for i, (a, b) in enumerate(
            (
                (lengths_in, lengths),
                (k_in, k),
                (q_in, q),
                (v_in, v),
                (gain_in, gain),
                (down, down_held),
            )
        )
    ]
    for copy in copies:
        copy.start()
    copies[0].wait()
    row = lax.broadcasted_iota(jnp.int32, (SLOTS, 1), 0)
    starts = jnp.zeros((SLOTS, 1), jnp.int32)
    ends = jnp.zeros((SLOTS, 1), jnp.int32)
    at = jnp.int32(0)
    for i in range(SLOTS):
        after = at + lengths[i]
        starts = jnp.where(row == i, at, starts)
        ends = jnp.where(row == i, after, ends)
        at = after
    position = lax.broadcasted_iota(jnp.int32, (SLOTS, POOL), 1)
    inside = (position >= starts) & (position < ends)
    offset = jnp.where(inside, jnp.float32(0.0), jnp.float32(-1e30))
    squares = jnp.zeros((SLOTS, HD), jnp.float32)
    ones = jnp.ones((POOL, HD), jnp.bfloat16)
    copies[1].wait()
    copies[2].wait()
    for kv in range(KVH):
        heads = range(kv * GROUP, (kv + 1) * GROUP)
        rows = jnp.concatenate([q[:, h * HD : (h + 1) * HD] for h in heads], axis=0)
        scores = lax.dot_general(
            rows,
            k[:, kv * HD : (kv + 1) * HD],
            (((1,), (1,)), ((), ())),
            preferred_element_type=jnp.float32,
        )
        masked = scores.reshape(GROUP, SLOTS, POOL) + offset[None]
        top = jnp.max(masked, axis=-1, keepdims=True)
        raised = jnp.exp2((masked - top) * jnp.float32(HD ** (-0.5) * math.log2(math.e)))
        if kv == 0:
            copies[3].wait()
        mixed = lax.dot_general(
            raised.astype(jnp.bfloat16).reshape(GROUP * SLOTS, POOL),
            jnp.concatenate([v[:, kv * HD : (kv + 1) * HD], ones], axis=1),
            (((1,), (0,)), ((), ())),
            preferred_element_type=jnp.float32,
        )
        mixed = (mixed[:, :HD] / mixed[:, HD:]).reshape(GROUP, SLOTS, HD)
        for g, h in enumerate(heads):
            part = mixed[g].astype(jnp.bfloat16)
            attended[:, h * HD : (h + 1) * HD] = part
            wide = part.astype(jnp.float32)
            squares = squares + wide * wide
    mean_square = jnp.sum(squares, axis=-1, keepdims=True) / D
    factor = lax.rsqrt(mean_square + 1e-05)
    copies[4].wait()
    normed[...] = (attended[...].astype(jnp.float32) * factor * gain[...]).astype(jnp.bfloat16)
    copies[5].wait()


def attend(queries, cache_keys, cache_values, lengths, norm_gain, down_rows):
    vmem = pl.BlockSpec(memory_space=pltpu.VMEM)
    any_space = pl.BlockSpec(memory_space=pl.ANY)
    return pl.pallas_call(
        attend_kernel,
        out_shape=(
            jax.ShapeDtypeStruct((SLOTS, D), jnp.bfloat16),
            jax.ShapeDtypeStruct((SLOTS, D), jnp.bfloat16),
            jax.ShapeDtypeStruct((HIDDEN, D), jnp.bfloat16),
        ),
        in_specs=[any_space] * 6,
        out_specs=(vmem, vmem, vmem),
        scratch_shapes=[
            pltpu.SMEM((SLOTS,), jnp.int32),
            pltpu.VMEM((SLOTS, D), jnp.bfloat16),
            pltpu.VMEM((POOL, KVH * HD), jnp.bfloat16),
            pltpu.VMEM((POOL, KVH * HD), jnp.bfloat16),
            pltpu.VMEM((1, D), jnp.float32),
            pltpu.SemaphoreType.DMA((6,)),
        ],
        compiler_params=pltpu.CompilerParams(vmem_limit_bytes=16 * 2**20),
        name="attend",
    )(*map(in_hbm, (lengths, queries, cache_keys, cache_values, norm_gain.reshape(1, D), down_rows)))


def fetch_kernel(weights, after, held, sem):
    copy = pltpu.make_async_copy(weights, held, sem)
    copy.start()
    copy.wait()


def fetch(weights, after):
    any_space = pl.BlockSpec(memory_space=pl.ANY)
    return pl.pallas_call(
        fetch_kernel,
        out_shape=jax.ShapeDtypeStruct((HIDDEN, D), jnp.bfloat16),
        in_specs=[any_space] * 2,
        out_specs=pl.BlockSpec(memory_space=pltpu.VMEM),
        scratch_shapes=[pltpu.SemaphoreType.DMA],
        compiler_params=pltpu.CompilerParams(vmem_limit_bytes=16 * 2**20),
        cost_estimate=pl.CostEstimate(flops=10**11, bytes_accessed=4 * HIDDEN * D, transcendentals=0),
        name="fetch",
    )(in_hbm(weights), after)


def up_kernel(*args):
    blocks, up, hidden = args[:8], args[8:10], args[10]
    lows, highs = slice(0, SLOTS), slice(SLOTS, PAIR)
    order = [(0, lows), (0, highs), (1, highs), (1, lows)]
    rows = jnp.concatenate([blocks[2 * t + part][half, :] for part, half in order for t in range(SIDE)], axis=0)
    value = lax.dot_general(
        jnp.concatenate([w[...] for w in up], axis=0),
        rows,
        (((1,), (1,)), ((), ())),
        preferred_element_type=jnp.float32,
    )
    hidden[...] = (value / (1.0 + jnp.exp(-value))).astype(jnp.bfloat16).T


def project_up(blocks, up):
    vmem = pl.BlockSpec(memory_space=pltpu.VMEM)
    rows = len(blocks) * PAIR
    return pl.pallas_call(
        up_kernel,
        out_shape=jax.ShapeDtypeStruct((rows, 2 * HIDDEN), jnp.bfloat16),
        in_specs=[vmem] * 10,
        out_specs=vmem,
        compiler_params=pltpu.CompilerParams(vmem_limit_bytes=16 * 2**20),
        cost_estimate=pl.CostEstimate(flops=4 * rows * HIDDEN * D, bytes_accessed=2 * rows * D, transcendentals=0),
        name="up",
    )(*blocks, *up)


def down_kernel(begin, hidden, one, two, *outs):
    product = jnp.dot(
        hidden[begin * PAIR : (begin + len(outs)) * PAIR, :],
        jnp.concatenate([one[...], two[...]], axis=0),
        preferred_element_type=jnp.float32,
    ).astype(jnp.bfloat16)
    for i, out in enumerate(outs):
        out[...] = product[i * PAIR : (i + 1) * PAIR]


def project_down(hidden, down, begin, end):
    vmem = pl.BlockSpec(memory_space=pltpu.VMEM)
    n = end - begin
    return pl.pallas_call(
        functools.partial(down_kernel, begin),
        out_shape=[jax.ShapeDtypeStruct((PAIR, D), jnp.bfloat16)] * n,
        in_specs=[vmem] * 3,
        out_specs=[vmem] * n,
        compiler_params=pltpu.CompilerParams(vmem_limit_bytes=16 * 2**20),
        cost_estimate=pl.CostEstimate(
            flops=4 * n * PAIR * HIDDEN * D, bytes_accessed=2 * n * PAIR * D, transcendentals=0
        ),
        name="down",
    )(hidden, *down)


def pack_kernel(one, two, block):
    block[:SLOTS] = one[...]
    block[SLOTS:] = two[...]


def pack(one, two):
    vmem = pl.BlockSpec(memory_space=pltpu.VMEM)
    return pl.pallas_call(
        pack_kernel,
        out_shape=jax.ShapeDtypeStruct((PAIR, D), jnp.bfloat16),
        in_specs=[vmem] * 2,
        out_specs=vmem,
        compiler_params=pltpu.CompilerParams(vmem_limit_bytes=16 * 2**20),
        name="pack",
    )(one, two)


def hand_kernel(*refs):
    pass


def hand(held, *after):
    vmem = pl.BlockSpec(memory_space=pltpu.VMEM)
    return pl.pallas_call(
        hand_kernel,
        out_shape=jax.ShapeDtypeStruct(held.shape, held.dtype),
        in_specs=[vmem] + [pl.BlockSpec(memory_space=pl.ANY)] * len(after),
        out_specs=vmem,
        input_output_aliases={0: 0},
        compiler_params=pltpu.CompilerParams(vmem_limit_bytes=16 * 2**20),
        name="hand",
    )(held, *after)


def merge_kernel(n, mine, arrived, *refs):
    waiting, (total, *later) = refs[:n], refs[-n - 1 :]
    total[...] = (mine[...].astype(jnp.float32) + arrived[...].astype(jnp.float32)).astype(jnp.bfloat16)
    for source, target in zip(waiting, later):
        target[...] = source[...]


def merge(mine, arrived, *waiting, after=()):
    vmem = pl.BlockSpec(memory_space=pltpu.VMEM)
    n = len(waiting)
    return pl.pallas_call(
        functools.partial(merge_kernel, n),
        out_shape=[jax.ShapeDtypeStruct((PAIR, D), jnp.bfloat16)] * (1 + n),
        in_specs=[vmem] * (2 + n) + [pl.BlockSpec(memory_space=pl.ANY)] * len(after),
        out_specs=[vmem] * (1 + n),
        compiler_params=pltpu.CompilerParams(vmem_limit_bytes=16 * 2**20),
        name="merge",
    )(mine, arrived, *waiting, *after)


def finish_kernel(own, direct, back, *refs):
    one, two = refs[-2:]
    value = sum(x[...].astype(jnp.float32) for x in (own, direct, back))
    one[...] = value[:SLOTS].astype(one.dtype)
    two[...] = value[SLOTS:].astype(two.dtype)


def finish(own, direct, back, kept_type, after=()):
    vmem = pl.BlockSpec(memory_space=pltpu.VMEM)
    return pl.pallas_call(
        finish_kernel,
        out_shape=[jax.ShapeDtypeStruct((SLOTS, D), kept_type), jax.ShapeDtypeStruct((SLOTS, D), jnp.bfloat16)],
        in_specs=[vmem] * 3 + [pl.BlockSpec(memory_space=pl.ANY)] * len(after),
        out_specs=[vmem] * 2,
        compiler_params=pltpu.CompilerParams(vmem_limit_bytes=16 * 2**20),
        name="finish",
    )(own, direct, back, *after)


def collect_kernel(*refs):
    *parts, out = refs
    out[...] = sum(x[...].astype(jnp.float32) for x in parts)


def collect(*parts):
    vmem = pl.BlockSpec(memory_space=pltpu.VMEM)
    return pl.pallas_call(
        collect_kernel,
        out_shape=jax.ShapeDtypeStruct((SLOTS, D), jnp.float32),
        in_specs=[vmem] * len(parts),
        out_specs=vmem,
        compiler_params=pltpu.CompilerParams(vmem_limit_bytes=16 * 2**20),
        name="collect",
    )(*parts)


def on_device(
    queries, cache_keys, cache_values, lengths, counts, norm_gain, up_weight, down_weight
):
    up_own = up_weight.T
    up_other = send(up_own, "core", "up")
    attended, normed, down_held = attend(
        queries, cache_keys, cache_values, lengths, norm_gain, down_weight
    )
    by_wrap, by_far, by_near = [send(normed, r, "gather") for r in ("swrap", "sfar", "snear")]
    early = pack(normed, by_near)
    late = pack(by_far, by_wrap)
    early_n, late_w = send(early, "tnear", "gather"), send(late, "twrap", "gather")
    late_n, early_w = send(late, "tnear", "gather"), send(early, "twrap", "gather")
    early_n = hand(early_n, early_w)
    early_f, late_f = send(early_n, "twrap", "gather2"), send(late_w, "tnear", "gather2")
    down_held = hand(down_held, up_other)
    down_other = send(down_held, "core", "down")
    up_held = fetch(up_own, late)
    hidden = project_up(
        [early, late, early_n, late_n, early_w, late_w, early_f, late_f], (up_held, up_other)
    )
    down = (down_held, down_other)
    early_f, late_f = project_down(hidden, down, 6, 8)
    early, late, early_n, late_n, early_w, late_w = project_down(hidden, down, 0, 6)
    far_late = send(late_f, "snear", "reduce2")
    far_early = send(early_f, "swrap", "reduce2")
    direct_late = send(late_n, "snear", "reduce")
    direct_early = send(early_w, "swrap", "reduce")
    (late_w,) = merge(late_w, far_late)
    back_late = send(late_w, "swrap", "reduce")
    (early_n,) = merge(early_n, far_early, after=(late_w,))
    back_early = send(early_n, "snear", "reduce")
    home_wrap, home_far = finish(late, direct_late, back_late, jnp.bfloat16, after=(direct_early,))
    own, home_near = finish(early, direct_early, back_early, jnp.float32, after=(home_wrap,))
    home_wrap, home_far = send(home_wrap, "twrap", "home"), send(home_far, "tfar", "home")
    home_near = send(home_near, "tnear", "home")
    mixed = collect(attended, own, home_far, home_wrap)
    live = jnp.arange(SLOTS, dtype=jnp.int32)[:, None] < counts[0]
    return jnp.where(live, mixed + home_near.astype(jnp.float32), jnp.float32(0.0)).astype(jnp.bfloat16)


def solution(mesh):
    in_specs = (
        P(("rep", "dp"), None),
        P(("rep", "dp"), None),
        P(("rep", "dp"), None),
        P(("rep", "dp")),
        P(("rep", "dp")),
        P(),
        P(None, "dp"),
        P("dp", None),
    )
    out_specs = P(("rep", "dp"), None)
    return jax.shard_map(
        on_device, mesh=mesh, in_specs=in_specs, out_specs=out_specs, check_vma=False
    )
```
